128 devices in a mesh: dp: 32 (over x_lo, z, y), section: 4 (over x_hi, core).
Axes of the slice: x: 4 (x_hi: 2, x_lo: 2; x = x_hi * 2 + x_lo), y: 4, z: 4, core: 2. Of those that a mesh axis runs over, the one named last changes fastest.
Arguments:
- canvas_in: bfloat16 [64, 400, 1152], P('dp', None, 'section'), may hold values from -6 to 6
- conditioning: bfloat16 [64, 1152], P('dp'), may hold values from -6 to 6
- grid_shape: int32 [64], P('dp'), may hold values from 0 to 2, as said below
- kept_rank: int32 [64, 128], P('dp'), may hold values from 0 to 255, as said below
- first_weight: bfloat16 [4, 1152, 4608], P('section')
- second_weight: bfloat16 [4, 4608, 1152], P('section')
- modulation_weight: bfloat16 [4, 1152, 3456], P('section')
- modulation_bias: float32 [4, 3456], P('section'), may hold values from -3 to 3
- out_grad: bfloat16 [64, 400, 1152], P('dp', None, 'section'), may hold values from -6 to 6
Outputs:
- result: bfloat16 [64, 400, 1152], P('dp', None, 'section')
- canvas_grad: bfloat16 [64, 400, 1152], P('dp', None, 'section')
- first_grad: float32 [4, 1152, 4608], P('section', None, 'dp')
- second_grad: float32 [4, 4608, 1152], P('section', 'dp')
- modulation_grad: float32 [4, 1152, 3456], P('section')
- bias_grad: float32 [4, 3456], P('section')
The draws below stay inside these ranges and needn't reach their ends.
Inputs may be any that keep to these rules, and one draw needn't show every extreme that they name: `grid_shape`: 0, 1 or 2 for each canvas. `kept_rank`: each row holds 128 different token numbers in increasing order, all below the number of real tokens of its canvas.
All inputs are finite; a program needn't handle non-finite values.
Results may differ from the reference program's by a relative error of at most 0.025.
Values may be sent and summed in bfloat16 or wider, within the bound.
A program may use at most 384 MiB of HBM per device.

```python
import math
import jax
import jax.numpy as jnp
from jax import lax

D = 1152
HEADS = 16
FF = 4608
SIDE = 20
SLOTS = 400
VALID = 256
KEPT = 128
CANVASES = 64
N_SECTION = 4


def shape_choice(key):
    return jax.random.randint(key, (CANVASES,), 0, 3).astype(jnp.int32)


def draw_grid_shape(key, part):
    return shape_choice(key)


def draw_kept_rank(key, part):
    shapes = shape_choice(key)
    key = jax.random.fold_in(key, 11)
    live_counts = jnp.where(shapes == 0, 256, 240).astype(jnp.int32)
    canvas_keys = jax.random.split(key, CANVASES)

    def choose_rows(one_key, live_count):
        shuffled = jax.random.permutation(one_key, VALID).astype(jnp.int32)
        order_ids = jnp.arange(VALID, dtype=jnp.int32)
        scored = shuffled + jnp.where(order_ids < live_count, 0, VALID).astype(jnp.int32)
        chosen = jnp.argsort(scored, stable=True)[:KEPT]
        return jnp.sort(chosen).astype(jnp.int32)
    return jax.vmap(choose_rows)(canvas_keys, live_counts)


def draw_first_weight(key, part):
    key = jax.random.fold_in(key, 5)
    noise = jax.random.normal(key, (N_SECTION, D, FF), jnp.float32)
    column = jnp.arange(FF)
    section_ids = jnp.arange(N_SECTION)
    attention_scale = jnp.where(column < 3 * D, 1.0, 4.0)
    scale_grid = jnp.where((section_ids % 2 == 0)[:, None], attention_scale[None, :], 1.0)
    return (noise * scale_grid[:, None, :] / math.sqrt(D)).astype(jnp.bfloat16)


def normal_values(key, shape, spread, limit):
    return jnp.clip(jax.random.normal(key, shape, jnp.float32) * spread, -limit, limit)


def draw_canvas_in(key, part):
    key = jax.random.fold_in(key, 21)
    shape = (CANVASES, SLOTS, D)
    values = normal_values(key, shape, 1.0, 6.0)
    return values.astype(jnp.bfloat16)


def draw_conditioning(key, part):
    key = jax.random.fold_in(key, 22)
    shape = (CANVASES, D)
    values = normal_values(key, shape, 1.0, 6.0)
    return values.astype(jnp.bfloat16)


def draw_out_grad(key, part):
    key = jax.random.fold_in(key, 23)
    shape = (CANVASES, SLOTS, D)
    values = normal_values(key, shape, 1.0, 6.0)
    return values.astype(jnp.bfloat16)


def draw_second_weight(key, part):
    key = jax.random.fold_in(key, 24)
    shape = (N_SECTION, FF, D)
    spread = 1.0 / math.sqrt(FF)
    values = normal_values(key, shape, spread, 6.0 * spread)
    return values.astype(jnp.bfloat16)


def draw_modulation_weight(key, part):
    key = jax.random.fold_in(key, 25)
    shape = (N_SECTION, D, 3 * D)
    spread = 1.0 / math.sqrt(D)
    values = normal_values(key, shape, spread, 6.0 * spread)
    return values.astype(jnp.bfloat16)


def draw_modulation_bias(key, part):
    key = jax.random.fold_in(key, 26)
    shape = (N_SECTION, 3 * D)
    values = normal_values(key, shape, 0.5, 3.0)
    return values.astype(jnp.float32)


def setup_inputs(seed: int = 0) -> dict:
    splits = jax.random.split(jax.random.key(seed), 10)
    return {
        "canvas_in": draw_canvas_in(jax.random.fold_in(splits[9], 71), 0),
        "conditioning": draw_conditioning(jax.random.fold_in(splits[9], 71), 0),
        "grid_shape": draw_grid_shape(jax.random.fold_in(splits[9], 71), 0),
        "kept_rank": draw_kept_rank(jax.random.fold_in(splits[9], 71), 0),
        "first_weight": draw_first_weight(jax.random.fold_in(splits[9], 71), 0),
        "second_weight": draw_second_weight(jax.random.fold_in(splits[9], 71), 0),
        "modulation_weight": draw_modulation_weight(jax.random.fold_in(splits[9], 71), 0),
        "modulation_bias": draw_modulation_bias(jax.random.fold_in(splits[9], 71), 0),
        "out_grad": draw_out_grad(jax.random.fold_in(splits[9], 71), 0),
    }


@jax.custom_vjp
def low(v):
    return lax.optimization_barrier(v.astype(jnp.bfloat16)).astype(jnp.float32)

@jax.custom_vjp
def low_back(v):
    return v

def low_keep(v):
    return (low(v), None)

def low_pass(kept, grad):
    return (grad,)

def back_keep(v):
    return (v, None)

def back_low(kept, grad):
    return (low(grad),)
low.defvjp(low_keep, low_pass)
low_back.defvjp(back_keep, back_low)
HIGHEST_PRECISION = lax.Precision.HIGHEST
EPSILON = 1e-06

def cross(values):
    return low(low_back(values))

def gelu_tanh(values):
    return jax.nn.gelu(values, approximate=True)

def modulate(rows_float, norm_shift, norm_scale):
    mean_row = lax.optimization_barrier(jnp.mean(rows_float, axis=-1, keepdims=True))
    centred = rows_float - mean_row
    variance = lax.optimization_barrier(jnp.mean(centred * centred, axis=-1, keepdims=True))
    return centred * lax.rsqrt(variance + EPSILON) * (1.0 + norm_scale) + norm_shift

def canvas_layout(shape_id):
    grid_rows = jnp.where(shape_id == 1, 12, jnp.where(shape_id == 2, 20, 16)).astype(jnp.int32)
    grid_width = jnp.where(shape_id == 1, 20, jnp.where(shape_id == 2, 12, 16)).astype(jnp.int32)
    token_order = jnp.arange(VALID, dtype=jnp.int32)
    token_live = token_order < grid_rows * grid_width
    token_slot = jnp.where(token_live, token_order // grid_width * SIDE + token_order % grid_width, 0).astype(jnp.int32)
    slot_index = jnp.arange(SIDE * SIDE, dtype=jnp.int32)
    slot_line = slot_index // SIDE
    slot_column = slot_index % SIDE
    filled = (slot_line < grid_rows) & (slot_column < grid_width)
    slot_token = jnp.where(filled, slot_line * grid_width + slot_column, 0).astype(jnp.int32)
    return (token_slot, token_live, slot_token, filled)

def attention_branch(rows_float, weights, modulation, key_mask):
    model_width = rows_float.shape[1]
    row_count = rows_float.shape[0]
    head_size = model_width // HEADS
    hidden = low(modulate(rows_float, modulation[:model_width], modulation[model_width:2 * model_width]))
    projected = low(low_back(jnp.dot(hidden, weights[:, :3 * model_width], precision=HIGHEST_PRECISION)))
    heads_split = projected.reshape(row_count, 3, HEADS, head_size)
    scores = jnp.einsum('qhd,khd->hqk', heads_split[:, 0], heads_split[:, 1], precision=HIGHEST_PRECISION) * (1.0 / math.sqrt(head_size))
    scores = low_back(jnp.where(key_mask[None, None, :], scores, -1000000000.0))
    softmaxed = jax.nn.softmax(scores, axis=-1)
    mixed_rows = jnp.einsum('hqk,khd->qhd', low(softmaxed), heads_split[:, 2], precision=HIGHEST_PRECISION)
    mixed_rows = low(low_back(mixed_rows.reshape(row_count, model_width)))
    branch = low_back(jnp.dot(mixed_rows, weights[:, 3 * model_width:], precision=HIGHEST_PRECISION))
    return rows_float + modulation[2 * model_width:] * branch

def feed_forward(rows_float, first_matrix, second_matrix, modulation):
    model_width = rows_float.shape[1]
    hidden = low(modulate(rows_float, modulation[:model_width], modulation[model_width:2 * model_width]))
    inner = low_back(jnp.dot(hidden, first_matrix, precision=HIGHEST_PRECISION))
    active = low(gelu_tanh(inner))
    branch = low_back(jnp.dot(active, second_matrix, precision=HIGHEST_PRECISION))
    return rows_float + modulation[2 * model_width:] * branch

def canvas_forward(weights, canvas, condition_row, shape_id, kept_rows):
    first_matrix, second_matrix, modulation_matrix, modulation_offset = weights
    token_slot, token_live, slot_token, filled = canvas_layout(shape_id)
    stream_rows = jnp.where(token_live[:, None], canvas[token_slot], 0.0)
    signal = low(jax.nn.silu(condition_row))
    modulation = jnp.einsum('d,sde->se', signal, modulation_matrix, precision=HIGHEST_PRECISION) + modulation_offset
    stream_rows = cross(attention_branch(stream_rows, first_matrix[0], modulation[0], token_live))
    stream_rows = cross(feed_forward(stream_rows, first_matrix[1], second_matrix[1], modulation[1]))
    every_key = jnp.ones((kept_rows.shape[0],), dtype=bool)
    routed = attention_branch(stream_rows[kept_rows], first_matrix[2], modulation[2], every_key)
    stream_rows = cross(stream_rows.at[kept_rows].set(routed))
    routed = feed_forward(stream_rows[kept_rows], first_matrix[3], second_matrix[3], modulation[3])
    stream_rows = stream_rows.at[kept_rows].set(routed)
    return jnp.where(filled[:, None], stream_rows[slot_token], 0.0)

def reference(canvas_in, conditioning, grid_shape, kept_rank, first_weight, second_weight, modulation_weight, modulation_bias, out_grad):
    weights = (first_weight.astype(jnp.float32), second_weight.astype(jnp.float32), modulation_weight.astype(jnp.float32), modulation_bias.astype(jnp.float32))
    condition = conditioning.astype(jnp.float32)
    checked_forward = jax.checkpoint(canvas_forward)

    def run(weight_set, canvases):

        def one_canvas(carry, item):
            return (carry, checked_forward(weight_set, item[0], item[1], item[2], item[3]))
        _, outputs = lax.scan(one_canvas, None, (canvases, condition, grid_shape, kept_rank))
        return outputs
    result, pull_back = jax.vjp(run, weights, canvas_in.astype(jnp.float32))
    weight_grads, input_grad = pull_back(out_grad.astype(jnp.float32))
    return (result.astype(jnp.bfloat16), input_grad.astype(jnp.bfloat16), weight_grads[0], weight_grads[1], weight_grads[2], weight_grads[3])
```

```python
import functools
import math

import jax
import jax.numpy as jnp
from jax import lax
from jax.experimental import pallas as pl
from jax.experimental.pallas import tpu as pltpu
from jax.sharding import PartitionSpec as P

HEADS = 16
SIDE = 20
SLOTS = SIDE * SIDE
VALID = 256
KEPT = 128
D = 1152
FF = 4608
HALF = FF // 2
QUARTER = D // 4
HEAD = D // HEADS
BLOCK = FF // 32
EPSILON = 1e-06
FACTOR = 1.0 / math.sqrt(HEAD)
LOG2E = math.log2(math.e)
NEGATIVE = -1e30
BF = jnp.bfloat16
F32 = jnp.float32
VMEM = pltpu.VMEM
MESH = pl.DeviceIdType.MESH
NT = (((1,), (1,)), ((), ()))
TN = (((0,), (0,)), ((), ()))
C0 = math.sqrt(2.0 / math.pi)


def mm(a, b, dims=(((1,), (0,)), ((), ()))):
    return lax.dot_general(a, b, dims, preferred_element_type=F32)


def params(mb=50):
    return pltpu.CompilerParams(vmem_limit_bytes=mb * 2**20)


def whole(shape):
    return pl.BlockSpec(shape, lambda *_: (0,) * len(shape))


def cost(flops, nbytes):
    return pl.CostEstimate(flops=int(flops), bytes_accessed=int(nbytes), transcendentals=0)


def array(*shape, dtype=BF):
    return jax.ShapeDtypeStruct(shape, dtype)


def norm_stats(x):
    mean = jnp.mean(x, axis=-1, keepdims=True)
    centred = x - mean
    rstd = lax.rsqrt(jnp.mean(centred * centred, axis=-1, keepdims=True) + EPSILON)
    return centred * rstd, rstd


def hidden_of(rows_ref, mod_ref):
    normed, _ = norm_stats(rows_ref[...].astype(F32))
    return (normed * (1.0 + mod_ref[1:2, :]) + mod_ref[0:1, :]).astype(BF)


def norm_backward(rows, mod_ref, upstream, hidden_grad, modgrad_ref):
    normed, rstd = norm_stats(rows)
    modgrad_ref[0:1, :] = jnp.sum(hidden_grad, axis=0, keepdims=True)
    modgrad_ref[1:2, :] = jnp.sum(hidden_grad * normed, axis=0, keepdims=True)
    scaled = hidden_grad * (1.0 + mod_ref[1:2, :])
    mean_scaled = jnp.mean(scaled, axis=-1, keepdims=True)
    mean_product = jnp.mean(scaled * normed, axis=-1, keepdims=True)
    return upstream + (scaled - mean_scaled - normed * mean_product) * rstd


def gelu_pair(v):
    square = v * v
    t = jnp.tanh(v * (C0 + (C0 * 0.044715) * square))
    half = 0.5 * (1.0 + t)
    slope = half + (0.5 * v) * (1.0 - t * t) * (C0 + (3.0 * C0 * 0.044715) * square)
    return v * half, slope


def pick_kept(rows, kept_col):
    lane = lax.broadcasted_iota(jnp.int32, (KEPT, VALID), 1)
    return mm((lane == kept_col).astype(BF), rows).astype(BF)


def merge_kept(base, kept_rows, kept_row):
    line = lax.broadcasted_iota(jnp.int32, (VALID, KEPT), 0)
    spread = (line == kept_row).astype(F32)
    chosen = jnp.sum(spread, axis=1, keepdims=True) > 0.5
    return jnp.where(chosen, mm(spread.astype(BF), kept_rows).astype(BF), base)


def windows():
    for head in range(HEADS):
        first = head * HEAD
        start = first // 128 * 128
        stop = (first + HEAD - 1) // 128 * 128 + 128
        yield start, stop - start, first - start


def only_head(value, offset):
    lane = lax.broadcasted_iota(jnp.int32, value.shape, 1)
    return jnp.where((lane >= offset) & (lane < offset + HEAD), value, jnp.zeros_like(value))


def key_bias(live_ref, keys):
    lane = lax.broadcasted_iota(jnp.int32, (1, keys), 1)
    return jnp.where(lane < live_ref[0], 0.0, NEGATIVE).astype(F32)


def softmax_of(q, k, bias):
    scores = mm(q, k, NT) + bias
    top = jnp.max(scores, axis=-1, keepdims=True)
    grown = jnp.exp2((scores - top) * (FACTOR * LOG2E))
    return grown * (1.0 / jnp.sum(grown, axis=-1, keepdims=True))


def attention_forward_kernel(
    live_ref, rows_ref, mod_ref, w_ref, out_ref, hidden_ref, joined_ref, branch_ref, proj, mixed
):
    step = pl.program_id(0)

    @pl.when(step == 0)
    def _():
        hidden_ref[...] = hidden_of(rows_ref, mod_ref)

    @pl.when(step < 3)
    def _():
        part = mm(hidden_ref[...], w_ref[...]).astype(BF)
        proj[step] = part
        joined_ref[...] = part

    @pl.when(step == 3)
    def _():
        bias = key_bias(live_ref, rows_ref.shape[0])
        mixed[...] = jnp.zeros_like(mixed)
        for start, width, offset in windows():
            cut = pl.ds(start, width)
            q = only_head(proj[0, :, cut], offset)
            v = only_head(proj[2, :, cut], offset)
            soft = softmax_of(q, proj[1, :, cut], bias).astype(BF)
            mixed[:, cut] += mm(soft, v)
        mixed_low = mixed[...].astype(BF)
        joined_ref[...] = mixed_low
        branch = mm(mixed_low, w_ref[...])
        branch_ref[...] = branch.astype(BF)
        out_ref[...] = (rows_ref[...].astype(F32) + mod_ref[2:3, :] * branch).astype(BF)


def attention_forward(r, live, rows, mod, weights):
    row = pl.BlockSpec((r, D), lambda j: (0, 0))
    return pl.pallas_call(
        attention_forward_kernel,
        grid=(4,),
        in_specs=[
            pl.BlockSpec(memory_space=pltpu.SMEM),
            row,
            whole((3, D)),
            pl.BlockSpec((D, D), lambda j: (0, j)),
        ],
        out_specs=[row, row, pl.BlockSpec((r, D), lambda j: (0, j)), row],
        out_shape=(array(VALID, D), array(VALID, D), array(VALID, FF), array(VALID, D)),
        scratch_shapes=[VMEM((3, r, D), BF), VMEM((r, D), F32)],
        compiler_params=params(),
        cost_estimate=cost(2 * r * D * FF, 2 * D * FF),
        name="attention_forward",
    )(live, rows, mod, weights)


def attention_backward_kernel(
    live_ref, rows_ref, mod_ref, w_ref, joined_ref, branch_ref, up_ref,
    grad_ref, kept_ref, sent_ref, modgrad_ref, parts, pg, bg_keep, hidden_grad,
):
    step = pl.program_id(0)

    @pl.when(step == 0)
    def _():
        up = up_ref[...].astype(F32)
        modgrad_ref[2:3, :] = jnp.sum(up * branch_ref[...].astype(F32), axis=0, keepdims=True)
        bg = (up * mod_ref[2:3, :]).astype(BF)
        bg_keep[...] = bg
        mixed_grad = mm(bg, w_ref[...], NT).astype(BF)
        bias = key_bias(live_ref, rows_ref.shape[0])
        parts[...] = jnp.zeros_like(parts)
        for start, width, offset in windows():
            cut = pl.ds(start, width)
            q = only_head(joined_ref[:, pl.ds(start, width)], offset)
            k = only_head(joined_ref[:, pl.ds(D + start, width)], offset)
            v = joined_ref[:, pl.ds(2 * D + start, width)]
            mg = only_head(mixed_grad[:, start : start + width], offset)
            soft = softmax_of(q, k, bias)
            soft_grad = mm(mg, v, NT)
            parts[2, :, cut] += mm(soft.astype(BF), mg, TN)
            product = soft * soft_grad
            total = jnp.sum(product, axis=-1, keepdims=True)
            score_grad = (product - soft * total).astype(BF)
            parts[0, :, cut] += mm(score_grad, k)
            parts[1, :, cut] += mm(score_grad, q, TN)
        pg[0] = (parts[0] * FACTOR).astype(BF)
        pg[1] = (parts[1] * FACTOR).astype(BF)
        pg[2] = parts[2].astype(BF)
        low = live_ref[1] == 0

        @pl.when(low)
        def _():
            kept_ref[0] = pg[0]
            kept_ref[1] = pg[1]
            sent_ref[0] = pg[2]
            sent_ref[1] = bg_keep[...]

        @pl.when(jnp.logical_not(low))
        def _():
            sent_ref[0] = pg[0]
            sent_ref[1] = pg[1]
            kept_ref[0] = pg[2]
            kept_ref[1] = bg_keep[...]

    @pl.when(step > 0)
    def _():
        part = mm(pg[step - 1], w_ref[...], NT)

        @pl.when(step == 1)
        def _():
            hidden_grad[...] = part

        @pl.when(step > 1)
        def _():
            hidden_grad[...] += part

    @pl.when(step == 3)
    def _():
        grad = norm_backward(
            rows_ref[...].astype(F32), mod_ref, up_ref[...].astype(F32), hidden_grad[...], modgrad_ref
        )
        grad_ref[...] = grad.astype(BF)


def attention_backward(r, live, rows, mod, weights, joined, branch, up):
    row = pl.BlockSpec((r, D), lambda j: (0, 0))
    pair = pl.BlockSpec((2, r, D), lambda j: (0, 0, 0))
    return pl.pallas_call(
        attention_backward_kernel,
        grid=(4,),
        in_specs=[
            pl.BlockSpec(memory_space=pltpu.SMEM),
            row,
            whole((3, D)),
            pl.BlockSpec((D, D), lambda j: (0, (j + 3) % 4)),
            pl.BlockSpec((r, 3 * D), lambda j: (0, 0)),
            row,
            row,
        ],
        out_specs=[row, pair, pair, whole((3, D))],
        out_shape=(array(VALID, D), array(2, VALID, D), array(2, VALID, D), array(3, D, dtype=F32)),
        scratch_shapes=[VMEM((3, r, D), F32), VMEM((3, r, D), BF), VMEM((r, D), BF), VMEM((r, D), F32)],
        compiler_params=params(),
        cost_estimate=cost(2 * r * D * FF, 2 * D * FF),
        name="attention_backward",
    )(live, rows, mod, weights, joined, branch, up)


def attention_weights_kernel(low_ref, *refs):
    lefts, hiddens, mixeds, out_ref = refs[0:4], refs[4:8], refs[8:12], refs[12]
    use_mixed = (low_ref[0] == 1) & (pl.program_id(0) == 1)

    def total(rights):
        parts = [mm(a[0], b[...], TN) for a, b in zip(lefts, rights)]
        out_ref[...] = sum(parts[1:], parts[0]).astype(BF)

    @pl.when(use_mixed)
    def _():
        total(mixeds)

    @pl.when(jnp.logical_not(use_mixed))
    def _():
        total(hiddens)


def attention_weights(r, low, lefts, hiddens, own_joined, other_mixed, chunk=384):
    left = pl.BlockSpec((1, r, chunk), lambda p, j, low: (p, 0, j))
    row = pl.BlockSpec((r, D), lambda p, j, low: (0, 0))
    joined = pl.BlockSpec((r, D), lambda p, j, low: (0, 3))
    per = D // chunk
    return pl.pallas_call(
        attention_weights_kernel,
        grid_spec=pltpu.PrefetchScalarGridSpec(
            num_scalar_prefetch=1,
            grid=(2, per),
            in_specs=[left] * 4 + [row] * 4 + [joined] * 2 + [row] * 2,
            out_specs=pl.BlockSpec((chunk, D), lambda p, j, low: (p * per + j, 0)),
        ),
        out_shape=array(HALF, D),
        compiler_params=params(),
        cost_estimate=cost(8 * r * D * HALF, 2 * D * HALF),
        name="attention_weights",
    )(low, *lefts, *hiddens, *own_joined, *other_mixed)


def feed_forward_kernel(
    rows_ref, mod_ref, w1_ref, w2_ref, kept_ref, out_ref, hidden_ref, active_ref, slope_ref, branch_ref, picked_ref, total
):
    step = pl.program_id(0)

    @pl.when(step == 0)
    def _():
        hidden_ref[...] = hidden_of(rows_ref, mod_ref)

    active, slope = gelu_pair(mm(hidden_ref[...], w1_ref[...]))
    active_low = active.astype(BF)
    active_ref[...] = active_low
    slope_ref[...] = slope.astype(BF)
    part = mm(active_low, w2_ref[...])

    @pl.when(step == 0)
    def _():
        total[...] = part

    @pl.when(step > 0)
    def _():
        total[...] += part

    @pl.when(step == pl.num_programs(0) - 1)
    def _():
        branch = total[...]
        branch_ref[...] = branch.astype(BF)
        out = (rows_ref[...].astype(F32) + mod_ref[2:3, :] * branch).astype(BF)
        out_ref[...] = out
        picked_ref[...] = pick_kept(out, kept_ref[...])


def feed_forward(rows, mod, w1, w2, kept_col, chunk=1152):
    r = VALID
    low = array(r, D)
    big = array(r, FF)
    col = pl.BlockSpec((r, chunk), lambda j: (0, j))
    return pl.pallas_call(
        feed_forward_kernel,
        grid=(FF // chunk,),
        in_specs=[
            whole((r, D)),
            whole((3, D)),
            pl.BlockSpec((D, chunk), lambda j: (0, j)),
            pl.BlockSpec((chunk, D), lambda j: (j, 0)),
            whole((KEPT, 1)),
        ],
        out_specs=[whole((r, D)), whole((r, D)), col, col, whole((r, D)), whole((KEPT, D))],
        out_shape=(low, low, big, big, low, array(KEPT, D)),
        scratch_shapes=[VMEM((r, D), F32)],
        compiler_params=params(),
        cost_estimate=cost(4 * r * D * FF, 4 * D * FF),
        name="feed_forward",
    )(rows, mod, w1, w2, kept_col)


def feed_backward_kernel(
    rows_ref, mod_ref, w1_ref, w2_ref, slope_ref, branch_ref, base_ref, picked_ref, kept_ref,
    grad_ref, bg_ref, ig_ref, modgrad_ref, total, up_low,
):
    step = pl.program_id(0)

    @pl.when(step == 0)
    def _():
        low = merge_kept(base_ref[...], picked_ref[...], kept_ref[...])
        up_low[...] = low
        up = low.astype(F32)
        modgrad_ref[2:3, :] = jnp.sum(up * branch_ref[...].astype(F32), axis=0, keepdims=True)
        bg_ref[...] = (up * mod_ref[2:3, :]).astype(BF)

    active_grad = mm(bg_ref[...], w2_ref[...], NT)
    inner_grad = (active_grad * slope_ref[...].astype(F32)).astype(BF)
    ig_ref[...] = inner_grad
    part = mm(inner_grad, w1_ref[...], NT)

    @pl.when(step == 0)
    def _():
        total[...] = part

    @pl.when(step > 0)
    def _():
        total[...] += part

    @pl.when(step == pl.num_programs(0) - 1)
    def _():
        grad = norm_backward(
            rows_ref[...].astype(F32), mod_ref, up_low[...].astype(F32), total[...], modgrad_ref
        )
        grad_ref[...] = grad.astype(BF)


def feed_backward(rows, mod, w1, w2, slope, branch, base, picked, kept_row, chunk=1152):
    r = VALID
    low = array(r, D)
    col = pl.BlockSpec((r, chunk), lambda j: (0, j))
    return pl.pallas_call(
        feed_backward_kernel,
        grid=(FF // chunk,),
        in_specs=[
            whole((r, D)),
            whole((3, D)),
            pl.BlockSpec((D, chunk), lambda j: (0, j)),
            pl.BlockSpec((chunk, D), lambda j: (j, 0)),
            col,
            whole((r, D)),
            whole((r, D)),
            whole((KEPT, D)),
            whole((1, KEPT)),
        ],
        out_specs=[whole((r, D)), whole((r, D)), col, whole((3, D))],
        out_shape=(low, low, array(r, FF), array(3, D, dtype=F32)),
        scratch_shapes=[VMEM((r, D), F32), VMEM((r, D), BF)],
        compiler_params=params(),
        cost_estimate=cost(4 * r * D * FF, 4 * D * FF),
        name="feed_backward",
    )(rows, mod, w1, w2, slope, branch, base, picked, kept_row)


def feed_both_kernel(
    rows_ref, mod_ref, w1_ref, w2_ref, up_ref,
    out_ref, hidden_ref, active_ref, grad_ref, bg_ref, ig_ref, modgrad_ref, total, back,
):
    step = pl.program_id(0)

    @pl.when(step == 0)
    def _():
        hidden_ref[...] = hidden_of(rows_ref, mod_ref)
        bg_ref[...] = (up_ref[...].astype(F32) * mod_ref[2:3, :]).astype(BF)
        total[...] = jnp.zeros_like(total)
        back[...] = jnp.zeros_like(back)

    inner = mm(hidden_ref[...], w1_ref[...])
    active_grad = mm(bg_ref[...], w2_ref[...], NT)
    active, slope = gelu_pair(inner)
    active_low = active.astype(BF)
    active_ref[...] = active_low
    inner_grad = (active_grad * slope).astype(BF)
    ig_ref[...] = inner_grad
    total[...] += mm(active_low, w2_ref[...])
    back[...] += mm(inner_grad, w1_ref[...], NT)

    @pl.when(step == pl.num_programs(0) - 1)
    def _():
        branch = total[...]
        rows = rows_ref[...].astype(F32)
        up = up_ref[...].astype(F32)
        out_ref[...] = (rows + mod_ref[2:3, :] * branch).astype(BF)
        modgrad_ref[2:3, :] = jnp.sum(up * branch, axis=0, keepdims=True)
        grad = norm_backward(rows, mod_ref, up, back[...], modgrad_ref)
        grad_ref[...] = grad.astype(BF)


def feed_both(rows, mod, w1, w2, up, chunk=768):
    r = KEPT
    row = pl.BlockSpec((r, D), lambda j: (0, 0))
    col = pl.BlockSpec((r, chunk), lambda j: (0, j))
    low = array(VALID, D)
    big = array(VALID, FF)
    return pl.pallas_call(
        feed_both_kernel,
        grid=(FF // chunk,),
        in_specs=[
            row,
            whole((3, D)),
            pl.BlockSpec((D, chunk), lambda j: (0, j)),
            pl.BlockSpec((chunk, D), lambda j: (j, 0)),
            row,
        ],
        out_specs=[row, row, col, row, row, col, whole((3, D))],
        out_shape=(low, low, big, low, low, big, array(3, D, dtype=F32)),
        scratch_shapes=[VMEM((r, D), F32), VMEM((r, D), F32)],
        compiler_params=params(),
        cost_estimate=cost(8 * r * D * FF, 4 * D * FF),
        name="feed_both",
    )(rows, mod, w1, w2, up)


def feed_weights_kernel(low_ref, *refs):
    hid_own, hid_other, bg_own, bg_other = refs[0:2], refs[2:4], refs[4:6], refs[6:8]
    active_own, ig_own = refs[8:10], refs[10:12]
    w1_ref, w2_ref, first_ref, second_ref = refs[12:16]
    first = second = None
    for c in range(2):
        part = mm(ig_own[c][...], hid_own[c][...], TN)
        first = part if first is None else first + part
        part = mm(active_own[c][...], bg_own[c][...], TN)
        second = part if second is None else second + part
    for c in range(2):
        hidden, bg = hid_other[c][...], bg_other[c][...]
        active, slope = gelu_pair(mm(hidden, w1_ref[...]))
        inner_grad = mm(bg, w2_ref[...], NT) * slope
        first = first + mm(inner_grad.astype(BF), hidden, TN)
        second = second + mm(active.astype(BF), bg, TN)
    first_ref[...] = first.astype(BF)
    second_ref[...] = second.astype(BF)


def feed_weights(r, low, hid_own, hid_other, bg_own, bg_other, active_own, ig_own, w1, w2, chunk=384):
    per = HALF // chunk
    row = pl.BlockSpec((r, D), lambda j, low: (0, 0))
    col = pl.BlockSpec((r, chunk), lambda j, low: (0, low[0] * per + j))
    out = pl.BlockSpec((chunk, D), lambda j, low: (j, 0))
    return pl.pallas_call(
        feed_weights_kernel,
        grid_spec=pltpu.PrefetchScalarGridSpec(
            num_scalar_prefetch=1,
            grid=(per,),
            in_specs=[row] * 8
            + [col] * 4
            + [
                pl.BlockSpec((D, chunk), lambda j, low: (0, low[0] * per + j)),
                pl.BlockSpec((chunk, D), lambda j, low: (low[0] * per + j, 0)),
            ],
            out_specs=[out, out],
        ),
        out_shape=(array(HALF, D), array(HALF, D)),
        compiler_params=params(),
        cost_estimate=cost(24 * r * D * HALF, 8 * D * HALF),
        name="feed_weights",
    )(low, *hid_own, *hid_other, *bg_own, *bg_other, *active_own, *ig_own, w1, w2)


def move_rows_kernel(count, refs):
    index_ref = refs[0]
    for i in range(count):
        source, target = refs[1 + i], refs[1 + count + i]
        for c in range(source.shape[0]):
            index = index_ref[c]
            lane = lax.broadcasted_iota(jnp.int32, (index.shape[0], source.shape[1]), 1)
            target[c] = mm((lane == index).astype(BF), source[c]).astype(BF)


def move_rows(index, *sources):
    count = len(sources)
    rows = index.shape[1]
    spec = pl.BlockSpec(memory_space=VMEM)
    return pl.pallas_call(
        lambda *refs: move_rows_kernel(count, refs),
        in_specs=[spec] * (1 + count),
        out_specs=[spec] * count,
        out_shape=[array(s.shape[0], rows, s.shape[2]) for s in sources],
        compiler_params=params(),
        name="move_rows",
    )(index, *sources)


def merge_kernel(base_ref, kept_ref, index_ref, out_ref):
    out_ref[...] = merge_kept(base_ref[...], kept_ref[...], index_ref[...])


def merge(base, kept, kept_row):
    return pl.pallas_call(
        merge_kernel,
        grid=(1,),
        in_specs=[whole((VALID, D)), pl.BlockSpec((KEPT, D), lambda j: (0, 0)), whole((1, KEPT))],
        out_specs=whole((VALID, D)),
        out_shape=array(VALID, D),
        compiler_params=params(),
        name="merge_kept",
    )(base, kept, kept_row)


def unwritten(*shapes):
    spec = pl.BlockSpec(memory_space=pl.ANY)
    return pl.pallas_call(lambda *refs: None, out_specs=[spec] * len(shapes), out_shape=list(shapes), name="unwritten")()


FLOWS = ((0, "y", 0, 640), (0, "z", 640, 512), (1, "y", 0, 512), (1, "z", 512, 640))
CUT = 80


def sum_kernel(first_ref, second_ref, first_out, second_out, *scratch):
    count = len(FLOWS)
    per = 6
    ones, twos, threes, sums, tiny1, tiny2, tiny3 = (scratch[i * count : (i + 1) * count] for i in range(7))
    ends = scratch[7 * count]
    arrive = scratch[7 * count + 1]
    dp, section = lax.axis_index("dp"), lax.axis_index("section")
    x, z, y = dp // 16, (dp // 4) % 4, dp % 4
    place = {"y": y, "z": z}

    def neighbour(axis, by):
        if axis == "y":
            return (x * 16 + z * 4 + (y + by) % 4, section)
        return (x * 16 + ((z + by) % 4) * 4 + y, section)

    barrier = pltpu.get_barrier_semaphore()
    for axis in ("y", "z"):
        for by in (1, 3):
            pl.semaphore_signal(barrier, inc=1, device_id=neighbour(axis, by), device_id_type=MESH)
    pl.semaphore_wait(barrier, 4)

    data = (first_ref, second_ref)
    outs = (first_out, second_out)

    def copy(flow, phase, kind, side, source, target):
        axis = FLOWS[flow][1]
        if phase == 1:
            axis = "z" if axis == "y" else "y"
        number = ((flow * 2 + phase) * 3 + kind) * 2 + side
        return pltpu.make_async_remote_copy(
            src_ref=source,
            dst_ref=target,
            send_sem=ends.at[number],
            recv_sem=arrive.at[number],
            device_id=neighbour(axis, 1 if side == 0 else 3),
            device_id_type=MESH,
        )

    halves = (pl.ds(0, 2), pl.ds(2, 2))
    cuts = (pl.ds(0, CUT), pl.ds(CUT, BLOCK - CUT))

    def block(flow, position, part):
        which, axis, low, width = FLOWS[flow]
        columns = pl.ds(low, width)
        if axis == "y":
            return data[which].at[part, position, :, columns]
        return data[which].at[position, part, :, columns]

    pending = {}

    def start(flow, phase, kind, side, build):
        pending[(flow, phase, kind, side)] = lambda: copy(flow, phase, kind, side, *build())
        pending[(flow, phase, kind, side)]().start()

    def begin(flow):
        for side in (0, 1):
            start(flow, 0, 0, side, lambda side=side: (block(flow, (place[FLOWS[flow][1]] + 2) % 4, halves[side]), ones[flow].at[side]))
        for side in (0, 1):
            start(flow, 0, 1, side, lambda side=side: (block(flow, (place[FLOWS[flow][1]] + (1, 3)[side]) % 4, halves[1 - side]), twos[flow].at[side]))

    def forward(flow):
        at = place[FLOWS[flow][1]]
        for side in (0, 1):
            pending[(flow, 0, 0, side)]().wait()
            own = block(flow, (at + (1, 3)[side]) % 4, halves[side])[...]
            ones[flow][side] = (ones[flow][side].astype(F32) + own.astype(F32)).astype(BF)
            start(flow, 0, 2, side, lambda side=side: (ones[flow].at[side], threes[flow].at[side]))

    def middle(flow):
        at = place[FLOWS[flow][1]]
        for side in (0, 1):
            pending[(flow, 0, 1, side)]().wait()
            pending[(flow, 0, 2, side)]().wait()
        for half in (0, 1):
            own = block(flow, at, halves[half])[...].astype(F32)
            total = own + threes[flow][half].astype(F32) + twos[flow][1 - half].astype(F32)
            sums[flow][halves[half]] = total.astype(BF)

        def slab(by, cut):
            second = place["z" if FLOWS[flow][1] == "y" else "y"]
            return sums[flow].at[(second + by) % 4, cut]

        for side in (0, 1):
            start(flow, 1, 0, side, lambda side=side: (slab(2, cuts[side]), tiny1[flow].at[cuts[side]]))
        for side in (0, 1):
            start(flow, 1, 1, side, lambda side=side: (slab((1, 3)[side], cuts[1 - side]), tiny2[flow].at[cuts[1 - side]]))

    def late(flow):
        second = place["z" if FLOWS[flow][1] == "y" else "y"]
        for side in (0, 1):
            pending[(flow, 1, 0, side)]().wait()
            own = sums[flow][(second + (1, 3)[side]) % 4, cuts[side]]
            tiny1[flow][cuts[side]] = (tiny1[flow][cuts[side]].astype(F32) + own.astype(F32)).astype(BF)
            start(flow, 1, 2, side, lambda side=side: (tiny1[flow].at[cuts[side]], tiny3[flow].at[cuts[side]]))

    def finish(flow):
        which, axis, low, width = FLOWS[flow]
        second = place["z" if axis == "y" else "y"]
        for side in (0, 1):
            pending[(flow, 1, 1, side)]().wait()
            pending[(flow, 1, 2, side)]().wait()
        total = sums[flow][second].astype(F32) + tiny2[flow][...].astype(F32) + tiny3[flow][...].astype(F32)
        outs[which][:, low : low + width] = total

    even = [i for i, f in enumerate(FLOWS) if f[0] == 0]
    odd = [i for i, f in enumerate(FLOWS) if f[0] == 1]
    is_odd = section % 2 == 1

    @pl.when(jnp.logical_not(is_odd))
    def _():
        second_out[...] = jnp.zeros_like(second_out)

    for stage in (begin, forward, middle, late, finish):
        for flow in even:
            stage(flow)

        @pl.when(is_odd)
        def _():
            for flow in odd:
                stage(flow)


def sum_blocks(first, second):
    spec = pl.BlockSpec(memory_space=VMEM)
    widths = [f[3] for f in FLOWS]
    count = len(FLOWS)
    pair = [VMEM((2, 2, BLOCK, w), BF) for w in widths]
    tiny = [VMEM((BLOCK, w), BF) for w in widths]
    return pl.pallas_call(
        sum_kernel,
        in_specs=[spec] * 2,
        out_specs=[spec] * 2,
        out_shape=[array(BLOCK, D, dtype=F32)] * 2,
        scratch_shapes=pair * 3
        + [VMEM((4, BLOCK, w), BF) for w in widths]
        + tiny * 3
        + [pltpu.SemaphoreType.DMA((count * 12,)), pltpu.SemaphoreType.DMA((count * 12,))],
        compiler_params=pltpu.CompilerParams(
            collective_id=0, has_side_effects=True, vmem_limit_bytes=56 * 2**20
        ),
        cost_estimate=cost(FF * D, 4 * FF * D),
        name="sum_blocks",
    )(first.reshape(4, 4, BLOCK, D), second.reshape(4, 4, BLOCK, D))


def canvas_layout(shape_id):
    grid_rows = jnp.where(shape_id == 1, 12, jnp.where(shape_id == 2, 20, 16)).astype(jnp.int32)
    grid_width = jnp.where(shape_id == 1, 20, jnp.where(shape_id == 2, 12, 16)).astype(jnp.int32)
    token = jnp.arange(VALID, dtype=jnp.int32)
    live = grid_rows * grid_width
    token_slot = jnp.where(token < live, token // grid_width * SIDE + token % grid_width, -1)
    slot = jnp.arange(SLOTS, dtype=jnp.int32)
    line, column = slot // SIDE, slot % SIDE
    filled = (line < grid_rows) & (column < grid_width)
    slot_token = jnp.where(filled, line * grid_width + column, -1)
    return live, token_slot[:, None], slot_token[:, None]


BOTH = ("dp", "section")


def hop(value, source, target):
    return lax.ppermute(value, BOTH, [(d * 4 + source, d * 4 + target) for d in range(32)])


def swap(value, sections, from_low=True, from_high=True):
    pairs = []
    for d in range(32):
        if from_low if d < 16 else from_high:
            pairs += [(d * 4 + s, (d + 16) % 32 * 4 + s) for s in sections]
    return lax.ppermute(value, BOTH, pairs)


def local(
    canvas_in,
    conditioning,
    grid_shape,
    kept_rank,
    first_weight,
    second_weight,
    modulation_weight,
    modulation_bias,
    out_grad,
):
    section = lax.axis_index("section")
    low = lax.axis_index("dp") // 16
    low_ref = jnp.reshape(low, (1,)).astype(jnp.int32)
    w1, w2 = first_weight[0], second_weight[0]
    live, token_slot, slot_token = jax.vmap(canvas_layout)(grid_shape)
    scalars = [jnp.stack([live[c], low]).astype(jnp.int32) for c in range(2)]
    kept_scalars = jnp.stack([jnp.int32(KEPT), low]).astype(jnp.int32)
    kept_col = [kept_rank[c][:, None] for c in range(2)]
    kept_row = [kept_rank[c][None, :] for c in range(2)]

    packed_in, packed_grad = move_rows(token_slot, canvas_in, out_grad)
    arrived = [[hop(packed_in[c], s, 0) for s in (1, 2, 3)] for c in range(2)]
    rows0 = [jnp.concatenate([packed_in[c]] + arrived[c], axis=1) for c in range(2)]
    whole_grad = lax.all_gather(packed_grad, "section", axis=2, tiled=True)

    signal = jax.nn.silu(conditioning.astype(F32)).astype(BF)
    modulation = jnp.dot(signal, modulation_weight[0], preferred_element_type=F32) + modulation_bias[0]
    mod = [modulation[c].reshape(3, D) for c in range(2)]
    kept_grad = move_rows(kept_rank[:, :, None], whole_grad)[0]

    low_shape, big_shape, kept_shape = array(VALID, D), array(VALID, FF), array(KEPT, D)
    pair_shape, mod_shape = array(2, VALID, D), array(3, D, dtype=F32)

    def by_section(**branches):
        first = next(iter(branches.values()))
        shapes = jax.eval_shape(first)
        idle = lambda: tuple(unwritten(*shapes))
        return lax.switch(section, [branches.get("s%d" % s, idle) for s in range(4)])

    def attend(c, rows):
        def run():
            out, hidden, joined, branch = attention_forward(VALID, scalars[c], rows, mod[c], w1)
            return (out, hidden, joined, branch) + tuple(unwritten(big_shape, kept_shape))

        return run

    def attend_kept(c, rows):
        def run():
            out, hidden, joined, branch = attention_forward(KEPT, kept_scalars, rows, mod[c], w1)
            return (out, hidden, joined, branch) + tuple(unwritten(big_shape, kept_shape))

        return run

    def feed(c, rows):
        def run():
            out, hidden, active, slope, branch, picked = feed_forward(rows, mod[c], w1, w2, kept_col[c])
            return out, hidden, active, branch, slope, picked

        return run

    t0 = by_section(s0=attend(0, rows0[0]))
    rows1 = [hop(t0[0], 0, 1)]
    t1 = by_section(s0=attend(1, rows0[1]), s1=feed(0, rows1[0]))
    rows1.append(hop(t1[0], 0, 1))
    picked = [hop(t1[5], 1, 2)]
    t2 = by_section(s1=feed(1, rows1[1]), s2=attend_kept(0, picked[0]))
    picked.append(hop(t2[5], 1, 2))
    rows3 = [hop(t2[0][:KEPT], 2, 3)]

    def both(c, rows):
        def run():
            out, hidden, active, grad, bg, ig, modgrad = feed_both(rows, mod[c], w1, w2, kept_grad[c])
            return (out, grad) + tuple(unwritten(pair_shape)) + (bg, modgrad, hidden, active, low_shape_of(), ig)

        return run

    def low_shape_of():
        return unwritten(low_shape)[0]

    def attend_three(c, rows):
        def run():
            out, hidden, joined, branch = attention_forward(KEPT, kept_scalars, rows, mod[c], w1)
            grad, kept, bg, modgrad, ig = unwritten(low_shape, pair_shape, low_shape, mod_shape, big_shape)
            return out, grad, kept, bg, modgrad, hidden, joined, branch, ig

        return run

    t3 = by_section(s2=attend_three(1, picked[1]), s3=both(0, rows3[0]))
    rows3.append(hop(t3[0][:KEPT], 2, 3))
    back2 = [hop(t3[1][:KEPT], 3, 2)]
    done = [hop(t3[0][:KEPT], 3, 1)]

    def back_kept(c, rows, joined, branch, up):
        def run():
            grad, kept, sent, modgrad = attention_backward(KEPT, kept_scalars, rows, mod[c], w1, joined, branch, up)
            return grad, kept, sent, modgrad

        return run

    def both_four(c, rows):
        def run():
            out, hidden, active, grad, bg, ig, modgrad = feed_both(rows, mod[c], w1, w2, kept_grad[c])
            kept, sent = unwritten(pair_shape, pair_shape)
            return grad, kept, sent, modgrad, out, hidden, active, bg, ig

        return run

    def back_kept_four(*a):
        run = back_kept(*a)
        return lambda: run() + tuple(unwritten(low_shape, low_shape, big_shape, low_shape, big_shape))

    t4 = by_section(s2=back_kept_four(0, picked[0], t2[2], t2[3], back2[0]), s3=both_four(1, rows3[1]))
    back2.append(hop(t4[0][:KEPT], 3, 2))
    done.append(hop(t4[4][:KEPT], 3, 1))
    back1 = [hop(t4[0][:KEPT], 2, 1)]

    def back_feed(c, rows, slope, branch, kept):
        def run():
            grad, bg, ig, modgrad = feed_backward(
                rows, mod[c], w1, w2, slope, branch, whole_grad[c], kept, kept_row[c]
            )
            return (grad,) + tuple(unwritten(pair_shape, pair_shape)) + (modgrad, bg, ig)

        return run

    def back_whole(c, rows, joined, branch, up):
        def run():
            return tuple(attention_backward(VALID, scalars[c], rows, mod[c], w1, joined, branch, up))

        return run

    def padded(run):
        return lambda: tuple(run()) + tuple(unwritten(low_shape, big_shape))

    t5 = by_section(
        s1=back_feed(0, rows1[0], t1[4], t1[3], back1[0]),
        s2=padded(back_kept(1, picked[1], t3[6], t3[7], back2[1])),
    )
    back1.append(hop(t5[0][:KEPT], 2, 1))
    back0 = [hop(t5[0], 1, 0)]
    t6 = by_section(
        s1=back_feed(1, rows1[1], t2[4], t2[3], back1[1]),
        s0=padded(back_whole(0, rows0[0], t0[2], t0[3], back0[0])),
    )
    back0.append(hop(t6[0], 1, 0))
    t7 = by_section(s0=back_whole(1, rows0[1], t1[2], t1[3], back0[1]))

    hid = [swap(t0[1], (0,)), swap(t1[1], (0, 1)), swap(t2[1], (1, 2)), swap(t3[5], (2, 3)), swap(t4[5], (3,))]
    mixed = [
        swap(t0[2][:, 3 * D :], (0,), from_high=False),
        swap(t1[2][:, 3 * D :], (0,), from_high=False),
        swap(t2[2][:, 3 * D :], (2,), from_high=False),
        swap(t3[6][:, 3 * D :], (2,), from_high=False),
    ]
    bg3, bg4 = swap(t3[3], (3,)), swap(t4[7], (3,))
    sent4, sent5 = swap(t4[2], (2,)), swap(t5[2], (2,))
    bg5, bg6 = swap(t5[4], (1,)), swap(t6[4], (1,))
    sent6, sent7 = swap(t6[2], (0,)), swap(t7[2], (0,))

    def weights_attention():
        first = attention_weights(
            VALID, low_ref, (t6[1], t7[1], sent6, sent7), (t0[1], t1[1], hid[0], hid[1]), (t0[2], t1[2]), mixed[:2]
        )
        return (first,) + tuple(unwritten(array(HALF, D)))

    def weights_attention_kept():
        first = attention_weights(
            KEPT, low_ref, (t4[1], t5[1], sent4, sent5), (t2[1], t3[5], hid[2], hid[3]), (t2[2], t3[6]), mixed[2:]
        )
        return (first,) + tuple(unwritten(array(HALF, D)))

    def weights_feed():
        return tuple(
            feed_weights(
                VALID, low_ref, (t1[1], t2[1]), (hid[1], hid[2]), (t5[4], t6[4]), (bg5, bg6),
                (t1[2], t2[2]), (t5[5], t6[5]), w1, w2,
            )
        )

    def weights_feed_kept():
        return tuple(
            feed_weights(
                KEPT, low_ref, (t3[5], t4[5]), (hid[3], hid[4]), (t3[3], t4[7]), (bg3, bg4),
                (t3[6], t4[6]), (t3[8], t4[8]), w1, w2,
            )
        )

    first_part, second_part = by_section(
        s0=weights_attention, s1=weights_feed, s2=weights_attention_kept, s3=weights_feed_kept
    )
    first_sum, second_sum = sum_blocks(first_part, second_part)

    rows4 = [merge((t1, t2)[c][0], done[c], kept_row[c]) for c in range(2)]

    def spread(rows, source):
        parts = [jnp.stack([rows[c][:, q * QUARTER : (q + 1) * QUARTER] for c in range(2)]) for q in range(4)]
        total = None
        for q in range(4):
            if q == source:
                here = jnp.where(section == q, parts[q], jnp.zeros_like(parts[q]))
            else:
                here = hop(parts[q], source, q)
            total = here if total is None else jnp.where(section == q, here, total)
        return total

    result = move_rows(slot_token, spread(rows4, 1))[0]
    canvas_grad = move_rows(slot_token, spread([t6[0], t7[0]], 0))[0]

    def chosen(*values):
        return lax.select_n(section, *values)

    modgrads = jnp.stack(
        [chosen(t6[3], t5[3], t4[3], t3[4]).reshape(-1), chosen(t7[3], t6[3], t5[3], t4[3]).reshape(-1)]
    )
    all_modgrads = lax.all_gather(modgrads.astype(BF), "dp", axis=0, tiled=True)
    all_signal = lax.all_gather(signal, "dp", axis=0, tiled=True)
    modulation_grad = mm(all_signal, all_modgrads, TN)
    bias_grad = jnp.sum(all_modgrads.astype(F32), axis=0)
    return (
        result,
        canvas_grad,
        first_sum.T[None],
        second_sum[None],
        modulation_grad[None],
        bias_grad[None],
    )


def solution(mesh):
    placed = (
        P("dp", None, "section"),
        P("dp", None),
        P("dp"),
        P("dp", None),
        P("section", None, None),
        P("section", None, None),
        P("section", None, None),
        P("section", None),
        P("dp", None, "section"),
    )
    return jax.shard_map(
        local,
        mesh=mesh,
        in_specs=placed,
        out_specs=(
            P("dp", None, "section"),
            P("dp", None, "section"),
            P("section", None, "dp"),
            P("section", "dp", None),
            P("section", None, None),
            P("section", None),
        ),
        check_vma=False,
    )
```

```python
import functools
import math

import jax
import jax.numpy as jnp
from jax import lax
from jax.experimental import pallas as pl
from jax.experimental.pallas import tpu as pltpu
from jax.sharding import PartitionSpec as P

HEADS = 16
SIDE = 20
SLOTS = SIDE * SIDE
VALID = 256
KEPT = 128
D = 1152
FF = 4608
HALF = FF // 2
QUARTER = D // 4
WINDOW = 384
PACKED = 80
HEAD = D // HEADS
BLOCK = FF // 32
EPSILON = 1e-06
FACTOR = 1.0 / math.sqrt(HEAD)
LOG2E = math.log2(math.e)
NEGATIVE = -1e30
BF = jnp.bfloat16
F32 = jnp.float32
VMEM = pltpu.VMEM
MESH = pl.DeviceIdType.MESH
NT = (((1,), (1,)), ((), ()))
TN = (((0,), (0,)), ((), ()))
C0 = math.sqrt(2.0 / math.pi)


def mm(a, b, dims=(((1,), (0,)), ((), ()))):
    return lax.dot_general(a, b, dims, preferred_element_type=F32)


def cost(flops, nbytes):
    return pl.CostEstimate(flops=int(flops), bytes_accessed=int(nbytes), transcendentals=0)


def array(*shape, dtype=BF):
    return jax.ShapeDtypeStruct(shape, dtype)


def norm_stats(x):
    mean = jnp.mean(x, axis=-1, keepdims=True)
    centred = x - mean
    rstd = lax.rsqrt(jnp.mean(centred * centred, axis=-1, keepdims=True) + EPSILON)
    return centred * rstd, rstd


def norm_forward(rows, shift, scale):
    normed, _ = norm_stats(rows)
    return (normed * (1.0 + scale) + shift).astype(BF)


def norm_backward(rows, scale, upstream, hidden_grad):
    normed, rstd = norm_stats(rows)
    shift_grad = jnp.sum(hidden_grad, axis=0, keepdims=True)
    scale_grad = jnp.sum(hidden_grad * normed, axis=0, keepdims=True)
    scaled = hidden_grad * (1.0 + scale)
    mean_scaled = jnp.mean(scaled, axis=-1, keepdims=True)
    mean_product = jnp.mean(scaled * normed, axis=-1, keepdims=True)
    grad = upstream + (scaled - mean_scaled - normed * mean_product) * rstd
    return grad.astype(BF), shift_grad, scale_grad


def gelu_pair(v):
    square = v * v
    t = jnp.tanh(v * (C0 + (C0 * 0.044715) * square))
    half = 0.5 * (1.0 + t)
    slope = half + (0.5 * v) * (1.0 - t * t) * (C0 + (3.0 * C0 * 0.044715) * square)
    return v * half, slope


def kept_spread(kept_row):
    line = lax.broadcasted_iota(jnp.int32, (VALID, KEPT), 0)
    return (line == kept_row).astype(F32)


def pick_kept(rows, kept_row):
    return mm(kept_spread(kept_row).astype(BF), rows, TN).astype(BF)


def merge_kept(base, kept_rows, kept_row):
    spread = kept_spread(kept_row)
    chosen = jnp.sum(spread, axis=1, keepdims=True) > 0.5
    return jnp.where(chosen, mm(spread.astype(BF), kept_rows).astype(BF), base)


def grid_of(shape_id):
    lines = jnp.where(shape_id == 1, 12, jnp.where(shape_id == 2, 20, 16))
    width = jnp.where(shape_id == 1, 20, jnp.where(shape_id == 2, 12, 16))
    return lines, width


def token_of_slot(shape_id, axis):
    lines, width = grid_of(shape_id)
    slot = lax.broadcasted_iota(jnp.int32, (1, SLOTS) if axis else (SLOTS, 1), axis)
    line = (slot * 3277) >> 16
    column = slot - line * SIDE
    return jnp.where((line < lines) & (column < width), line * width + column, -1)


def shift_matrix(section):
    line = lax.broadcasted_iota(jnp.int32, (QUARTER, WINDOW), 0)
    lane = lax.broadcasted_iota(jnp.int32, (QUARTER, WINDOW), 1)
    return (lane == line + 32 * section).astype(BF)


def windows():
    for head in range(HEADS):
        first = head * HEAD
        start = first // 128 * 128
        stop = (first + HEAD - 1) // 128 * 128 + 128
        yield start, stop - start, first - start


def only_head(value, offset):
    lane = lax.broadcasted_iota(jnp.int32, value.shape, 1)
    return jnp.where((lane >= offset) & (lane < offset + HEAD), value, jnp.zeros_like(value))


def key_bias(live, keys):
    lane = lax.broadcasted_iota(jnp.int32, (1, keys), 1)
    return jnp.where(lane < live, 0.0, NEGATIVE).astype(F32)


def softmax_of(q, k, bias):
    scores = mm(q, k, NT)
    if bias is not None:
        scores = scores + bias
    top = jnp.max(scores, axis=-1, keepdims=True)
    grown = jnp.exp2((scores - top) * (FACTOR * LOG2E))
    return grown * (1.0 / jnp.sum(grown, axis=-1, keepdims=True))


class Copies:
    def __init__(self, send, arrive):
        self.send, self.arrive, self.first, self.size = send, arrive, {}, 0

    def name(self, key, count):
        self.first[key] = self.size
        self.size += count

    def remote(self, key, index, source, target, device, sender=None):
        at = self.first[key]
        return pltpu.make_async_remote_copy(
            src_ref=source,
            dst_ref=target,
            send_sem=self.send.at[at + (index if sender is None else sender)],
            recv_sem=self.arrive.at[at + index],
            device_id=device,
            device_id_type=MESH,
        )

    def local(self, key, index, source, target):
        return pltpu.make_async_copy(source, target, self.send.at[self.first[key] + index])


PIPE_COPIES = (
    ("wm", 3), ("w1", 4), ("w2", 4), ("in", 8), ("og", 16), ("forward", 2), ("rows2", 2), ("backward", 2), ("result", 8),
    ("hidden", 2), ("mixed", 2), ("pair", 4), ("own_hidden", 2), ("own_mixed", 2), ("own_x", 4), ("own_y", 4), ("own_grad", 2),
)


def pipeline_kernel(
    shape_ref, canvas_ref, ograd_ref, kept_ref, cond_ref, bias_ref, w1_hbm, w2_hbm, wm_hbm,
    hidden_own, hidden_other, mixed_own, mixed_other, x_own, y_own, grad_own, window_out, packed_out,
    w1, w2, rows, packs, quarters, grads, up, base, hidden, big, branch, outs, picked, back, bgs, parts, acc, rows2, mod,
    small, send, arrive,
):
    dp, section = lax.axis_index("dp"), lax.axis_index("section")
    high = dp // 16
    partner = ((dp + 16) % 32, section)
    copies = Copies(send, arrive)
    for key, count in PIPE_COPIES:
        copies.name(key, count)
    is_feed = section % 2 == 1

    def load_wm(j):
        return copies.local("wm", j, wm_hbm.at[:, pl.ds(j * D, D)], w2.at[j])

    def load_w1(j):
        return copies.local("w1", j, w1_hbm.at[:, pl.ds(j * D, D)], w1.at[j])

    def load_w2(j):
        return copies.local("w2", j, w2_hbm.at[pl.ds(j * D, D), :], w2.at[j])

    for j in range(3):
        load_wm(j).start()
    for j in range(4):
        load_w1(j).start()

    barrier = pltpu.get_barrier_semaphore()
    for by in (1, 2, 3):
        pl.semaphore_signal(barrier, inc=1, device_id=(dp, (section + by) % 4), device_id_type=MESH)
    pl.semaphore_signal(barrier, inc=1, device_id=partner, device_id_type=MESH)

    shift = shift_matrix(section)

    def pack(source, c):
        line = lax.broadcasted_iota(jnp.int32, (VALID, SLOTS), 0)
        hot = (line == token_of_slot(shape_ref[c], 1)).astype(BF)
        return mm(mm(hot, source[c]).astype(BF), shift).astype(BF)

    def send_in(c):
        return copies.remote("in", c * 4 + section, packs.at[0, c], quarters.at[c, section], (dp, 0), c * 4)

    def send_og(c, target):
        return copies.remote(
            "og", c * 4 + section, packs.at[1, c], grads.at[c, section], (dp, target), 8 + c * 4 + target
        )

    def take_in(c, s):
        return copies.remote("in", c * 4 + s, packs.at[0, c], quarters.at[c, s], (dp, 0), c * 4)

    def take_og(c, s):
        return copies.remote("og", c * 4 + s, packs.at[1, c], grads.at[c, s], (dp, 0), 8 + c * 4)

    packs[0, 0] = pack(canvas_ref, 0)
    pl.semaphore_wait(barrier, 4)

    @pl.when(section != 0)
    def _():
        send_in(0).start()

    packs[0, 1] = pack(canvas_ref, 1)

    @pl.when(section != 0)
    def _():
        send_in(1).start()

    for c in range(2):
        packs[1, c] = pack(ograd_ref, c)
        for target in (3, 1):

            @pl.when(section != target)
            def _():
                send_og(c, target).start()

    cond = cond_ref[...].astype(F32)
    signal = (cond * (1.0 / (1.0 + jnp.exp(-cond)))).astype(BF)
    small[...] = jnp.zeros_like(small)
    for c in range(2):
        for i in range(9):
            small[54 + c * 9 + i : 55 + c * 9 + i, :] = signal[c : c + 1, i * 128 : (i + 1) * 128].astype(F32)
    for j in range(3):
        load_wm(j).wait()
        part = mm(signal, w2[j]) + bias_ref[:, j * D : (j + 1) * D]
        for c in range(2):
            mod[c, j : j + 1, :] = part[c : c + 1, :]

    @pl.when(is_feed)
    def _():
        for j in range(4):
            load_w2(j).start()

    for j in range(4):
        load_w1(j).wait()

    def shift_of(c):
        return mod[c, 0:1, :]

    def scale_of(c):
        return mod[c, 1:2, :]

    def gate_of(c):
        return mod[c, 2:3, :]

    def put_sums(c, which, value):
        for i in range(9):
            small[pl.ds(c * 27 + which * 9 + i, 1), :] = value[:, i * 128 : (i + 1) * 128]

    def join(parts_ref, c, own, target):
        tiles = {}
        for q in range(4):
            value = own if q == target else parts_ref[c, q]
            for t in range(3):
                tile = value[:, t * 128 : (t + 1) * 128]
                at = 2 * q + t
                tiles[at] = tile if at not in tiles else tiles[at] + tile
        return jnp.concatenate([tiles[t] for t in range(9)], axis=1)

    def part(r):
        return pl.ds(0, r)

    def send_forward(c, r, source):
        return copies.remote("forward", c, source.at[c, part(r)], rows.at[c, part(r)], (dp, (section + 1) % 4))

    def send_backward(c, r):
        return copies.remote("backward", c, back.at[c, part(r)], up.at[c, part(r)], (dp, (section + 3) % 4))

    def send_rows2(c):
        return copies.remote("rows2", c, outs.at[c], rows2.at[c], (dp, 3))

    def send_hidden(c, r):
        return copies.remote("hidden", c, hidden.at[c, part(r)], hidden_other.at[c, part(r)], partner)

    def keep_hidden(c, r):
        return copies.local("own_hidden", c, hidden.at[c, part(r)], hidden_own.at[c, part(r)])

    def send_mixed(c, r, source, at):
        return copies.remote("mixed", c, source.at[at, part(r)], mixed_other.at[c, part(r)], partner)

    def keep_mixed(c, r, source, at):
        return copies.local("own_mixed", c, source.at[at, part(r)], mixed_own.at[c, part(r)])

    def keep_x(c, k, r, at):
        return copies.local("own_x", c * 2 + k, big.at[at, part(r)], x_own.at[c, k, part(r)])

    def keep_y(c, k, r):
        return copies.local("own_y", c * 2 + k, big.at[8 + c * 4 + high * 2 + k, part(r)], y_own.at[c, k, part(r)])

    def send_pair(c, k, r):
        source = big.at[8 + c * 4 + (1 - high) * 2 + k, part(r)]
        return copies.remote("pair", c * 2 + k, source, y_own.at[c, k, part(r)], partner)

    def keep_grad(c):
        return copies.local("own_grad", c, back.at[c], grad_own.at[c])

    def attend(c, r, live):
        x = rows[c, part(r)].astype(F32)
        hid = norm_forward(x, shift_of(c), scale_of(c))
        hidden[c, part(r)] = hid
        send_hidden(c, r).start()
        keep_hidden(c, r).start()
        for j in range(3):
            big[c * 4 + j, part(r)] = mm(hid, w1[j]).astype(BF)
        bias = None if live is None else key_bias(live, r)
        parts[0, part(r)] = jnp.zeros((r, D), F32)
        for start, width, offset in windows():
            cut = pl.ds(start, width)
            q = only_head(big[c * 4, part(r), cut], offset)
            v = only_head(big[c * 4 + 2, part(r), cut], offset)
            soft = softmax_of(q, big[c * 4 + 1, part(r), cut], bias).astype(BF)
            parts[0, part(r), cut] += mm(soft, v)
        mixed = parts[0, part(r)].astype(BF)
        big[c * 4 + 3, part(r)] = mixed
        send_mixed(c, r, big, c * 4 + 3).start()
        keep_mixed(c, r, big, c * 4 + 3).start()
        out = mm(mixed, w1[3])
        branch[c, part(r)] = out.astype(BF)
        outs[c, part(r)] = (rows[c, part(r)].astype(F32) + gate_of(c) * out).astype(BF)
        send_forward(c, r, outs).start()

    def attend_back(c, r, live, to_section):
        upstream = up[c, part(r)].astype(F32)
        put_sums(c, 2, jnp.sum(upstream * branch[c, part(r)].astype(F32), axis=0, keepdims=True))
        bg = (upstream * gate_of(c)).astype(BF)
        big[8 + c * 4 + 3, part(r)] = bg
        mixed_grad = mm(bg, w1[3], NT).astype(BF)
        bias = None if live is None else key_bias(live, r)
        parts[:, part(r)] = jnp.zeros((3, r, D), F32)
        for start, width, offset in windows():
            cut = pl.ds(start, width)
            q = only_head(big[c * 4, part(r), cut], offset)
            k = only_head(big[c * 4 + 1, part(r), cut], offset)
            v = big[c * 4 + 2, part(r), cut]
            mg = only_head(mixed_grad[:, start : start + width], offset)
            soft = softmax_of(q, k, bias)
            soft_grad = mm(mg, v, NT)
            parts[2, part(r), cut] += mm(soft.astype(BF), mg, TN)
            product = soft * soft_grad
            score_grad = (product - soft * jnp.sum(product, axis=-1, keepdims=True)).astype(BF)
            parts[0, part(r), cut] += mm(score_grad, k)
            parts[1, part(r), cut] += mm(score_grad, q, TN)
        big[8 + c * 4, part(r)] = (parts[0, part(r)] * FACTOR).astype(BF)
        big[8 + c * 4 + 1, part(r)] = (parts[1, part(r)] * FACTOR).astype(BF)
        big[8 + c * 4 + 2, part(r)] = parts[2, part(r)].astype(BF)
        for k in range(2):
            send_pair(c, k, r).start()
            keep_x(c, k, r, 8 + c * 4 + high * 2 + k).start()
        hidden_grad = mm(big[8 + c * 4, part(r)], w1[0], NT)
        hidden_grad += mm(big[8 + c * 4 + 1, part(r)], w1[1], NT)
        hidden_grad += mm(big[8 + c * 4 + 2, part(r)], w1[2], NT)
        grad, shift_grad, scale_grad = norm_backward(
            rows[c, part(r)].astype(F32), scale_of(c), up[c, part(r)].astype(F32), hidden_grad
        )
        back[c, part(r)] = grad
        if to_section:
            send_backward(c, r).start()
        else:
            keep_grad(c).start()
        put_sums(c, 0, shift_grad)
        put_sums(c, 1, scale_grad)

    def finish_attention(r, to_section):
        for c in range(2):
            send_hidden(c, r).wait()
            keep_hidden(c, r).wait()
            send_mixed(c, r, big, c * 4 + 3).wait()
            keep_mixed(c, r, big, c * 4 + 3).wait()
            send_forward(c, r, outs).wait_send()
            for k in range(2):
                send_pair(c, k, r).wait()
                keep_x(c, k, r, 8 + c * 4 + high * 2 + k).wait()
            if to_section:
                send_backward(c, r).wait_send()
            else:
                keep_grad(c).wait()

    @pl.when(section == 0)
    def _():
        def live_of(c):
            lines, width = grid_of(shape_ref[c])
            return lines * width

        def forward(c, carry):
            for s in (1, 2, 3):
                take_in(c, s).wait_recv()
            rows[c] = join(quarters, c, packs[0, c], 0)
            attend(c, VALID, live_of(c))
            return carry

        def backward(c, carry):
            send_backward(c, VALID).wait_recv()
            attend_back(c, VALID, live_of(c), False)
            return carry

        lax.fori_loop(0, 2, forward, 0)
        lax.fori_loop(0, 2, backward, 0)
        finish_attention(VALID, False)

    @pl.when(section == 1)
    def _():
        for j in range(4):
            load_w2(j).wait()

        def forward(c, carry):
            send_forward(c, VALID, outs).wait_recv()
            hid = norm_forward(rows[c].astype(F32), shift_of(c), scale_of(c))
            hidden[c] = hid
            send_hidden(c, VALID).start()
            keep_hidden(c, VALID).start()
            for j in range(4):
                active, slope = gelu_pair(mm(hid, w1[j]))
                low = active.astype(BF)
                big[c * 4 + j] = low
                big[8 + c * 4 + j] = slope.astype(BF)
                if j == 0:
                    acc[...] = mm(low, w2[j])
                else:
                    acc[...] += mm(low, w2[j])
            for k in range(2):
                keep_x(c, k, VALID, c * 4 + high * 2 + k).start()
            out = acc[...]
            branch[c] = out.astype(BF)
            low = (rows[c].astype(F32) + gate_of(c) * out).astype(BF)
            outs[c] = low
            picked[c] = pick_kept(low, kept_ref[pl.ds(c, 1), :])
            send_forward(c, KEPT, picked).start()
            send_rows2(c).start()
            return carry

        lax.fori_loop(0, 2, forward, 0)
        for c in range(2):
            for s in (0, 2, 3):
                take_og(c, s).wait_recv()
            base[c] = join(grads, c, packs[1, c], 1)

        def backward(c, carry):
            send_backward(c, KEPT).wait_recv()
            low = merge_kept(base[c], up[c, part(KEPT)], kept_ref[pl.ds(c, 1), :])
            base[c] = low
            upstream = low.astype(F32)
            bg = (upstream * gate_of(c)).astype(BF)
            bgs[c] = bg
            send_mixed(c, VALID, bgs, c).start()
            keep_mixed(c, VALID, bgs, c).start()
            put_sums(c, 2, jnp.sum(upstream * branch[c].astype(F32), axis=0, keepdims=True))
            for j in range(4):
                slope = big[8 + c * 4 + j].astype(F32)
                inner_grad = (mm(bg, w2[j], NT) * slope).astype(BF)
                big[8 + c * 4 + j] = inner_grad
                if j == 0:
                    acc[...] = mm(inner_grad, w1[j], NT)
                else:
                    acc[...] += mm(inner_grad, w1[j], NT)
            for k in range(2):
                keep_y(c, k, VALID).start()
            grad, shift_grad, scale_grad = norm_backward(
                rows[c].astype(F32), scale_of(c), base[c].astype(F32), acc[...]
            )
            back[c] = grad
            send_backward(c, VALID).start()
            put_sums(c, 0, shift_grad)
            put_sums(c, 1, scale_grad)
            return carry

        lax.fori_loop(0, 2, backward, 0)
        for c in range(2):
            send_hidden(c, VALID).wait()
            keep_hidden(c, VALID).wait()
            send_mixed(c, VALID, bgs, c).wait()
            keep_mixed(c, VALID, bgs, c).wait()
            send_forward(c, KEPT, picked).wait_send()
            send_rows2(c).wait_send()
            send_backward(c, VALID).wait_send()
            for k in range(2):
                keep_x(c, k, VALID, c * 4 + high * 2 + k).wait()
                keep_y(c, k, VALID).wait()

    @pl.when(section == 2)
    def _():
        def forward(c, carry):
            send_forward(c, KEPT, outs).wait_recv()
            attend(c, KEPT, None)
            return carry

        def backward(c, carry):
            send_backward(c, KEPT).wait_recv()
            attend_back(c, KEPT, None, True)
            return carry

        lax.fori_loop(0, 2, forward, 0)
        lax.fori_loop(0, 2, backward, 0)
        finish_attention(KEPT, True)

    def send_result(c, q):
        return copies.remote(
            "result", c, outs.at[c, :, pl.ds(256 * q, WINDOW)], window_out.at[c], (dp, q), c * 4 + q
        )

    @pl.when(section == 3)
    def _():
        for j in range(4):
            load_w2(j).wait()
        for c in range(2):
            for s in (0, 1, 2):
                take_og(c, s).wait_recv()
            whole = join(grads, c, packs[1, c], 3)
            low = pick_kept(whole, kept_ref[c : c + 1, :])
            base[c, part(KEPT)] = low
            bg = (low.astype(F32) * gate_of(c)).astype(BF)
            bgs[c, part(KEPT)] = bg
            send_mixed(c, KEPT, bgs, c).start()
            keep_mixed(c, KEPT, bgs, c).start()

        def run(c, carry):
            send_forward(c, KEPT, outs).wait_recv()
            hid = norm_forward(rows[c, part(KEPT)].astype(F32), shift_of(c), scale_of(c))
            hidden[c, part(KEPT)] = hid
            send_hidden(c, KEPT).start()
            keep_hidden(c, KEPT).start()
            bg = bgs[c, part(KEPT)]
            for j in range(4):
                active, slope = gelu_pair(mm(hid, w1[j]))
                low = active.astype(BF)
                inner_grad = (mm(bg, w2[j], NT) * slope).astype(BF)
                big[c * 4 + j, part(KEPT)] = low
                big[8 + c * 4 + j, part(KEPT)] = inner_grad
                ahead, behind = mm(low, w2[j]), mm(inner_grad, w1[j], NT)
                if j == 0:
                    parts[0, part(KEPT)] = ahead
                    parts[1, part(KEPT)] = behind
                else:
                    parts[0, part(KEPT)] += ahead
                    parts[1, part(KEPT)] += behind
            x = rows[c, part(KEPT)].astype(F32)
            upstream = base[c, part(KEPT)].astype(F32)
            grad, shift_grad, scale_grad = norm_backward(x, scale_of(c), upstream, parts[1, part(KEPT)])
            back[c, part(KEPT)] = grad
            send_backward(c, KEPT).start()
            out = parts[0, part(KEPT)]
            picked[c] = (x + gate_of(c) * out).astype(BF)
            put_sums(c, 0, shift_grad)
            put_sums(c, 1, scale_grad)
            put_sums(c, 2, jnp.sum(upstream * out, axis=0, keepdims=True))
            for k in range(2):
                keep_x(c, k, KEPT, c * 4 + high * 2 + k).start()
                keep_y(c, k, KEPT).start()
            return carry

        lax.fori_loop(0, 2, run, 0)
        for c in range(2):
            send_rows2(c).wait_recv()
            outs[c] = merge_kept(rows2[c], picked[c], kept_ref[c : c + 1, :])
            for q in range(3):
                send_result(c, q).start()
            copies.local("result", c * 4 + 3, outs.at[c, :, pl.ds(768, WINDOW)], window_out.at[c]).start()
        for c in range(2):
            send_hidden(c, KEPT).wait()
            keep_hidden(c, KEPT).wait()
            send_mixed(c, KEPT, bgs, c).wait()
            keep_mixed(c, KEPT, bgs, c).wait()
            send_backward(c, KEPT).wait_send()
            for k in range(2):
                keep_x(c, k, KEPT, c * 4 + high * 2 + k).wait()
                keep_y(c, k, KEPT).wait()
            for q in range(3):
                send_result(c, q).wait_send()
            copies.local("result", c * 4 + 3, outs.at[c, :, pl.ds(768, WINDOW)], window_out.at[c]).wait()

    @pl.when(section != 3)
    def _():
        for c in range(2):
            send_result(c, 0).wait_recv()

    for c in range(2):

        @pl.when(section != 0)
        def _():
            send_in(c).wait_send()

        for target in (3, 1):

            @pl.when(section != target)
            def _():
                send_og(c, target).wait_send()

    packed_out[...] = small[...].astype(BF)


def pipeline(grid_shape, canvas_in, out_grad, kept_rank, conditioning, bias, w1, w2, wm):
    anywhere = pl.BlockSpec(memory_space=pl.ANY)
    vmem = pl.BlockSpec(memory_space=VMEM)
    canvas = array(2, VALID, D)
    count = sum(n for _, n in PIPE_COPIES)
    return pl.pallas_call(
        pipeline_kernel,
        in_specs=[pl.BlockSpec(memory_space=pltpu.SMEM)] + [vmem] * 5 + [anywhere] * 3,
        out_specs=[anywhere] * 8 + [vmem],
        out_shape=[canvas] * 4 + [array(2, 2, VALID, D)] * 2 + [canvas, array(2, VALID, WINDOW), array(PACKED, 128)],
        scratch_shapes=[
            VMEM((4, D, D), BF),
            VMEM((4, D, D), BF),
            VMEM((2, VALID, D), BF),
            VMEM((2, 2, VALID, WINDOW), BF),
            VMEM((2, 4, VALID, WINDOW), BF),
            VMEM((2, 4, VALID, WINDOW), BF),
            VMEM((2, VALID, D), BF),
            VMEM((2, VALID, D), BF),
            VMEM((2, VALID, D), BF),
            VMEM((16, VALID, D), BF),
            VMEM((2, VALID, D), BF),
            VMEM((2, VALID, D), BF),
            VMEM((2, KEPT, D), BF),
            VMEM((2, VALID, D), BF),
            VMEM((2, VALID, D), BF),
            VMEM((3, VALID, D), F32),
            VMEM((VALID, D), F32),
            VMEM((2, VALID, D), BF),
            VMEM((2, 3, D), F32),
            VMEM((PACKED, 128), F32),
            pltpu.SemaphoreType.DMA((count,)),
            pltpu.SemaphoreType.DMA((count,)),
        ],
        compiler_params=pltpu.CompilerParams(collective_id=1, has_side_effects=True, vmem_limit_bytes=63 * 2**20),
        cost_estimate=cost(40e9, 60e6),
        name="pipeline",
    )(grid_shape, canvas_in, out_grad, kept_rank, conditioning, bias, w1, w2, wm)


FLOWS = ((0, "y", 0, 640), (0, "z", 640, 512), (1, "y", 0, 512), (1, "z", 512, 640))
CUT = 80
FINAL_COPIES = (
    ("flow", 12 * len(FLOWS)), ("left", 8), ("right", 8), ("other", 8), ("weights", 4),
    ("gather_y", 6), ("gather_z", 6), ("gather_x", 1), ("window", 8),
)


def final_kernel(
    shape_ref, packed_ref, result_ref, hidden_own, hidden_other, mixed_own, mixed_other, x_own, y_own, grad_own, w1_hbm, w2_hbm,
    first_out, second_out, result_out, canvas_out, all_packed,
    left, right, other, w1, w2, sums_first, sums_second, windows_in, *scratch,
):
    count = len(FLOWS)
    ones, twos, threes, sums, tiny1, tiny2, tiny3 = (scratch[i * count : (i + 1) * count] for i in range(7))
    copies = Copies(scratch[7 * count], scratch[7 * count + 1])
    for key, number in FINAL_COPIES:
        copies.name(key, number)
    dp, section = lax.axis_index("dp"), lax.axis_index("section")
    x, z, y = dp // 16, (dp // 4) % 4, dp % 4
    place = {"y": y, "z": z}
    is_odd = section % 2 == 1

    def neighbour(axis, by):
        if axis == "y":
            return (x * 16 + z * 4 + (y + by) % 4, section)
        return (x * 16 + ((z + by) % 4) * 4 + y, section)

    partner = ((dp + 16) % 32, section)
    barrier = pltpu.get_barrier_semaphore()
    for axis in ("y", "z"):
        for by in (1, 2, 3):
            pl.semaphore_signal(barrier, inc=1, device_id=neighbour(axis, by), device_id_type=MESH)
    pl.semaphore_signal(barrier, inc=1, device_id=partner, device_id_type=MESH)

    @pl.when(section != 0)
    def _():
        pl.semaphore_signal(barrier, inc=1, device_id=(dp, 0), device_id_type=MESH)

    def load(r, feed):
        part = pl.ds(0, r)
        result = []
        for c in range(2):
            for k in range(2):
                result.append(copies.local("left", c * 2 + k, x_own.at[c, k, part], left.at[k, pl.ds(c * r, r)]))
                target = other if feed else left
                at = c * r if feed else (2 + c) * r
                result.append(copies.local("left", 4 + c * 2 + k, y_own.at[c, k, part], target.at[k, pl.ds(at, r)]))
            result.append(copies.local("right", c, hidden_own.at[c, part], right.at[0, pl.ds(c * r, r)]))
            result.append(copies.local("right", 2 + c, hidden_other.at[c, part], right.at[0, pl.ds((2 + c) * r, r)]))
            result.append(copies.local("right", 4 + c, mixed_own.at[c, part], right.at[1, pl.ds(c * r, r)]))
            result.append(copies.local("right", 6 + c, mixed_other.at[c, part], right.at[1, pl.ds((2 + c) * r, r)]))
        if feed:
            for k in range(2):
                columns = pl.ds((x * 2 + k) * D, D)
                result.append(copies.local("weights", k, w1_hbm.at[:, columns], w1.at[k]))
                result.append(copies.local("weights", 2 + k, w2_hbm.at[columns, :], w2.at[k]))
        return result

    for which, (r, feed) in enumerate(((VALID, False), (VALID, True), (KEPT, False), (KEPT, True))):

        @pl.when(section == which)
        def _():
            for c in load(r, feed):
                c.start()

    all_packed[x, z, y] = packed_ref[...]

    def put(target, k, value):
        target[pl.ds(8 * k, 8)] = value.astype(BF).reshape(8, BLOCK, D)

    def first_products(r, feed):
        for c in load(r, feed):
            c.wait()
        rows = pl.ds(0, 4 * r)
        if feed:
            for c in range(2):
                hid, bg = right[0, pl.ds((2 + c) * r, r)], right[1, pl.ds((2 + c) * r, r)]
                for k in range(2):
                    active, slope = gelu_pair(mm(hid, w1[k]))
                    inner_grad = mm(bg, w2[k], NT) * slope
                    left[k, pl.ds((2 + c) * r, r)] = active.astype(BF)
                    other[k, pl.ds((2 + c) * r, r)] = inner_grad.astype(BF)
            for k in range(2):
                put(sums_first, k, mm(other[k, rows], right[0, rows], TN))
        else:
            put(sums_first, 0, mm(left[0, rows], right[0, rows], TN))

            @pl.when(x == 0)
            def _():
                put(sums_first, 1, mm(left[1, rows], right[0, rows], TN))

            @pl.when(x == 1)
            def _():
                put(sums_first, 1, mm(left[1, rows], right[1, rows], TN))

    def second_products(r):
        rows = pl.ds(0, 4 * r)
        for k in range(2):
            put(sums_second, k, mm(left[k, rows], right[1, rows], TN))

    data = (sums_first, sums_second)
    outs = (first_out, second_out)
    halves = (pl.ds(0, 2), pl.ds(2, 2))
    cuts = (pl.ds(0, CUT), pl.ds(CUT, BLOCK - CUT))

    def axes(flow):
        axis = FLOWS[flow][1]
        return axis, "z" if axis == "y" else "y"

    def step(flow, phase, kind, side, source, target):
        number = ((flow * 2 + phase) * 3 + kind) * 2 + side
        return copies.remote("flow", number, source, target, neighbour(axes(flow)[phase], (1, 3)[side]))

    def block(flow, by, half):
        which, axis, low, width = FLOWS[flow]
        position = (place[axis] + by) % 4
        columns = pl.ds(low, width)
        if axis == "y":
            return [data[which].at[4 * (2 * half + i) + position, :, columns] for i in range(2)]
        return [data[which].at[4 * position + 2 * half + i, :, columns] for i in range(2)]

    def pair_ref(flow, by, half):
        which, axis, low, width = FLOWS[flow]
        position = (place[axis] + by) % 4
        columns = pl.ds(low, width)
        grid = data[which].reshape(4, 4, BLOCK, D)
        if axis == "y":
            return grid.at[pl.ds(2 * half, 2), position, :, columns]
        return grid.at[position, pl.ds(2 * half, 2), :, columns]

    def first_a(flow, side):
        return step(flow, 0, 0, side, pair_ref(flow, 2, side), ones[flow].at[side])

    def first_b(flow, side):
        return step(flow, 0, 1, side, pair_ref(flow, (1, 3)[side], 1 - side), twos[flow].at[side])

    def first_c(flow, side):
        return step(flow, 0, 2, side, ones[flow].at[side], threes[flow].at[side])

    def slab(flow, by, cut):
        return sums[flow].at[(place[axes(flow)[1]] + by) % 4, cut]

    def second_a(flow, side):
        return step(flow, 1, 0, side, slab(flow, 2, cuts[side]), tiny1[flow].at[cuts[side]])

    def second_b(flow, side):
        cut = cuts[1 - side]
        return step(flow, 1, 1, side, slab(flow, (1, 3)[side], cut), tiny2[flow].at[cut])

    def second_c(flow, side):
        return step(flow, 1, 2, side, tiny1[flow].at[cuts[side]], tiny3[flow].at[cuts[side]])

    def begin(flow):
        for side in (0, 1):
            first_a(flow, side).start()
        for side in (0, 1):
            first_b(flow, side).start()

    def forward(flow):
        for side in (0, 1):
            first_a(flow, side).wait()
            own = block(flow, (1, 3)[side], side)
            for i in range(2):
                total = ones[flow][side, i].astype(F32) + own[i][...].astype(F32)
                ones[flow][side, i] = total.astype(BF)
            first_c(flow, side).start()

    def middle(flow):
        for side in (0, 1):
            first_b(flow, side).wait()
            first_c(flow, side).wait()
        for half in (0, 1):
            own = block(flow, 0, half)
            for i in range(2):
                total = own[i][...].astype(F32) + threes[flow][half, i].astype(F32)
                sums[flow][2 * half + i] = (total + twos[flow][1 - half, i].astype(F32)).astype(BF)
        for side in (0, 1):
            second_a(flow, side).start()
        for side in (0, 1):
            second_b(flow, side).start()

    def late(flow):
        for side in (0, 1):
            second_a(flow, side).wait()
            own = slab(flow, (1, 3)[side], cuts[side])[...]
            tiny1[flow][cuts[side]] = (tiny1[flow][cuts[side]].astype(F32) + own.astype(F32)).astype(BF)
            second_c(flow, side).start()

    def finish(flow):
        which, axis, low, width = FLOWS[flow]
        for side in (0, 1):
            second_b(flow, side).wait()
            second_c(flow, side).wait()
        own = sums[flow][place[axes(flow)[1]]].astype(F32)
        outs[which][:, low : low + width] = own + tiny2[flow][...].astype(F32) + tiny3[flow][...].astype(F32)

    even = [i for i, f in enumerate(FLOWS) if f[0] == 0]
    odd = [i for i, f in enumerate(FLOWS) if f[0] == 1]

    def stage(work, flows):
        for flow in flows:
            work(flow)

    def gather(axis, by):
        if axis == "y":
            ref = all_packed.at[x, z, y]
            return copies.remote("gather_y", by - 1, ref, ref, neighbour("y", by), 2 + by)
        if axis == "z":
            ref = all_packed.at[x, z]
            return copies.remote("gather_z", by - 1, ref, ref, neighbour("z", by), 2 + by)
        return copies.remote("gather_x", 0, all_packed.at[x], all_packed.at[x], partner)

    def gathered(axis, by):
        if axis == "y":
            ref = all_packed.at[x, z, (y + 4 - by) % 4]
            return copies.remote("gather_y", by - 1, ref, ref, neighbour("y", by), 2 + by)
        if axis == "z":
            ref = all_packed.at[x, (z + 4 - by) % 4]
            return copies.remote("gather_z", by - 1, ref, ref, neighbour("z", by), 2 + by)
        ref = all_packed.at[1 - x]
        return copies.remote("gather_x", 0, ref, ref, partner)

    def window(c, q):
        source = grad_own.at[c, :, pl.ds(256 * q, WINDOW)]
        return copies.remote("window", c * 4, source, windows_in.at[c], (dp, q), c * 4 + q)

    def own_window(c):
        return copies.local("window", c * 4, grad_own.at[c, :, pl.ds(0, WINDOW)], windows_in.at[c])

    shift = shift_matrix(section)

    def unpack(value, c):
        lane = lax.broadcasted_iota(jnp.int32, (SLOTS, VALID), 1)
        hot = (lane == token_of_slot(shape_ref[c], 0)).astype(BF)
        return mm(hot, mm(value, shift, NT).astype(BF)).astype(BF)

    @pl.when(section == 0)
    def _():
        pl.semaphore_wait(barrier, 10)

    @pl.when(section != 0)
    def _():
        pl.semaphore_wait(barrier, 7)

    @pl.when(section == 0)
    def _():
        for c in range(2):
            own_window(c).start()
            for q in (1, 2, 3):
                window(c, q).start()

    for by in (1, 2, 3):
        gather("y", by).start()

    for which, (r, feed) in enumerate(((VALID, False), (VALID, True), (KEPT, False), (KEPT, True))):

        @pl.when(section == which)
        def _():
            first_products(r, feed)

    stage(begin, even)
    for by in (1, 2, 3):
        gather("y", by).wait_send()
        gathered("y", by).wait_recv()
    for by in (1, 2, 3):
        gather("z", by).start()

    for r, which in ((VALID, 1), (KEPT, 3)):

        @pl.when(section == which)
        def _():
            second_products(r)

    @pl.when(is_odd)
    def _():
        stage(begin, odd)

    @pl.when(jnp.logical_not(is_odd))
    def _():
        second_out[...] = jnp.zeros_like(second_out)

    stage(forward, even)
    for by in (1, 2, 3):
        gather("z", by).wait_send()
        gathered("z", by).wait_recv()
    gather("x", 0).start()

    @pl.when(is_odd)
    def _():
        stage(forward, odd)

    for c in range(2):
        result_out[c] = unpack(result_ref[c], c)
    for work in (middle, late, finish):
        stage(work, even)

        @pl.when(is_odd)
        def _():
            stage(work, odd)

    gather("x", 0).wait_send()
    gathered("x", 0).wait_recv()

    for c in range(2):

        @pl.when(section == 0)
        def _():
            own_window(c).wait()
            for q in (1, 2, 3):
                window(c, q).wait_send()

        @pl.when(section != 0)
        def _():
            window(c, 0).wait_recv()

        canvas_out[c] = unpack(windows_in[c], c)


def final(grid_shape, packed, result_window, parts, w1, w2):
    anywhere = pl.BlockSpec(memory_space=pl.ANY)
    vmem = pl.BlockSpec(memory_space=VMEM)
    widths = [f[3] for f in FLOWS]
    pair = [VMEM((2, 2, BLOCK, w), BF) for w in widths]
    tiny = [VMEM((BLOCK, w), BF) for w in widths]
    count = sum(n for _, n in FINAL_COPIES)
    canvas = array(2, SLOTS, QUARTER)
    return pl.pallas_call(
        final_kernel,
        in_specs=[pl.BlockSpec(memory_space=pltpu.SMEM)] + [vmem] * 2 + [anywhere] * 9,
        out_specs=[vmem] * 5,
        out_shape=[array(BLOCK, D, dtype=F32)] * 2 + [canvas] * 2 + [array(2, 4, 4, PACKED, 128)],
        scratch_shapes=[
            VMEM((2, 4 * VALID, D), BF),
            VMEM((2, 4 * VALID, D), BF),
            VMEM((2, 4 * VALID, D), BF),
            VMEM((2, D, D), BF),
            VMEM((2, D, D), BF),
            VMEM((16, BLOCK, D), BF),
            VMEM((16, BLOCK, D), BF),
            VMEM((2, VALID, WINDOW), BF),
        ]
        + pair * 3
        + [VMEM((4, BLOCK, w), BF) for w in widths]
        + tiny * 3
        + [pltpu.SemaphoreType.DMA((count,)), pltpu.SemaphoreType.DMA((count,))],
        compiler_params=pltpu.CompilerParams(collective_id=0, has_side_effects=True, vmem_limit_bytes=63 * 2**20),
        cost_estimate=cost(20e9, 60e6),
        name="final",
    )(grid_shape, packed, result_window, *parts, w1, w2)


def local(
    canvas_in,
    conditioning,
    grid_shape,
    kept_rank,
    first_weight,
    second_weight,
    modulation_weight,
    modulation_bias,
    out_grad,
):
    w1, w2 = first_weight[0], second_weight[0]
    outputs = pipeline(
        grid_shape, canvas_in, out_grad, kept_rank, conditioning, modulation_bias, w1, w2, modulation_weight[0]
    )
    first_sum, second_sum, result, canvas_grad, packed = final(grid_shape, outputs[8], outputs[7], outputs[:7], w1, w2)
    packed = packed.reshape(32, PACKED, 128)
    all_sums = packed[:, :54].reshape(64, 3 * D)
    all_signal = packed[:, 54:72].reshape(64, D)
    modulation_grad = mm(all_signal, all_sums, TN)
    bias_grad = jnp.sum(all_sums.astype(F32), axis=0)
    return (
        result,
        canvas_grad,
        first_sum.T[None],
        second_sum[None],
        modulation_grad[None],
        bias_grad[None],
    )


def solution(mesh):
    placed = (
        P("dp", None, "section"),
        P("dp", None),
        P("dp"),
        P("dp", None),
        P("section", None, None),
        P("section", None, None),
        P("section", None, None),
        P("section", None),
        P("dp", None, "section"),
    )
    return jax.shard_map(
        local,
        mesh=mesh,
        in_specs=placed,
        out_specs=(
            P("dp", None, "section"),
            P("dp", None, "section"),
            P("section", None, "dp"),
            P("section", "dp", None),
            P("section", None, None),
            P("section", None),
        ),
        check_vma=False,
    )
```

```python
import functools
import math

import jax
import jax.numpy as jnp
from jax import lax
from jax.experimental import pallas as pl
from jax.experimental.pallas import tpu as pltpu
from jax.sharding import PartitionSpec as P

HEADS = 16
SIDE = 20
SLOTS = SIDE * SIDE
VALID = 256
KEPT = 128
D = 1152
FF = 4608
HALF = FF // 2
QUARTER = D // 4
WINDOW = 384
PACKED = 80
EARLY = 512
HEAD = D // HEADS
BLOCK = FF // 32
EPSILON = 1e-06
FACTOR = 1.0 / math.sqrt(HEAD)
LOG2E = math.log2(math.e)
NEGATIVE = -1e30
BF = jnp.bfloat16
F32 = jnp.float32
VMEM = pltpu.VMEM
MESH = pl.DeviceIdType.MESH
NT = (((1,), (1,)), ((), ()))
TN = (((0,), (0,)), ((), ()))
C0 = math.sqrt(2.0 / math.pi)


def mm(a, b, dims=(((1,), (0,)), ((), ()))):
    return lax.dot_general(a, b, dims, preferred_element_type=F32)


def cost(flops, nbytes):
    return pl.CostEstimate(flops=int(flops), bytes_accessed=int(nbytes), transcendentals=0)


def array(*shape, dtype=BF):
    return jax.ShapeDtypeStruct(shape, dtype)


def norm_stats(x):
    mean = jnp.mean(x, axis=-1, keepdims=True)
    centred = x - mean
    rstd = lax.rsqrt(jnp.mean(centred * centred, axis=-1, keepdims=True) + EPSILON)
    return centred * rstd, rstd


def norm_forward(rows, shift, scale):
    normed, _ = norm_stats(rows)
    return (normed * (1.0 + scale) + shift).astype(BF)


def norm_backward(rows, scale, upstream, hidden_grad):
    normed, rstd = norm_stats(rows)
    shift_grad = jnp.sum(hidden_grad, axis=0, keepdims=True)
    scale_grad = jnp.sum(hidden_grad * normed, axis=0, keepdims=True)
    scaled = hidden_grad * (1.0 + scale)
    mean_scaled = jnp.mean(scaled, axis=-1, keepdims=True)
    mean_product = jnp.mean(scaled * normed, axis=-1, keepdims=True)
    grad = upstream + (scaled - mean_scaled - normed * mean_product) * rstd
    return grad.astype(BF), shift_grad, scale_grad


def gelu_pair(v):
    square = v * v
    t = jnp.tanh(v * (C0 + (C0 * 0.044715) * square))
    half = 0.5 * (1.0 + t)
    slope = half + (0.5 * v) * (1.0 - t * t) * (C0 + (3.0 * C0 * 0.044715) * square)
    return v * half, slope


def kept_spread(kept_row):
    line = lax.broadcasted_iota(jnp.int32, (VALID, KEPT), 0)
    return (line == kept_row).astype(F32)


def pick_kept(rows, kept_row):
    return mm(kept_spread(kept_row).astype(BF), rows, TN).astype(BF)


def merge_kept(base, kept_rows, kept_row):
    spread = kept_spread(kept_row)
    chosen = jnp.sum(spread, axis=1, keepdims=True) > 0.5
    return jnp.where(chosen, mm(spread.astype(BF), kept_rows).astype(BF), base)


def grid_of(shape_id):
    lines = jnp.where(shape_id == 1, 12, jnp.where(shape_id == 2, 20, 16))
    width = jnp.where(shape_id == 1, 20, jnp.where(shape_id == 2, 12, 16))
    return lines, width


def slots_of_tokens(shape_id):
    lines, width = grid_of(shape_id)
    slot = lax.broadcasted_iota(jnp.int32, (1, SLOTS), 1)
    line = (slot * 3277) >> 16
    column = slot - line * SIDE
    token = jnp.where((line < lines) & (column < width), line * width + column, -1)
    return (lax.broadcasted_iota(jnp.int32, (VALID, SLOTS), 0) == token).astype(BF)


def shift_matrix(section):
    line = lax.broadcasted_iota(jnp.int32, (QUARTER, WINDOW), 0)
    lane = lax.broadcasted_iota(jnp.int32, (QUARTER, WINDOW), 1)
    return (lane == line + 32 * section).astype(BF)


HEADS_OF_GROUP = ((0, 0), (0, 72), (128, 16), (128, 88))


def overlaid(parts):
    first, last = parts[0] + parts[1], parts[2] + parts[3]
    return jnp.concatenate([first[:, 0:128], first[:, 128:256] + last[:, 0:128], last[:, 128:256]], axis=1)


def only_head(value, offset):
    lane = lax.broadcasted_iota(jnp.int32, value.shape, 1)
    return jnp.where((lane >= offset) & (lane < offset + HEAD), value, jnp.zeros_like(value))


def key_bias(live, keys):
    lane = lax.broadcasted_iota(jnp.int32, (1, keys), 1)
    return jnp.where(lane < live, 0.0, NEGATIVE).astype(F32)


def softmax_of(q, k, bias):
    scores = mm(q, k, NT)
    if bias is not None:
        scores = scores + bias
    top = jnp.max(scores, axis=-1, keepdims=True)
    grown = jnp.exp2((scores - top) * (FACTOR * LOG2E))
    return grown * (1.0 / jnp.sum(grown, axis=-1, keepdims=True))


class Copies:
    def __init__(self, send, arrive):
        self.send, self.arrive, self.first, self.size = send, arrive, {}, 0

    def name(self, key, count):
        self.first[key] = self.size
        self.size += count

    def remote(self, key, index, source, target, device, sender=None):
        at = self.first[key]
        return pltpu.make_async_remote_copy(
            src_ref=source,
            dst_ref=target,
            send_sem=self.send.at[at + (index if sender is None else sender)],
            recv_sem=self.arrive.at[at + index],
            device_id=device,
            device_id_type=MESH,
        )

    def local(self, key, index, source, target):
        return pltpu.make_async_copy(source, target, self.send.at[self.first[key] + index])


PIPE_COPIES = (
    ("wm", 3), ("w1", 2), ("w2", 2), ("in", 8), ("og", 16), ("forward", 2), ("done", 2), ("backward", 2), ("result", 8),
    ("hidden", 2), ("mixed", 2), ("pair", 8), ("own_hidden", 2), ("own_mixed", 2), ("own_x", 2), ("own_y", 2), ("own_grad", 2),
    ("other_hidden", 2), ("other_active", 2), ("other_slope", 2),
)


def pipeline_kernel(
    shape_ref, canvas_ref, ograd_ref, kept_ref, cond_ref, bias_ref, w1_hbm, w2_hbm, wm_hbm,
    hidden_own, hidden_other, mixed_own, mixed_other, x_own, y_own, grad_own, active_other, slope_other, window_out, packed_out,
    w1, w2, rows, packs, packs_kept, quarters, grads, up, base, hidden, big, branch, outs, picked, landed, back, bgs, parts, acc, up_mixed, hidden2, extra, mod,
    small, send, arrive, go,
):
    dp, section = lax.axis_index("dp"), lax.axis_index("section")
    high = dp // 16
    partner = ((dp + 16) % 32, section)
    copies = Copies(send, arrive)
    for key, count in PIPE_COPIES:
        copies.name(key, count)
    is_feed = section % 2 == 1

    def load_wm(j):
        return copies.local("wm", j, wm_hbm.at[:, pl.ds(j * D, D)], w2.at[j // 2, pl.ds(j % 2 * D, D)])

    def load_w1(j):
        return copies.local("w1", j, w1_hbm.at[:, pl.ds(j * HALF, HALF)], w1.at[j])

    def load_w2(j):
        return copies.local("w2", j, w2_hbm.at[pl.ds(j * HALF, HALF), :], w2.at[j])

    barrier = pltpu.get_barrier_semaphore()
    for by in (1, 2, 3):
        pl.semaphore_signal(barrier, inc=1, device_id=(dp, (section + by) % 4), device_id_type=MESH)
    pl.semaphore_signal(barrier, inc=1, device_id=partner, device_id_type=MESH)

    for j in range(3):
        load_wm(j).start()
    for j in range(2):
        load_w1(j).start()

    shift = shift_matrix(section)

    def pack(source, c):
        return mm(mm(slots_of_tokens(shape_ref[c]), source[c], NT).astype(BF), shift).astype(BF)

    def send_in(c):
        return copies.remote("in", c * 4 + section, packs.at[0, c], quarters.at[c, section], (dp, 0), c * 4)

    def og_copy(c, s, target):
        if target == 3:
            source, landing = packs_kept.at[c], grads.at[c, s, pl.ds(0, KEPT)]
        else:
            source, landing = packs.at[1, c], grads.at[c, s]
        return copies.remote("og", c * 4 + s, source, landing, (dp, target), 8 + c * 4 + target)

    def take_in(c, s):
        return copies.remote("in", c * 4 + s, packs.at[0, c], quarters.at[c, s], (dp, 0), c * 4)

    packs[0, 0] = pack(canvas_ref, 0)
    pl.semaphore_wait(barrier, 4)

    @pl.when(section != 0)
    def _():
        send_in(0).start()

    packs[0, 1] = pack(canvas_ref, 1)

    @pl.when(section >= 2)
    def _():
        send_in(0).wait_send()

    @pl.when(section != 0)
    def _():
        send_in(1).start()

    for c in range(2):
        low = pack(ograd_ref, c)
        packs[1, c] = low
        packs_kept[c] = pick_kept(low, kept_ref[c : c + 1, :])

    cond = cond_ref[...].astype(F32)
    signal = (cond * (1.0 / (1.0 + jnp.exp(-cond)))).astype(BF)
    small[...] = jnp.zeros_like(small)
    for c in range(2):
        for i in range(9):
            small[54 + c * 9 + i : 55 + c * 9 + i, :] = signal[c : c + 1, i * 128 : (i + 1) * 128].astype(F32)
    for j in range(3):
        load_wm(j).wait()
        part = mm(signal, w2[j // 2, j % 2 * D : (j % 2 + 1) * D]) + bias_ref[:, j * D : (j + 1) * D]
        for c in range(2):
            mod[c, j : j + 1, :] = part[c : c + 1, :]

    @pl.when(is_feed)
    def _():
        for j in range(2):
            load_w2(j).start()

    @pl.when(section >= 2)
    def _():
        send_in(1).wait_send()

    for target in (3, 1):
        for c in range(2):

            @pl.when(section != target)
            def _():
                og_copy(c, section, target).start()

    for j in range(2):
        load_w1(j).wait()

    def shift_of(c):
        return mod[c, 0:1, :]

    def scale_of(c):
        return mod[c, 1:2, :]

    def gate_of(c):
        return mod[c, 2:3, :]

    def put_sums(c, which, value):
        for i in range(9):
            small[pl.ds(c * 27 + which * 9 + i, 1), :] = value[:, i * 128 : (i + 1) * 128]

    def join(parts_ref, c, r, own, target):
        tiles = {}
        for q in range(4):
            value = own if q == target else parts_ref[c, q, part(r)]
            for t in range(3):
                tile = value[:, t * 128 : (t + 1) * 128]
                at = 2 * q + t
                tiles[at] = tile if at not in tiles else tiles[at] + tile
        return jnp.concatenate([tiles[t] for t in range(9)], axis=1)

    def part(r):
        return pl.ds(0, r)

    def send_forward(c, r, source):
        return copies.remote("forward", c, source.at[c, part(r)], rows.at[c, part(r)], (dp, (section + 1) % 4))

    def send_backward(c, r):
        return copies.remote("backward", c, back.at[c, part(r)], up.at[c, part(r)], (dp, (section + 3) % 4))

    def send_done(c):
        return copies.remote("done", c, picked.at[c], landed.at[c], (dp, 1))

    def send_hidden(c, r):
        return copies.remote("hidden", c, hidden.at[c, part(r)], hidden2.at[c, part(r)], partner)

    def keep_hidden(c, r):
        return copies.local("own_hidden", c, hidden.at[c, part(r)], hidden_own.at[c, part(r)])

    def send_mixed(c, r, source, at):
        return copies.remote("mixed", c, source.at[at, part(r)], mixed_other.at[c, part(r)], partner)

    def keep_mixed(c, r, source, at):
        return copies.local("own_mixed", c, source.at[at, part(r)], mixed_own.at[c, part(r)])

    def keep_x(c, r, at):
        return copies.local("own_x", c, big.at[at, part(r)], x_own.at[c, part(r)])

    def keep_y(c, r):
        return copies.local("own_y", c, big.at[4 + c * 2 + high, part(r)], y_own.at[c, part(r)])

    def send_pair(c, k, half, r):
        columns = pl.ds(k * D + (0, EARLY)[half], (EARLY, D - EARLY)[half])
        source = big.at[4 + c * 2 + 1 - high, part(r), columns]
        return copies.remote("pair", (c * 2 + k) * 2 + half, source, y_own.at[c, part(r), columns], partner)

    def mixed_keep(c, r):
        return copies.local("own_mixed", c, big.at[c * 2 + 1, part(r), pl.ds(D, D)], mixed_own.at[c, part(r)])

    def mixed_send(c, r):
        source = big.at[c * 2 + 1, part(r), pl.ds(D, D)]
        return copies.remote("mixed", c, source, mixed_other.at[c, part(r)], partner)

    def keep_grad(c):
        return copies.local("own_grad", c, back.at[c], grad_own.at[c])

    def attend(c, r, live):
        x = rows[c, part(r)].astype(F32)
        hid = norm_forward(x, shift_of(c), scale_of(c))
        hidden[c, part(r)] = hid
        send_hidden(c, r).start()
        keep_hidden(c, r).start()
        big[c * 2, part(r)] = mm(hid, w1[0]).astype(BF)
        big[c * 2 + 1, part(r), 0:D] = mm(hid, w1[1, :, 0:D]).astype(BF)
        bias = None if live is None else key_bias(live, r)
        parts[0, part(r)] = jnp.zeros((r, D), F32)

        def group(g, carry):
            cut = pl.ds(pl.multiple_of(g * 256, 128), WINDOW)
            cut_k = pl.ds(pl.multiple_of(D + g * 256, 128), WINDOW)
            q4 = big[c * 2, part(r), cut]
            k4 = big[c * 2, part(r), cut_k]
            v4 = big[c * 2 + 1, part(r), cut]
            results = []
            for start, offset in HEADS_OF_GROUP:
                side = slice(start, start + 256)
                q = only_head(q4[:, side], offset + 32 * g)
                v = only_head(v4[:, side], offset + 32 * g)
                results.append(mm(softmax_of(q, k4[:, side], bias).astype(BF), v))
            parts[0, part(r), cut] += overlaid(results)
            return carry

        lax.fori_loop(0, 4, group, 0)
        mixed = parts[0, part(r)].astype(BF)
        big[c * 2 + 1, part(r), D:HALF] = mixed
        mixed_keep(c, r).start()
        out = mm(mixed, w1[1, :, D:HALF])
        branch[c, part(r)] = out.astype(BF)
        outs[c, part(r)] = (rows[c, part(r)].astype(F32) + gate_of(c) * out).astype(BF)
        send_forward(c, r, outs).start()

    def attend_back(c, r, live, to_section):
        upstream = up[c, part(r)].astype(F32)
        put_sums(c, 2, jnp.sum(upstream * branch[c, part(r)].astype(F32), axis=0, keepdims=True))
        bg = (upstream * gate_of(c)).astype(BF)
        big[4 + c * 2 + 1, part(r), D:HALF] = bg
        up_mixed[part(r)] = mm(bg, w1[1, :, D:HALF], NT).astype(BF)
        bias = None if live is None else key_bias(live, r)
        parts[:, part(r)] = jnp.zeros((3, r, D), F32)

        def put_parts(low, width):
            cut = pl.ds(low, width)
            big[4 + c * 2, part(r), cut] = (parts[0, part(r), cut] * FACTOR).astype(BF)
            big[4 + c * 2, part(r), pl.ds(D + low, width)] = (parts[1, part(r), cut] * FACTOR).astype(BF)
            big[4 + c * 2 + 1, part(r), cut] = parts[2, part(r), cut].astype(BF)

        def group(g, carry):
            if not to_section:

                @pl.when(g == 2)
                def _():
                    put_parts(0, EARLY)
                    for k in range(2):
                        send_pair(c, k, 0, r).start()

            cut = pl.ds(pl.multiple_of(g * 256, 128), WINDOW)
            cut_k = pl.ds(pl.multiple_of(D + g * 256, 128), WINDOW)
            q4 = big[c * 2, part(r), cut]
            k4 = big[c * 2, part(r), cut_k]
            v4 = big[c * 2 + 1, part(r), cut]
            mg4 = up_mixed[part(r), cut]
            dq, dk, dv = [], [], []
            for start, offset in HEADS_OF_GROUP:
                side = slice(start, start + 256)
                q = only_head(q4[:, side], offset + 32 * g)
                k = only_head(k4[:, side], offset + 32 * g)
                mg = only_head(mg4[:, side], offset + 32 * g)
                soft = softmax_of(q, k, bias)
                soft_grad = mm(mg, v4[:, side], NT)
                dv.append(mm(soft.astype(BF), mg, TN))
                product = soft * soft_grad
                score_grad = (product - soft * jnp.sum(product, axis=-1, keepdims=True)).astype(BF)
                dq.append(mm(score_grad, k))
                dk.append(mm(score_grad, q, TN))
            parts[0, part(r), cut] += overlaid(dq)
            parts[1, part(r), cut] += overlaid(dk)
            parts[2, part(r), cut] += overlaid(dv)
            return carry

        lax.fori_loop(0, 4, group, 0)
        if to_section:
            put_parts(0, EARLY)
        put_parts(EARLY, D - EARLY)
        if not to_section:
            for k in range(2):
                send_pair(c, k, 1, r).start()
        keep_x(c, r, 4 + c * 2 + high).start()
        hidden_grad = mm(big[4 + c * 2, part(r)], w1[0], NT)
        hidden_grad += mm(big[4 + c * 2 + 1, part(r), 0:D], w1[1, :, 0:D], NT)
        grad, shift_grad, scale_grad = norm_backward(
            rows[c, part(r)].astype(F32), scale_of(c), up[c, part(r)].astype(F32), hidden_grad
        )
        back[c, part(r)] = grad
        if to_section:
            send_backward(c, r).start()
        else:
            keep_grad(c).start()
        put_sums(c, 0, shift_grad)
        put_sums(c, 1, scale_grad)

    def exchange_mixed(r):
        for c in range(2):

            @pl.when(high == 0)
            def _():
                mixed_send(c, r).start()

    def finish_attention(r, to_section):
        for c in range(2):
            send_hidden(c, r).wait()
            keep_hidden2(c, r).start()
            keep_hidden(c, r).wait()

            @pl.when(high == 0)
            def _():
                mixed_send(c, r).wait_send()

            @pl.when(high == 1)
            def _():
                mixed_send(c, r).wait_recv()

            mixed_keep(c, r).wait()
            send_forward(c, r, outs).wait_send()
            keep_x(c, r, 4 + c * 2 + high).wait()
            for k in range(2):
                for half in range(2):
                    send_pair(c, k, half, r).wait()
            keep_hidden2(c, r).wait()
            if not to_section:
                keep_grad(c).wait()

    def keep_hidden2(c, r):
        return copies.local("other_hidden", c, hidden2.at[c, part(r)], hidden_other.at[c, part(r)])

    def keep_other(c, r):
        return (
            keep_hidden2(c, r),
            copies.local("other_active", c, extra.at[0, c, part(r)], active_other.at[c, part(r)]),
            copies.local("other_slope", c, extra.at[1, c, part(r)], slope_other.at[c, part(r)]),
        )

    def work_for_partner(c, r):
        active, slope = gelu_pair(mm(hidden2[c, part(r)], w1[high]))
        extra[0, c, part(r)] = active.astype(BF)
        extra[1, c, part(r)] = slope.astype(BF)
        for copy in keep_other(c, r):
            copy.start()

    def send_result(c, q):
        return copies.remote(
            "result", c, outs.at[c, :, pl.ds(256 * q, WINDOW)], window_out.at[c], (dp, q), c * 4 + q
        )

    def keep_result(c):
        return copies.local("result", c * 4 + 1, outs.at[c, :, pl.ds(256, WINDOW)], window_out.at[c])

    @pl.when(section == 0)
    def _():
        def live_of(c):
            lines, width = grid_of(shape_ref[c])
            return lines * width

        def forward(c, carry):
            for s in (1, 2, 3):
                take_in(c, s).wait_recv()
            rows[c] = join(quarters, c, VALID, packs[0, c], 0)
            attend(c, VALID, live_of(c))
            return carry

        def backward(c, carry):
            send_backward(c, VALID).wait_recv()
            attend_back(c, VALID, live_of(c), False)
            return carry

        lax.fori_loop(0, 2, forward, 0)
        pl.semaphore_wait(go, 1)
        exchange_mixed(VALID)
        lax.fori_loop(0, 2, backward, 0)
        finish_attention(VALID, False)

    @pl.when(section == 1)
    def _():
        for j in range(2):
            load_w2(j).wait()

        def forward(c, carry):
            send_forward(c, VALID, outs).wait_recv()
            hid = norm_forward(rows[c].astype(F32), shift_of(c), scale_of(c))
            hidden[c] = hid
            keep_hidden(c, VALID).start()
            for j in range(2):
                active, slope = gelu_pair(mm(hid, w1[j]))
                low = active.astype(BF)
                big[c * 2 + j] = low
                big[4 + c * 2 + j] = slope.astype(BF)
                if j == 0:
                    acc[...] = mm(low, w2[j])
                else:
                    acc[...] += mm(low, w2[j])
            keep_x(c, VALID, c * 2 + high).start()
            out = acc[...]
            branch[c] = out.astype(BF)
            low = (rows[c].astype(F32) + gate_of(c) * out).astype(BF)
            outs[c] = low
            picked[c] = pick_kept(low, kept_ref[pl.ds(c, 1), :])
            send_forward(c, KEPT, picked).start()
            return carry

        lax.fori_loop(0, 2, forward, 0)
        for c in range(2):
            send_forward(c, KEPT, picked).wait_send()
        for c in range(2):
            send_hidden(c, VALID).start()
        for c in range(2):
            for s in (0, 2, 3):
                og_copy(c, s, 1).wait_recv()
            base[c] = join(grads, c, VALID, packs[1, c], 1)
        for c in range(2):
            send_hidden(c, VALID).wait()
        pl.semaphore_signal(go, inc=1, device_id=(dp, 0), device_id_type=MESH)
        for c in range(2):
            work_for_partner(c, VALID)
        for c in range(2):
            send_done(c).wait_recv()
            outs[c] = merge_kept(outs[c], landed[c], kept_ref[c : c + 1, :])
            for q in (0, 2, 3):
                send_result(c, q).start()
            keep_result(c).start()

        def backward(c, carry):
            send_backward(c, KEPT).wait_recv()
            low = merge_kept(base[c], up[c, part(KEPT)], kept_ref[pl.ds(c, 1), :])
            base[c] = low
            upstream = low.astype(F32)
            bg = (upstream * gate_of(c)).astype(BF)
            bgs[c] = bg
            send_mixed(c, VALID, bgs, c).start()
            keep_mixed(c, VALID, bgs, c).start()
            put_sums(c, 2, jnp.sum(upstream * branch[c].astype(F32), axis=0, keepdims=True))
            for j in range(2):
                slope = big[4 + c * 2 + j].astype(F32)
                inner_grad = (mm(bg, w2[j], NT) * slope).astype(BF)
                big[4 + c * 2 + j] = inner_grad
                if j == 0:
                    acc[...] = mm(inner_grad, w1[j], NT)
                else:
                    acc[...] += mm(inner_grad, w1[j], NT)
            keep_y(c, VALID).start()
            grad, shift_grad, scale_grad = norm_backward(
                rows[c].astype(F32), scale_of(c), base[c].astype(F32), acc[...]
            )
            back[c] = grad
            send_backward(c, VALID).start()
            put_sums(c, 0, shift_grad)
            put_sums(c, 1, scale_grad)
            return carry

        lax.fori_loop(0, 2, backward, 0)
        for c in range(2):
            for copy in keep_other(c, VALID):
                copy.wait()
            keep_hidden(c, VALID).wait()
            send_mixed(c, VALID, bgs, c).wait()
            keep_mixed(c, VALID, bgs, c).wait()
            send_backward(c, VALID).wait_send()
            for q in (0, 2, 3):
                send_result(c, q).wait_send()
            keep_result(c).wait()
            keep_x(c, VALID, c * 2 + high).wait()
            keep_y(c, VALID).wait()

    @pl.when(section == 2)
    def _():
        def forward(c, carry):
            send_forward(c, KEPT, outs).wait_recv()
            attend(c, KEPT, None)
            return carry

        def backward(c, carry):
            send_backward(c, KEPT).wait_recv()
            attend_back(c, KEPT, None, True)
            return carry

        lax.fori_loop(0, 2, forward, 0)
        exchange_mixed(KEPT)
        lax.fori_loop(0, 2, backward, 0)
        for c in range(2):
            send_backward(c, KEPT).wait_send()
        for c in range(2):
            for k in range(2):
                for half in range(2):
                    send_pair(c, k, half, KEPT).start()
        finish_attention(KEPT, True)


    @pl.when(section == 3)
    def _():
        for j in range(2):
            load_w2(j).wait()
        for c in range(2):
            for s in (0, 1, 2):
                og_copy(c, s, 3).wait_recv()
            low = join(grads, c, KEPT, packs_kept[c], 3)
            base[c, part(KEPT)] = low
            bg = (low.astype(F32) * gate_of(c)).astype(BF)
            bgs[c, part(KEPT)] = bg
            send_mixed(c, KEPT, bgs, c).start()
            keep_mixed(c, KEPT, bgs, c).start()

        def run(c, carry):
            send_forward(c, KEPT, outs).wait_recv()
            hid = norm_forward(rows[c, part(KEPT)].astype(F32), shift_of(c), scale_of(c))
            hidden[c, part(KEPT)] = hid
            send_hidden(c, KEPT).start()
            keep_hidden(c, KEPT).start()
            bg = bgs[c, part(KEPT)]
            for j in range(2):
                active, slope = gelu_pair(mm(hid, w1[j]))
                low = active.astype(BF)
                inner_grad = (mm(bg, w2[j], NT) * slope).astype(BF)
                big[c * 2 + j, part(KEPT)] = low
                big[4 + c * 2 + j, part(KEPT)] = inner_grad
                ahead, behind = mm(low, w2[j]), mm(inner_grad, w1[j], NT)
                if j == 0:
                    parts[0, part(KEPT)] = ahead
                    parts[1, part(KEPT)] = behind
                else:
                    parts[0, part(KEPT)] += ahead
                    parts[1, part(KEPT)] += behind
            x = rows[c, part(KEPT)].astype(F32)
            upstream = base[c, part(KEPT)].astype(F32)
            grad, shift_grad, scale_grad = norm_backward(x, scale_of(c), upstream, parts[1, part(KEPT)])
            back[c, part(KEPT)] = grad
            send_backward(c, KEPT).start()
            out = parts[0, part(KEPT)]
            picked[c] = (x + gate_of(c) * out).astype(BF)
            send_done(c).start()
            put_sums(c, 0, shift_grad)
            put_sums(c, 1, scale_grad)
            put_sums(c, 2, jnp.sum(upstream * out, axis=0, keepdims=True))
            keep_x(c, KEPT, c * 2 + high).start()
            keep_y(c, KEPT).start()
            return carry

        lax.fori_loop(0, 2, run, 0)
        for c in range(2):
            send_hidden(c, KEPT).wait()
            work_for_partner(c, KEPT)
        for c in range(2):
            for copy in keep_other(c, KEPT):
                copy.wait()
            keep_hidden(c, KEPT).wait()
            send_mixed(c, KEPT, bgs, c).wait()
            keep_mixed(c, KEPT, bgs, c).wait()
            send_backward(c, KEPT).wait_send()
            keep_x(c, KEPT, c * 2 + high).wait()
            keep_y(c, KEPT).wait()
            send_done(c).wait_send()

    @pl.when(section != 1)
    def _():
        for c in range(2):
            send_result(c, 0).wait_recv()

    for c in range(2):

        @pl.when(section == 1)
        def _():
            send_in(c).wait_send()

        for target in (3, 1):

            @pl.when(section != target)
            def _():
                og_copy(c, section, target).wait_send()

    packed_out[...] = small[...].astype(BF)


def pipeline(grid_shape, canvas_in, out_grad, kept_rank, conditioning, bias, w1, w2, wm):
    anywhere = pl.BlockSpec(memory_space=pl.ANY)
    vmem = pl.BlockSpec(memory_space=VMEM)
    canvas = array(2, VALID, D)
    count = sum(n for _, n in PIPE_COPIES)
    return pl.pallas_call(
        pipeline_kernel,
        in_specs=[pl.BlockSpec(memory_space=pltpu.SMEM)] + [vmem] * 5 + [anywhere] * 3,
        out_specs=[anywhere] * 10 + [vmem],
        out_shape=[canvas] * 4
        + [array(2, VALID, HALF)] * 2
        + [canvas]
        + [array(2, VALID, HALF)] * 2
        + [array(2, VALID, WINDOW), array(PACKED, 128)],
        scratch_shapes=[
            VMEM((2, D, HALF), BF),
            VMEM((2, HALF, D), BF),
            VMEM((2, VALID, D), BF),
            VMEM((2, 2, VALID, WINDOW), BF),
            VMEM((2, KEPT, WINDOW), BF),
            VMEM((2, 4, VALID, WINDOW), BF),
            VMEM((2, 4, VALID, WINDOW), BF),
            VMEM((2, VALID, D), BF),
            VMEM((2, VALID, D), BF),
            VMEM((2, VALID, D), BF),
            VMEM((8, VALID, HALF), BF),
            VMEM((2, VALID, D), BF),
            VMEM((2, VALID, D), BF),
            VMEM((2, KEPT, D), BF),
            VMEM((2, KEPT, D), BF),
            VMEM((2, VALID, D), BF),
            VMEM((2, VALID, D), BF),
            VMEM((3, VALID, D), F32),
            VMEM((VALID, D), F32),
            VMEM((VALID, D), BF),
            VMEM((2, VALID, D), BF),
            VMEM((2, 2, VALID, HALF), BF),
            VMEM((2, 3, D), F32),
            VMEM((PACKED, 128), F32),
            pltpu.SemaphoreType.DMA((count,)),
            pltpu.SemaphoreType.DMA((count,)),
            pltpu.SemaphoreType.REGULAR,
        ],
        compiler_params=pltpu.CompilerParams(collective_id=1, has_side_effects=True, vmem_limit_bytes=63 * 2**20),
        cost_estimate=cost(40e9, 60e6),
        name="pipeline",
    )(grid_shape, canvas_in, out_grad, kept_rank, conditioning, bias, w1, w2, wm)


FLOWS = ((0, "y", 0, 640), (0, "z", 640, 512), (1, "y", 0, 512), (1, "z", 512, 640))
CUT = 80
FINAL_COPIES = (
    ("flow", 48), ("left", 8), ("right", 8), ("weights", 1),
    ("gather_y", 6), ("gather_z", 6), ("gather_x", 1), ("window", 8),
)


def final_kernel(
    shape_ref, packed_ref, result_ref, hidden_own, hidden_other, mixed_own, mixed_other, x_own, y_own, grad_own, active_other, slope_other, w2_hbm,
    first_out, second_out, result_out, canvas_out, all_packed,
    left, right, other, w2, sums_first, sums_second, windows_in, *scratch,
):
    count = len(FLOWS)
    ones, twos, threes, sums, tiny1, tiny2, tiny3 = (scratch[i * count : (i + 1) * count] for i in range(7))
    copies = Copies(scratch[7 * count], scratch[7 * count + 1])
    for key, number in FINAL_COPIES:
        copies.name(key, number)
    dp, section = lax.axis_index("dp"), lax.axis_index("section")
    x, z, y = dp // 16, (dp // 4) % 4, dp % 4
    place = {"y": y, "z": z}
    is_odd = section % 2 == 1

    def neighbour(axis, by):
        if axis == "y":
            return (x * 16 + z * 4 + (y + by) % 4, section)
        return (x * 16 + ((z + by) % 4) * 4 + y, section)

    partner = ((dp + 16) % 32, section)
    barrier = pltpu.get_barrier_semaphore()
    for axis in ("y", "z"):
        for by in (1, 2, 3):
            pl.semaphore_signal(barrier, inc=1, device_id=neighbour(axis, by), device_id_type=MESH)
    pl.semaphore_signal(barrier, inc=1, device_id=partner, device_id_type=MESH)

    @pl.when(section != 0)
    def _():
        pl.semaphore_signal(barrier, inc=1, device_id=(dp, 0), device_id_type=MESH)

    def load_left(r, feed):
        result = []
        for c in range(2):
            part, own, theirs = pl.ds(0, r), pl.ds(c * r, r), pl.ds((2 + c) * r, r)
            result.append(copies.local("left", c, x_own.at[c, part], left.at[own]))
            if feed:
                result.append(copies.local("left", 2 + c, active_other.at[c, part], left.at[theirs]))
            else:
                result.append(copies.local("left", 2 + c, y_own.at[c, part], left.at[theirs]))
            result.append(copies.local("right", 4 + c, mixed_own.at[c, part], right.at[1, own]))
            result.append(copies.local("right", 6 + c, mixed_other.at[c, part], right.at[1, theirs]))
        return result

    def load_right(r, feed):
        result = []
        for c in range(2):
            part, own, theirs = pl.ds(0, r), pl.ds(c * r, r), pl.ds((2 + c) * r, r)
            if feed:
                result.append(copies.local("left", 4 + c, y_own.at[c, part], other.at[own]))
                result.append(copies.local("left", 6 + c, slope_other.at[c, part], other.at[theirs]))
            result.append(copies.local("right", c, hidden_own.at[c, part], right.at[0, own]))
            result.append(copies.local("right", 2 + c, hidden_other.at[c, part], right.at[0, theirs]))
        if feed:
            result.append(copies.local("weights", 0, w2_hbm.at[pl.ds(x * HALF, HALF), :], w2))
        return result

    for which, (r, feed) in enumerate(((VALID, False), (VALID, True), (KEPT, False), (KEPT, True))):

        @pl.when(section == which)
        def _():
            for c in load_left(r, feed) + load_right(r, feed):
                c.start()

    all_packed[x, z, y] = packed_ref[...]

    def put(target, k, value):
        target[pl.ds(8 * k, 8)] = value.astype(BF).reshape(8, BLOCK, D)

    def columns(k):
        return pl.ds(pl.multiple_of(k * D, 128), D)

    data = (sums_first, sums_second)
    outs = (first_out, second_out)
    halves = (pl.ds(0, 2), pl.ds(2, 2))
    cuts = (pl.ds(0, CUT), pl.ds(CUT, BLOCK - CUT))

    def axes(flow):
        axis = FLOWS[flow][1]
        return axis, "z" if axis == "y" else "y"

    def step(flow, phase, kind, side, source, target):
        number = ((flow * 2 + phase) * 3 + kind) * 2 + side
        return copies.remote("flow", number, source, target, neighbour(axes(flow)[phase], (1, 3)[side]))

    def block(flow, by, half):
        which, axis, low, width = FLOWS[flow]
        position = (place[axis] + by) % 4
        columns = pl.ds(low, width)
        if axis == "y":
            return [data[which].at[4 * (2 * half + i) + position, :, columns] for i in range(2)]
        return [data[which].at[4 * position + 2 * half + i, :, columns] for i in range(2)]

    def pair_ref(flow, by, half):
        which, axis, low, width = FLOWS[flow]
        position = (place[axis] + by) % 4
        columns = pl.ds(low, width)
        grid = data[which].reshape(4, 4, BLOCK, D)
        if axis == "y":
            return grid.at[pl.ds(2 * half, 2), position, :, columns]
        return grid.at[position, pl.ds(2 * half, 2), :, columns]

    def first_a(flow, side):
        return step(flow, 0, 0, side, pair_ref(flow, 2, side), ones[flow].at[side])

    def first_b(flow, side):
        return step(flow, 0, 1, side, pair_ref(flow, (1, 3)[side], 1 - side), twos[flow].at[side])

    def first_c(flow, side):
        return step(flow, 0, 2, side, ones[flow].at[side], threes[flow].at[side])

    def slab(flow, by, cut):
        return sums[flow].at[(place[axes(flow)[1]] + by) % 4, cut]

    def second_a(flow, side):
        return step(flow, 1, 0, side, slab(flow, 2, cuts[side]), tiny1[flow].at[cuts[side]])

    def second_b(flow, side):
        cut = cuts[1 - side]
        return step(flow, 1, 1, side, slab(flow, (1, 3)[side], cut), tiny2[flow].at[cut])

    def second_c(flow, side):
        return step(flow, 1, 2, side, tiny1[flow].at[cuts[side]], tiny3[flow].at[cuts[side]])

    def begin(flow):
        for side in (0, 1):
            first_a(flow, side).start()
        for side in (0, 1):
            first_b(flow, side).start()

    def forward(flow):
        for side in (0, 1):
            first_a(flow, side).wait()
            own = block(flow, (1, 3)[side], side)
            for i in range(2):
                total = ones[flow][side, i].astype(F32) + own[i][...].astype(F32)
                ones[flow][side, i] = total.astype(BF)
            first_c(flow, side).start()

    def middle(flow):
        for side in (0, 1):
            first_b(flow, side).wait()
            first_c(flow, side).wait()
        for half in (0, 1):
            own = block(flow, 0, half)
            for i in range(2):
                total = own[i][...].astype(F32) + threes[flow][half, i].astype(F32)
                sums[flow][2 * half + i] = (total + twos[flow][1 - half, i].astype(F32)).astype(BF)
        for side in (0, 1):
            second_a(flow, side).start()
        for side in (0, 1):
            second_b(flow, side).start()

    def late(flow):
        for side in (0, 1):
            second_a(flow, side).wait()
            own = slab(flow, (1, 3)[side], cuts[side])[...]
            tiny1[flow][cuts[side]] = (tiny1[flow][cuts[side]].astype(F32) + own.astype(F32)).astype(BF)
            second_c(flow, side).start()

    def finish(flow):
        which, axis, low, width = FLOWS[flow]
        for side in (0, 1):
            second_b(flow, side).wait()
            second_c(flow, side).wait()
        own = sums[flow][place[axes(flow)[1]]].astype(F32)
        outs[which][:, low : low + width] = own + tiny2[flow][...].astype(F32) + tiny3[flow][...].astype(F32)

    even = [i for i, f in enumerate(FLOWS) if f[0] == 0]
    odd = [i for i, f in enumerate(FLOWS) if f[0] == 1]

    def stage(work, flows):
        for flow in flows:
            work(flow)

    def gather(axis, by):
        if axis == "y":
            ref = all_packed.at[x, z, y]
            return copies.remote("gather_y", by - 1, ref, ref, neighbour("y", by), 2 + by)
        if axis == "z":
            ref = all_packed.at[x, z]
            return copies.remote("gather_z", by - 1, ref, ref, neighbour("z", by), 2 + by)
        return copies.remote("gather_x", 0, all_packed.at[x], all_packed.at[x], partner)

    def gathered(axis, by):
        if axis == "y":
            ref = all_packed.at[x, z, (y + 4 - by) % 4]
            return copies.remote("gather_y", by - 1, ref, ref, neighbour("y", by), 2 + by)
        if axis == "z":
            ref = all_packed.at[x, (z + 4 - by) % 4]
            return copies.remote("gather_z", by - 1, ref, ref, neighbour("z", by), 2 + by)
        ref = all_packed.at[1 - x]
        return copies.remote("gather_x", 0, ref, ref, partner)

    def window(c, q):
        source = grad_own.at[c, :, pl.ds(256 * q, WINDOW)]
        return copies.remote("window", c * 4, source, windows_in.at[c], (dp, q), c * 4 + q)

    def own_window(c):
        return copies.local("window", c * 4, grad_own.at[c, :, pl.ds(0, WINDOW)], windows_in.at[c])

    shift = shift_matrix(section)

    def unpack(value, c):
        return mm(mm(value, shift, NT).astype(BF), slots_of_tokens(shape_ref[c]), TN).astype(BF)

    @pl.when(section == 0)
    def _():
        pl.semaphore_wait(barrier, 10)

    @pl.when(section != 0)
    def _():
        pl.semaphore_wait(barrier, 7)

    @pl.when(section == 0)
    def _():
        for c in range(2):
            own_window(c).start()
            for q in (1, 2, 3):
                window(c, q).start()

    for by in (1, 2, 3):
        gather("y", by).start()

    def attention_products(r):
        rows = pl.ds(0, 4 * r)
        for copy in load_left(r, False) + load_right(r, False):
            copy.wait()

        def product(k, carry):
            put(sums_first, k, mm(left[rows, columns(k)], right[x * k, rows], TN))
            return carry

        lax.fori_loop(0, 2, product, 0)
        stage(begin, even)
        second_out[...] = jnp.zeros_like(second_out)

    def feed_products(r):
        rows = pl.ds(0, 4 * r)
        for copy in load_left(r, True):
            copy.wait()

        def second_product(k, carry):
            put(sums_second, k, mm(left[rows, columns(k)], right[1, rows], TN))
            return carry

        def first_product(k, carry):
            put(sums_first, k, mm(other[rows, columns(k)], right[0, rows], TN))

            @pl.when(k == 0)
            def _():
                stage(forward, odd)

            return carry

        lax.fori_loop(0, 2, second_product, 0)
        stage(begin, odd)
        for copy in load_right(r, True):
            copy.wait()

        def inner_gradient(c, carry):
            theirs = pl.ds(pl.multiple_of((2 + c) * r, 128), r)
            active_grad = mm(right[1, theirs], w2[...], NT)
            other[theirs] = (active_grad * other[theirs].astype(F32)).astype(BF)
            return carry

        lax.fori_loop(0, 2, inner_gradient, 0)
        lax.fori_loop(0, 2, first_product, 0)
        stage(begin, even)

    for which, r in ((0, VALID), (2, KEPT)):

        @pl.when(section == which)
        def _():
            attention_products(r)

    for which, r in ((1, VALID), (3, KEPT)):

        @pl.when(section == which)
        def _():
            feed_products(r)

    for by in (1, 2, 3):
        gather("y", by).wait_send()
        gathered("y", by).wait_recv()
    for by in (1, 2, 3):
        gather("z", by).start()

    @pl.when(is_odd)
    def _():
        stage(middle, odd)

    stage(forward, even)
    for by in (1, 2, 3):
        gather("z", by).wait_send()
        gathered("z", by).wait_recv()
    gather("x", 0).start()
    for c in range(2):
        result_out[c] = unpack(result_ref[c], c)
    for work, later in ((middle, late), (late, finish)):

        @pl.when(is_odd)
        def _():
            stage(later, odd)

        stage(work, even)
    stage(finish, even)

    gather("x", 0).wait_send()
    gathered("x", 0).wait_recv()

    for c in range(2):

        @pl.when(section == 0)
        def _():
            own_window(c).wait()
            for q in (1, 2, 3):
                window(c, q).wait_send()

        @pl.when(section != 0)
        def _():
            window(c, 0).wait_recv()

        canvas_out[c] = unpack(windows_in[c], c)


def final(grid_shape, packed, result_window, parts, w2):
    anywhere = pl.BlockSpec(memory_space=pl.ANY)
    vmem = pl.BlockSpec(memory_space=VMEM)
    widths = [f[3] for f in FLOWS]
    pair = [VMEM((2, 2, BLOCK, w), BF) for w in widths]
    tiny = [VMEM((BLOCK, w), BF) for w in widths]
    count = sum(n for _, n in FINAL_COPIES)
    canvas = array(2, QUARTER, SLOTS)
    return pl.pallas_call(
        final_kernel,
        in_specs=[pl.BlockSpec(memory_space=pltpu.SMEM)] + [vmem] * 2 + [anywhere] * 10,
        out_specs=[vmem] * 5,
        out_shape=[array(BLOCK, D, dtype=F32)] * 2 + [canvas] * 2 + [array(2, 4, 4, PACKED, 128)],
        scratch_shapes=[
            VMEM((4 * VALID, HALF), BF),
            VMEM((2, 4 * VALID, D), BF),
            VMEM((4 * VALID, HALF), BF),
            VMEM((HALF, D), BF),
            VMEM((16, BLOCK, D), BF),
            VMEM((16, BLOCK, D), BF),
            VMEM((2, VALID, WINDOW), BF),
        ]
        + pair * 3
        + [VMEM((4, BLOCK, w), BF) for w in widths]
        + tiny * 3
        + [pltpu.SemaphoreType.DMA((count,)), pltpu.SemaphoreType.DMA((count,))],
        compiler_params=pltpu.CompilerParams(collective_id=0, has_side_effects=True, vmem_limit_bytes=63 * 2**20),
        cost_estimate=cost(20e9, 60e6),
        name="final",
    )(grid_shape, packed, result_window, *parts, w2)


def local(
    canvas_in,
    conditioning,
    grid_shape,
    kept_rank,
    first_weight,
    second_weight,
    modulation_weight,
    modulation_bias,
    out_grad,
):
    w1, w2 = first_weight[0], second_weight[0]
    outputs = pipeline(
        grid_shape,
        canvas_in.transpose(0, 2, 1),
        out_grad.transpose(0, 2, 1),
        kept_rank,
        conditioning,
        modulation_bias,
        w1,
        w2,
        modulation_weight[0],
    )
    first_sum, second_sum, result, canvas_grad, packed = final(grid_shape, outputs[10], outputs[9], outputs[:9], w2)
    packed = packed.reshape(32, PACKED, 128)
    all_sums = packed[:, :54].reshape(64, 3 * D)
    all_signal = packed[:, 54:72].reshape(64, D)
    modulation_grad = mm(all_signal, all_sums, TN)
    bias_grad = jnp.sum(all_sums.astype(F32), axis=0)
    return (
        result.transpose(0, 2, 1),
        canvas_grad.transpose(0, 2, 1),
        first_sum.T[None],
        second_sum[None],
        modulation_grad[None],
        bias_grad[None],
    )


def solution(mesh):
    placed = (
        P("dp", None, "section"),
        P("dp", None),
        P("dp"),
        P("dp", None),
        P("section", None, None),
        P("section", None, None),
        P("section", None, None),
        P("section", None),
        P("dp", None, "section"),
    )
    return jax.shard_map(
        local,
        mesh=mesh,
        in_specs=placed,
        out_specs=(
            P("dp", None, "section"),
            P("dp", None, "section"),
            P("section", None, "dp"),
            P("section", "dp", None),
            P("section", None, None),
            P("section", None),
        ),
        check_vma=False,
    )
```

```python
import functools
import math

import jax
import jax.numpy as jnp
from jax import lax
from jax.experimental import pallas as pl
from jax.experimental.pallas import tpu as pltpu
from jax.sharding import PartitionSpec as P

HEADS = 16
SIDE = 20
SLOTS = SIDE * SIDE
VALID = 256
KEPT = 128
D = 1152
FF = 4608
HALF = FF // 2
QUARTER = D // 4
WINDOW = 384
PACKED = 80
EARLY = 512
HEAD = D // HEADS
BLOCK = FF // 32
EPSILON = 1e-06
FACTOR = 1.0 / math.sqrt(HEAD)
LOG2E = math.log2(math.e)
NEGATIVE = -1e30
BF = jnp.bfloat16
F32 = jnp.float32
VMEM = pltpu.VMEM
MESH = pl.DeviceIdType.MESH
NT = (((1,), (1,)), ((), ()))
TN = (((0,), (0,)), ((), ()))
C0 = math.sqrt(2.0 / math.pi)


def mm(a, b, dims=(((1,), (0,)), ((), ()))):
    return lax.dot_general(a, b, dims, preferred_element_type=F32)


def cost(flops, nbytes):
    return pl.CostEstimate(flops=int(flops), bytes_accessed=int(nbytes), transcendentals=0)


def array(*shape, dtype=BF):
    return jax.ShapeDtypeStruct(shape, dtype)


def norm_stats(x):
    mean = jnp.mean(x, axis=-1, keepdims=True)
    centred = x - mean
    rstd = lax.rsqrt(jnp.mean(centred * centred, axis=-1, keepdims=True) + EPSILON)
    return centred * rstd, rstd


def norm_forward(rows, shift, scale):
    normed, _ = norm_stats(rows)
    return (normed * (1.0 + scale) + shift).astype(BF)


def norm_backward(rows, scale, upstream, hidden_grad):
    normed, rstd = norm_stats(rows)
    shift_grad = jnp.sum(hidden_grad, axis=0, keepdims=True)
    scale_grad = jnp.sum(hidden_grad * normed, axis=0, keepdims=True)
    scaled = hidden_grad * (1.0 + scale)
    mean_scaled = jnp.mean(scaled, axis=-1, keepdims=True)
    mean_product = jnp.mean(scaled * normed, axis=-1, keepdims=True)
    grad = upstream + (scaled - mean_scaled - normed * mean_product) * rstd
    return grad.astype(BF), shift_grad, scale_grad


def gelu_pair(v):
    square = v * v
    t = jnp.tanh(v * (C0 + (C0 * 0.044715) * square))
    half = 0.5 * (1.0 + t)
    slope = half + (0.5 * v) * (1.0 - t * t) * (C0 + (3.0 * C0 * 0.044715) * square)
    return v * half, slope


def kept_spread(kept_row):
    line = lax.broadcasted_iota(jnp.int32, (VALID, KEPT), 0)
    return (line == kept_row).astype(F32)


def pick_kept(rows, kept_row):
    return mm(kept_spread(kept_row).astype(BF), rows, TN).astype(BF)


def merge_kept(base, kept_rows, kept_row):
    spread = kept_spread(kept_row)
    chosen = jnp.sum(spread, axis=1, keepdims=True) > 0.5
    return jnp.where(chosen, mm(spread.astype(BF), kept_rows).astype(BF), base)


def grid_of(shape_id):
    lines = jnp.where(shape_id == 1, 12, jnp.where(shape_id == 2, 20, 16))
    width = jnp.where(shape_id == 1, 20, jnp.where(shape_id == 2, 12, 16))
    return lines, width


def slots_of_tokens(shape_id):
    lines, width = grid_of(shape_id)
    slot = lax.broadcasted_iota(jnp.int32, (1, SLOTS), 1)
    line = (slot * 3277) >> 16
    column = slot - line * SIDE
    token = jnp.where((line < lines) & (column < width), line * width + column, -1)
    return (lax.broadcasted_iota(jnp.int32, (VALID, SLOTS), 0) == token).astype(BF)


def shift_matrix(section):
    line = lax.broadcasted_iota(jnp.int32, (QUARTER, WINDOW), 0)
    lane = lax.broadcasted_iota(jnp.int32, (QUARTER, WINDOW), 1)
    return (lane == line + 32 * section).astype(BF)


HEADS_OF_GROUP = ((0, 0), (0, 72), (128, 16), (128, 88))


def overlaid(parts):
    first, last = parts[0] + parts[1], parts[2] + parts[3]
    return jnp.concatenate([first[:, 0:128], first[:, 128:256] + last[:, 0:128], last[:, 128:256]], axis=1)


def only_head(value, offset):
    lane = lax.broadcasted_iota(jnp.int32, value.shape, 1)
    return jnp.where((lane >= offset) & (lane < offset + HEAD), value, jnp.zeros_like(value))


def key_bias(live, keys):
    lane = lax.broadcasted_iota(jnp.int32, (1, keys), 1)
    return jnp.where(lane < live, 0.0, NEGATIVE).astype(F32)


def softmax_of(q, k, bias):
    scores = mm(q, k, NT)
    if bias is not None:
        scores = scores + bias
    top = jnp.max(scores, axis=-1, keepdims=True)
    grown = jnp.exp2((scores - top) * (FACTOR * LOG2E))
    return grown * (1.0 / jnp.sum(grown, axis=-1, keepdims=True))


class Copies:
    def __init__(self, send, arrive):
        self.send, self.arrive, self.first, self.size = send, arrive, {}, 0

    def name(self, key, count):
        self.first[key] = self.size
        self.size += count

    def remote(self, key, index, source, target, device, sender=None):
        at = self.first[key]
        return pltpu.make_async_remote_copy(
            src_ref=source,
            dst_ref=target,
            send_sem=self.send.at[at + (index if sender is None else sender)],
            recv_sem=self.arrive.at[at + index],
            device_id=device,
            device_id_type=MESH,
        )

    def local(self, key, index, source, target):
        return pltpu.make_async_copy(source, target, self.send.at[self.first[key] + index])


PIPE_COPIES = (
    ("wm", 3), ("w1", 2), ("w2", 2), ("in", 8), ("og", 16), ("forward", 2), ("done", 2), ("backward", 2), ("result", 8),
    ("hidden", 2), ("mixed", 2), ("pair", 8), ("own_hidden", 2), ("own_mixed", 2), ("own_x", 2), ("own_y", 2), ("own_grad", 2),
    ("other_hidden", 2), ("other_active", 2), ("other_slope", 2),
)


def pipeline_kernel(
    shape_ref, canvas_ref, ograd_ref, kept_ref, cond_ref, bias_ref, w1_hbm, w2_hbm, wm_hbm,
    hidden_own, hidden_other, mixed_own, mixed_other, x_own, y_own, grad_own, active_other, slope_other, window_out, packed_out,
    w1, w2, rows, packs, packs_kept, quarters, grads, up, base, hidden, big, branch, outs, picked, landed, back, bgs, parts, acc, up_mixed, hidden2, extra, mod,
    small, send, arrive, go,
):
    dp, section = lax.axis_index("dp"), lax.axis_index("section")
    high = dp // 16
    partner = ((dp + 16) % 32, section)
    copies = Copies(send, arrive)
    for key, count in PIPE_COPIES:
        copies.name(key, count)
    is_feed = section % 2 == 1

    def load_wm(j):
        return copies.local("wm", j, wm_hbm.at[:, pl.ds(j * D, D)], w2.at[j // 2, pl.ds(j % 2 * D, D)])

    def load_w1(j):
        return copies.local("w1", j, w1_hbm.at[:, pl.ds(j * HALF, HALF)], w1.at[j])

    def load_w2(j):
        return copies.local("w2", j, w2_hbm.at[pl.ds(j * HALF, HALF), :], w2.at[j])

    barrier = pltpu.get_barrier_semaphore()
    for by in (1, 2, 3):
        pl.semaphore_signal(barrier, inc=1, device_id=(dp, (section + by) % 4), device_id_type=MESH)
    pl.semaphore_signal(barrier, inc=1, device_id=partner, device_id_type=MESH)

    for j in range(3):
        load_wm(j).start()
    for j in range(2):
        load_w1(j).start()

    shift = shift_matrix(section)

    def pack(source, c):
        return mm(mm(slots_of_tokens(shape_ref[c]), source[c], NT).astype(BF), shift).astype(BF)

    def send_in(c):
        return copies.remote("in", c * 4 + section, packs.at[0, c], quarters.at[c, section], (dp, 0), c * 4)

    def og_copy(c, s, target):
        if target == 3:
            source, landing = packs_kept.at[c], grads.at[c, s, pl.ds(0, KEPT)]
        else:
            source, landing = packs.at[1, c], grads.at[c, s]
        return copies.remote("og", c * 4 + s, source, landing, (dp, target), 8 + c * 4 + target)

    def take_in(c, s):
        return copies.remote("in", c * 4 + s, packs.at[0, c], quarters.at[c, s], (dp, 0), c * 4)

    packs[0, 0] = pack(canvas_ref, 0)
    pl.semaphore_wait(barrier, 4)

    @pl.when(section != 0)
    def _():
        send_in(0).start()

    packs[0, 1] = pack(canvas_ref, 1)

    @pl.when(section >= 2)
    def _():
        send_in(0).wait_send()

    @pl.when(section != 0)
    def _():
        send_in(1).start()

    for c in range(2):
        low = pack(ograd_ref, c)
        packs[1, c] = low
        packs_kept[c] = pick_kept(low, kept_ref[c : c + 1, :])

    cond = cond_ref[...].astype(F32)
    signal = (cond * (1.0 / (1.0 + jnp.exp(-cond)))).astype(BF)
    small[...] = jnp.zeros_like(small)
    for c in range(2):
        for i in range(9):
            small[54 + c * 9 + i : 55 + c * 9 + i, :] = signal[c : c + 1, i * 128 : (i + 1) * 128].astype(F32)
    for j in range(3):
        load_wm(j).wait()
        part = mm(signal, w2[j // 2, j % 2 * D : (j % 2 + 1) * D]) + bias_ref[:, j * D : (j + 1) * D]
        for c in range(2):
            mod[c, j : j + 1, :] = part[c : c + 1, :]

    @pl.when(is_feed)
    def _():
        for j in range(2):
            load_w2(j).start()

    @pl.when(section >= 2)
    def _():
        send_in(1).wait_send()

    for target in (3, 1):
        for c in range(2):

            @pl.when(section != target)
            def _():
                og_copy(c, section, target).start()

    for j in range(2):
        load_w1(j).wait()

    def shift_of(c):
        return mod[c, 0:1, :]

    def scale_of(c):
        return mod[c, 1:2, :]

    def gate_of(c):
        return mod[c, 2:3, :]

    def put_sums(c, which, value):
        for i in range(9):
            small[pl.ds(c * 27 + which * 9 + i, 1), :] = value[:, i * 128 : (i + 1) * 128]

    def join(parts_ref, c, r, own, target):
        tiles = {}
        for q in range(4):
            value = own if q == target else parts_ref[c, q, part(r)]
            for t in range(3):
                tile = value[:, t * 128 : (t + 1) * 128]
                at = 2 * q + t
                tiles[at] = tile if at not in tiles else tiles[at] + tile
        return jnp.concatenate([tiles[t] for t in range(9)], axis=1)

    def part(r):
        return pl.ds(0, r)

    def send_forward(c, r, source):
        return copies.remote("forward", c, source.at[c, part(r)], rows.at[c, part(r)], (dp, (section + 1) % 4))

    def send_backward(c, r):
        return copies.remote("backward", c, back.at[c, part(r)], up.at[c, part(r)], (dp, (section + 3) % 4))

    def send_done(c):
        return copies.remote("done", c, picked.at[c], landed.at[c], (dp, 1))

    def send_hidden(c, r):
        return copies.remote("hidden", c, hidden.at[c, part(r)], hidden2.at[c, part(r)], partner)

    def keep_hidden(c, r):
        return copies.local("own_hidden", c, hidden.at[c, part(r)], hidden_own.at[c, part(r)])

    def send_mixed(c, r, source, at):
        return copies.remote("mixed", c, source.at[at, part(r)], mixed_other.at[c, part(r)], partner)

    def keep_mixed(c, r, source, at):
        return copies.local("own_mixed", c, source.at[at, part(r)], mixed_own.at[c, part(r)])

    def keep_x(c, r, at):
        return copies.local("own_x", c, big.at[at, part(r)], x_own.at[c, part(r)])

    def keep_y(c, r):
        return copies.local("own_y", c, big.at[4 + c * 2 + high, part(r)], y_own.at[c, part(r)])

    def send_pair(c, k, half, r):
        columns = pl.ds(k * D + (0, EARLY)[half], (EARLY, D - EARLY)[half])
        source = big.at[4 + c * 2 + 1 - high, part(r), columns]
        return copies.remote("pair", (c * 2 + k) * 2 + half, source, y_own.at[c, part(r), columns], partner)

    def mixed_keep(c, r):
        return copies.local("own_mixed", c, big.at[c * 2 + 1, part(r), pl.ds(D, D)], mixed_own.at[c, part(r)])

    def mixed_send(c, r):
        source = big.at[c * 2 + 1, part(r), pl.ds(D, D)]
        return copies.remote("mixed", c, source, mixed_other.at[c, part(r)], partner)

    def keep_grad(c):
        return copies.local("own_grad", c, back.at[c], grad_own.at[c])

    def attend(c, r, live):
        x = rows[c, part(r)].astype(F32)
        hid = norm_forward(x, shift_of(c), scale_of(c))
        hidden[c, part(r)] = hid
        send_hidden(c, r).start()
        keep_hidden(c, r).start()
        big[c * 2, part(r)] = mm(hid, w1[0]).astype(BF)
        big[c * 2 + 1, part(r), 0:D] = mm(hid, w1[1, :, 0:D]).astype(BF)
        bias = None if live is None else key_bias(live, r)
        parts[0, part(r)] = jnp.zeros((r, D), F32)

        def group(g, carry):
            cut = pl.ds(pl.multiple_of(g * 256, 128), WINDOW)
            cut_k = pl.ds(pl.multiple_of(D + g * 256, 128), WINDOW)
            q4 = big[c * 2, part(r), cut]
            k4 = big[c * 2, part(r), cut_k]
            v4 = big[c * 2 + 1, part(r), cut]
            results = []
            for start, offset in HEADS_OF_GROUP:
                side = slice(start, start + 256)
                q = only_head(q4[:, side], offset + 32 * g)
                v = only_head(v4[:, side], offset + 32 * g)
                results.append(mm(softmax_of(q, k4[:, side], bias).astype(BF), v))
            parts[0, part(r), cut] += overlaid(results)
            return carry

        lax.fori_loop(0, 4, group, 0)
        mixed = parts[0, part(r)].astype(BF)
        big[c * 2 + 1, part(r), D:HALF] = mixed
        mixed_keep(c, r).start()
        out = mm(mixed, w1[1, :, D:HALF])
        branch[c, part(r)] = out.astype(BF)
        outs[c, part(r)] = (rows[c, part(r)].astype(F32) + gate_of(c) * out).astype(BF)
        send_forward(c, r, outs).start()

    def attend_back(c, r, live, to_section):
        upstream = up[c, part(r)].astype(F32)
        put_sums(c, 2, jnp.sum(upstream * branch[c, part(r)].astype(F32), axis=0, keepdims=True))
        bg = (upstream * gate_of(c)).astype(BF)
        big[4 + c * 2 + 1, part(r), D:HALF] = bg
        up_mixed[part(r)] = mm(bg, w1[1, :, D:HALF], NT).astype(BF)
        bias = None if live is None else key_bias(live, r)
        parts[:, part(r)] = jnp.zeros((3, r, D), F32)

        def put_parts(low, width):
            cut = pl.ds(low, width)
            big[4 + c * 2, part(r), cut] = (parts[0, part(r), cut] * FACTOR).astype(BF)
            big[4 + c * 2, part(r), pl.ds(D + low, width)] = (parts[1, part(r), cut] * FACTOR).astype(BF)
            big[4 + c * 2 + 1, part(r), cut] = parts[2, part(r), cut].astype(BF)

        def group(g, carry):
            if not to_section:

                @pl.when(g == 2)
                def _():
                    put_parts(0, EARLY)
                    for k in range(2):
                        send_pair(c, k, 0, r).start()

            cut = pl.ds(pl.multiple_of(g * 256, 128), WINDOW)
            cut_k = pl.ds(pl.multiple_of(D + g * 256, 128), WINDOW)
            q4 = big[c * 2, part(r), cut]
            k4 = big[c * 2, part(r), cut_k]
            v4 = big[c * 2 + 1, part(r), cut]
            mg4 = up_mixed[part(r), cut]
            dq, dk, dv = [], [], []
            for start, offset in HEADS_OF_GROUP:
                side = slice(start, start + 256)
                q = only_head(q4[:, side], offset + 32 * g)
                k = only_head(k4[:, side], offset + 32 * g)
                mg = only_head(mg4[:, side], offset + 32 * g)
                soft = softmax_of(q, k, bias)
                soft_grad = mm(mg, v4[:, side], NT)
                dv.append(mm(soft.astype(BF), mg, TN))
                product = soft * soft_grad
                score_grad = (product - soft * jnp.sum(product, axis=-1, keepdims=True)).astype(BF)
                dq.append(mm(score_grad, k))
                dk.append(mm(score_grad, q, TN))
            parts[0, part(r), cut] += overlaid(dq)
            parts[1, part(r), cut] += overlaid(dk)
            parts[2, part(r), cut] += overlaid(dv)
            return carry

        lax.fori_loop(0, 4, group, 0)
        if to_section:
            put_parts(0, EARLY)
        put_parts(EARLY, D - EARLY)
        if not to_section:
            for k in range(2):
                send_pair(c, k, 1, r).start()
        keep_x(c, r, 4 + c * 2 + high).start()
        hidden_grad = mm(big[4 + c * 2, part(r)], w1[0], NT)
        hidden_grad += mm(big[4 + c * 2 + 1, part(r), 0:D], w1[1, :, 0:D], NT)
        grad, shift_grad, scale_grad = norm_backward(
            rows[c, part(r)].astype(F32), scale_of(c), up[c, part(r)].astype(F32), hidden_grad
        )
        back[c, part(r)] = grad
        if to_section:
            send_backward(c, r).start()
        else:
            keep_grad(c).start()
        put_sums(c, 0, shift_grad)
        put_sums(c, 1, scale_grad)

    def exchange_mixed(r):
        for c in range(2):

            @pl.when(high == 0)
            def _():
                mixed_send(c, r).start()

    def finish_attention(r, to_section):
        for c in range(2):
            send_hidden(c, r).wait()
            keep_hidden2(c, r).start()
            keep_hidden(c, r).wait()

            @pl.when(high == 0)
            def _():
                mixed_send(c, r).wait_send()

            @pl.when(high == 1)
            def _():
                mixed_send(c, r).wait_recv()

            mixed_keep(c, r).wait()
            send_forward(c, r, outs).wait_send()
            keep_x(c, r, 4 + c * 2 + high).wait()
            for k in range(2):
                for half in range(2):
                    send_pair(c, k, half, r).wait()
            keep_hidden2(c, r).wait()
            if not to_section:
                keep_grad(c).wait()

    def keep_hidden2(c, r):
        return copies.local("other_hidden", c, hidden2.at[c, part(r)], hidden_other.at[c, part(r)])

    def keep_other(c, r):
        return (
            keep_hidden2(c, r),
            copies.local("other_active", c, extra.at[0, c, part(r)], active_other.at[c, part(r)]),
            copies.local("other_slope", c, extra.at[1, c, part(r)], slope_other.at[c, part(r)]),
        )

    def work_for_partner(c, r):
        active, slope = gelu_pair(mm(hidden2[c, part(r)], w1[high]))
        extra[0, c, part(r)] = active.astype(BF)
        extra[1, c, part(r)] = slope.astype(BF)
        for copy in keep_other(c, r):
            copy.start()

    def send_result(c, q):
        return copies.remote(
            "result", c, outs.at[c, :, pl.ds(256 * q, WINDOW)], window_out.at[c], (dp, q), c * 4 + q
        )

    def keep_result(c):
        return copies.local("result", c * 4 + 1, outs.at[c, :, pl.ds(256, WINDOW)], window_out.at[c])

    @pl.when(section == 0)
    def _():
        def live_of(c):
            lines, width = grid_of(shape_ref[c])
            return lines * width

        def forward(c, carry):
            for s in (1, 2, 3):
                take_in(c, s).wait_recv()
            rows[c] = join(quarters, c, VALID, packs[0, c], 0)
            attend(c, VALID, live_of(c))
            return carry

        def backward(c, carry):
            send_backward(c, VALID).wait_recv()
            attend_back(c, VALID, live_of(c), False)
            return carry

        lax.fori_loop(0, 2, forward, 0)
        pl.semaphore_wait(go, 1)
        exchange_mixed(VALID)
        lax.fori_loop(0, 2, backward, 0)
        finish_attention(VALID, False)

    @pl.when(section == 1)
    def _():
        for j in range(2):
            load_w2(j).wait()

        def forward(c, carry):
            send_forward(c, VALID, outs).wait_recv()
            hid = norm_forward(rows[c].astype(F32), shift_of(c), scale_of(c))
            hidden[c] = hid
            keep_hidden(c, VALID).start()
            for j in range(2):
                active, slope = gelu_pair(mm(hid, w1[j]))
                low = active.astype(BF)
                big[c * 2 + j] = low
                big[4 + c * 2 + j] = slope.astype(BF)
                if j == 0:
                    acc[...] = mm(low, w2[j])
                else:
                    acc[...] += mm(low, w2[j])
            keep_x(c, VALID, c * 2 + high).start()
            out = acc[...]
            branch[c] = out.astype(BF)
            low = (rows[c].astype(F32) + gate_of(c) * out).astype(BF)
            outs[c] = low
            picked[c] = pick_kept(low, kept_ref[pl.ds(c, 1), :])
            send_forward(c, KEPT, picked).start()
            return carry

        lax.fori_loop(0, 2, forward, 0)
        for c in range(2):
            send_forward(c, KEPT, picked).wait_send()
        for c in range(2):
            send_hidden(c, VALID).start()
        for c in range(2):
            for s in (0, 2, 3):
                og_copy(c, s, 1).wait_recv()
            base[c] = join(grads, c, VALID, packs[1, c], 1)
        for c in range(2):
            send_hidden(c, VALID).wait()
        pl.semaphore_signal(go, inc=1, device_id=(dp, 0), device_id_type=MESH)
        for c in range(2):
            work_for_partner(c, VALID)
        for c in range(2):
            send_done(c).wait_recv()
            outs[c] = merge_kept(outs[c], landed[c], kept_ref[c : c + 1, :])
            for q in (0, 2, 3):
                send_result(c, q).start()
            keep_result(c).start()

        def backward(c, carry):
            send_backward(c, KEPT).wait_recv()
            low = merge_kept(base[c], up[c, part(KEPT)], kept_ref[pl.ds(c, 1), :])
            base[c] = low
            upstream = low.astype(F32)
            bg = (upstream * gate_of(c)).astype(BF)
            bgs[c] = bg
            send_mixed(c, VALID, bgs, c).start()
            keep_mixed(c, VALID, bgs, c).start()
            put_sums(c, 2, jnp.sum(upstream * branch[c].astype(F32), axis=0, keepdims=True))
            for j in range(2):
                slope = big[4 + c * 2 + j].astype(F32)
                inner_grad = (mm(bg, w2[j], NT) * slope).astype(BF)
                big[4 + c * 2 + j] = inner_grad
                if j == 0:
                    acc[...] = mm(inner_grad, w1[j], NT)
                else:
                    acc[...] += mm(inner_grad, w1[j], NT)
            keep_y(c, VALID).start()
            grad, shift_grad, scale_grad = norm_backward(
                rows[c].astype(F32), scale_of(c), base[c].astype(F32), acc[...]
            )
            back[c] = grad
            send_backward(c, VALID).start()
            put_sums(c, 0, shift_grad)
            put_sums(c, 1, scale_grad)
            return carry

        lax.fori_loop(0, 2, backward, 0)
        for c in range(2):
            for copy in keep_other(c, VALID):
                copy.wait()
            keep_hidden(c, VALID).wait()
            send_mixed(c, VALID, bgs, c).wait()
            keep_mixed(c, VALID, bgs, c).wait()
            send_backward(c, VALID).wait_send()
            for q in (0, 2, 3):
                send_result(c, q).wait_send()
            keep_result(c).wait()
            keep_x(c, VALID, c * 2 + high).wait()
            keep_y(c, VALID).wait()

    @pl.when(section == 2)
    def _():
        def forward(c, carry):
            send_forward(c, KEPT, outs).wait_recv()
            attend(c, KEPT, None)
            return carry

        def backward(c, carry):
            send_backward(c, KEPT).wait_recv()
            attend_back(c, KEPT, None, True)
            return carry

        lax.fori_loop(0, 2, forward, 0)
        exchange_mixed(KEPT)
        lax.fori_loop(0, 2, backward, 0)
        for c in range(2):
            send_backward(c, KEPT).wait_send()
        for c in range(2):
            for k in range(2):
                for half in range(2):
                    send_pair(c, k, half, KEPT).start()
        finish_attention(KEPT, True)


    @pl.when(section == 3)
    def _():
        for j in range(2):
            load_w2(j).wait()
        for c in range(2):
            for s in (0, 1, 2):
                og_copy(c, s, 3).wait_recv()
            low = join(grads, c, KEPT, packs_kept[c], 3)
            base[c, part(KEPT)] = low
            bg = (low.astype(F32) * gate_of(c)).astype(BF)
            bgs[c, part(KEPT)] = bg
            send_mixed(c, KEPT, bgs, c).start()
            keep_mixed(c, KEPT, bgs, c).start()

        def run(c, carry):
            send_forward(c, KEPT, outs).wait_recv()
            hid = norm_forward(rows[c, part(KEPT)].astype(F32), shift_of(c), scale_of(c))
            hidden[c, part(KEPT)] = hid
            send_hidden(c, KEPT).start()
            keep_hidden(c, KEPT).start()
            bg = bgs[c, part(KEPT)]
            for j in range(2):
                active, slope = gelu_pair(mm(hid, w1[j]))
                low = active.astype(BF)
                inner_grad = (mm(bg, w2[j], NT) * slope).astype(BF)
                big[c * 2 + j, part(KEPT)] = low
                big[4 + c * 2 + j, part(KEPT)] = inner_grad
                ahead, behind = mm(low, w2[j]), mm(inner_grad, w1[j], NT)
                if j == 0:
                    parts[0, part(KEPT)] = ahead
                    parts[1, part(KEPT)] = behind
                else:
                    parts[0, part(KEPT)] += ahead
                    parts[1, part(KEPT)] += behind
            x = rows[c, part(KEPT)].astype(F32)
            upstream = base[c, part(KEPT)].astype(F32)
            grad, shift_grad, scale_grad = norm_backward(x, scale_of(c), upstream, parts[1, part(KEPT)])
            back[c, part(KEPT)] = grad
            send_backward(c, KEPT).start()
            out = parts[0, part(KEPT)]
            picked[c] = (x + gate_of(c) * out).astype(BF)
            send_done(c).start()
            put_sums(c, 0, shift_grad)
            put_sums(c, 1, scale_grad)
            put_sums(c, 2, jnp.sum(upstream * out, axis=0, keepdims=True))
            keep_x(c, KEPT, c * 2 + high).start()
            keep_y(c, KEPT).start()
            return carry

        lax.fori_loop(0, 2, run, 0)
        for c in range(2):
            send_hidden(c, KEPT).wait()
            work_for_partner(c, KEPT)
        for c in range(2):
            for copy in keep_other(c, KEPT):
                copy.wait()
            keep_hidden(c, KEPT).wait()
            send_mixed(c, KEPT, bgs, c).wait()
            keep_mixed(c, KEPT, bgs, c).wait()
            send_backward(c, KEPT).wait_send()
            keep_x(c, KEPT, c * 2 + high).wait()
            keep_y(c, KEPT).wait()
            send_done(c).wait_send()

    @pl.when(section != 1)
    def _():
        for c in range(2):
            send_result(c, 0).wait_recv()

    for c in range(2):

        @pl.when(section == 1)
        def _():
            send_in(c).wait_send()

        for target in (3, 1):

            @pl.when(section != target)
            def _():
                og_copy(c, section, target).wait_send()

    packed_out[...] = small[...].astype(BF)


def pipeline(grid_shape, canvas_in, out_grad, kept_rank, conditioning, bias, w1, w2, wm):
    anywhere = pl.BlockSpec(memory_space=pl.ANY)
    vmem = pl.BlockSpec(memory_space=VMEM)
    canvas = array(2, VALID, D)
    count = sum(n for _, n in PIPE_COPIES)
    return pl.pallas_call(
        pipeline_kernel,
        in_specs=[pl.BlockSpec(memory_space=pltpu.SMEM)] + [vmem] * 5 + [anywhere] * 3,
        out_specs=[anywhere] * 10 + [vmem],
        out_shape=[canvas] * 4
        + [array(2, VALID, HALF)] * 2
        + [canvas]
        + [array(2, VALID, HALF)] * 2
        + [array(2, VALID, WINDOW), array(PACKED, 128)],
        scratch_shapes=[
            VMEM((2, D, HALF), BF),
            VMEM((2, HALF, D), BF),
            VMEM((2, VALID, D), BF),
            VMEM((2, 2, VALID, WINDOW), BF),
            VMEM((2, KEPT, WINDOW), BF),
            VMEM((2, 4, VALID, WINDOW), BF),
            VMEM((2, 4, VALID, WINDOW), BF),
            VMEM((2, VALID, D), BF),
            VMEM((2, VALID, D), BF),
            VMEM((2, VALID, D), BF),
            VMEM((8, VALID, HALF), BF),
            VMEM((2, VALID, D), BF),
            VMEM((2, VALID, D), BF),
            VMEM((2, KEPT, D), BF),
            VMEM((2, KEPT, D), BF),
            VMEM((2, VALID, D), BF),
            VMEM((2, VALID, D), BF),
            VMEM((3, VALID, D), F32),
            VMEM((VALID, D), F32),
            VMEM((VALID, D), BF),
            VMEM((2, VALID, D), BF),
            VMEM((2, 2, VALID, HALF), BF),
            VMEM((2, 3, D), F32),
            VMEM((PACKED, 128), F32),
            pltpu.SemaphoreType.DMA((count,)),
            pltpu.SemaphoreType.DMA((count,)),
            pltpu.SemaphoreType.REGULAR,
        ],
        compiler_params=pltpu.CompilerParams(collective_id=1, has_side_effects=True, vmem_limit_bytes=63 * 2**20),
        cost_estimate=cost(40e9, 60e6),
        name="pipeline",
    )(grid_shape, canvas_in, out_grad, kept_rank, conditioning, bias, w1, w2, wm)


FLOWS = ((0, "y", 0, 640), (0, "z", 640, 512), (1, "y", 0, 512), (1, "z", 512, 640))
CUT = 80
FINAL_COPIES = (
    ("flow", 48), ("left", 8), ("right", 8), ("weights", 1),
    ("gather_y", 6), ("gather_z", 6), ("gather_x", 1), ("window", 8),
)


def final_kernel(
    shape_ref, packed_ref, result_ref, hidden_own, hidden_other, mixed_own, mixed_other, x_own, y_own, grad_own, active_other, slope_other, w2_hbm,
    first_out, second_out, result_out, canvas_out, all_packed,
    left, right, other, w2, sums_first, sums_second, windows_in, *scratch,
):
    count = len(FLOWS)
    ones, twos, threes, sums, tiny1, tiny2, tiny3 = (scratch[i * count : (i + 1) * count] for i in range(7))
    copies = Copies(scratch[7 * count], scratch[7 * count + 1])
    for key, number in FINAL_COPIES:
        copies.name(key, number)
    dp, section = lax.axis_index("dp"), lax.axis_index("section")
    x, z, y = dp // 16, (dp // 4) % 4, dp % 4
    place = {"y": y, "z": z}
    is_odd = section % 2 == 1

    def neighbour(axis, by):
        if axis == "y":
            return (x * 16 + z * 4 + (y + by) % 4, section)
        return (x * 16 + ((z + by) % 4) * 4 + y, section)

    partner = ((dp + 16) % 32, section)
    barrier = pltpu.get_barrier_semaphore()
    for axis in ("y", "z"):
        for by in (1, 2, 3):
            pl.semaphore_signal(barrier, inc=1, device_id=neighbour(axis, by), device_id_type=MESH)
    pl.semaphore_signal(barrier, inc=1, device_id=partner, device_id_type=MESH)

    @pl.when(section != 0)
    def _():
        pl.semaphore_signal(barrier, inc=1, device_id=(dp, 0), device_id_type=MESH)

    def load_left(r, feed):
        result = []
        for c in range(2):
            part, own, theirs = pl.ds(0, r), pl.ds(c * r, r), pl.ds((2 + c) * r, r)
            result.append(copies.local("left", c, x_own.at[c, part], left.at[own]))
            if feed:
                result.append(copies.local("left", 2 + c, active_other.at[c, part], left.at[theirs]))
            else:
                result.append(copies.local("left", 2 + c, y_own.at[c, part], left.at[theirs]))
            result.append(copies.local("right", 4 + c, mixed_own.at[c, part], right.at[1, own]))
            result.append(copies.local("right", 6 + c, mixed_other.at[c, part], right.at[1, theirs]))
        return result

    def load_right(r, feed):
        result = []
        for c in range(2):
            part, own, theirs = pl.ds(0, r), pl.ds(c * r, r), pl.ds((2 + c) * r, r)
            if feed:
                result.append(copies.local("left", 4 + c, y_own.at[c, part], other.at[own]))
                result.append(copies.local("left", 6 + c, slope_other.at[c, part], other.at[theirs]))
            result.append(copies.local("right", c, hidden_own.at[c, part], right.at[0, own]))
            result.append(copies.local("right", 2 + c, hidden_other.at[c, part], right.at[0, theirs]))
        if feed:
            result.append(copies.local("weights", 0, w2_hbm.at[pl.ds(x * HALF, HALF), :], w2))
        return result

    for which, (r, feed) in enumerate(((VALID, False), (VALID, True), (KEPT, False), (KEPT, True))):

        @pl.when(section == which)
        def _():
            for c in load_left(r, feed) + load_right(r, feed):
                c.start()

    all_packed[x, z, y] = packed_ref[...]

    def put(target, k, value):
        target[pl.ds(8 * k, 8)] = value.astype(BF).reshape(8, BLOCK, D)

    def columns(k):
        return pl.ds(pl.multiple_of(k * D, 128), D)

    data = (sums_first, sums_second)
    outs = (first_out, second_out)
    halves = (pl.ds(0, 2), pl.ds(2, 2))
    cuts = (pl.ds(0, CUT), pl.ds(CUT, BLOCK - CUT))

    def axes(flow):
        axis = FLOWS[flow][1]
        return axis, "z" if axis == "y" else "y"

    def step(flow, phase, kind, side, source, target):
        number = ((flow * 2 + phase) * 3 + kind) * 2 + side
        return copies.remote("flow", number, source, target, neighbour(axes(flow)[phase], (1, 3)[side]))

    def block(flow, by, half):
        which, axis, low, width = FLOWS[flow]
        position = (place[axis] + by) % 4
        columns = pl.ds(low, width)
        if axis == "y":
            return [data[which].at[4 * (2 * half + i) + position, :, columns] for i in range(2)]
        return [data[which].at[4 * position + 2 * half + i, :, columns] for i in range(2)]

    def pair_ref(flow, by, half):
        which, axis, low, width = FLOWS[flow]
        position = (place[axis] + by) % 4
        columns = pl.ds(low, width)
        grid = data[which].reshape(4, 4, BLOCK, D)
        if axis == "y":
            return grid.at[pl.ds(2 * half, 2), position, :, columns]
        return grid.at[position, pl.ds(2 * half, 2), :, columns]

    def first_a(flow, side):
        return step(flow, 0, 0, side, pair_ref(flow, 2, side), ones[flow].at[side])

    def first_b(flow, side):
        return step(flow, 0, 1, side, pair_ref(flow, (1, 3)[side], 1 - side), twos[flow].at[side])

    def first_c(flow, side):
        return step(flow, 0, 2, side, ones[flow].at[side], threes[flow].at[side])

    def slab(flow, by, cut):
        return sums[flow].at[(place[axes(flow)[1]] + by) % 4, cut]

    def second_a(flow, side):
        return step(flow, 1, 0, side, slab(flow, 2, cuts[side]), tiny1[flow].at[cuts[side]])

    def second_b(flow, side):
        cut = cuts[1 - side]
        return step(flow, 1, 1, side, slab(flow, (1, 3)[side], cut), tiny2[flow].at[cut])

    def second_c(flow, side):
        return step(flow, 1, 2, side, tiny1[flow].at[cuts[side]], tiny3[flow].at[cuts[side]])

    def begin(flow):
        for side in (0, 1):
            first_a(flow, side).start()
        for side in (0, 1):
            first_b(flow, side).start()

    def forward(flow):
        for side in (0, 1):
            first_a(flow, side).wait()
            own = block(flow, (1, 3)[side], side)
            for i in range(2):
                total = ones[flow][side, i].astype(F32) + own[i][...].astype(F32)
                ones[flow][side, i] = total.astype(BF)
            first_c(flow, side).start()

    def middle(flow):
        for side in (0, 1):
            first_b(flow, side).wait()
            first_c(flow, side).wait()
        for half in (0, 1):
            own = block(flow, 0, half)
            for i in range(2):
                total = own[i][...].astype(F32) + threes[flow][half, i].astype(F32)
                sums[flow][2 * half + i] = (total + twos[flow][1 - half, i].astype(F32)).astype(BF)
        for side in (0, 1):
            second_a(flow, side).start()
        for side in (0, 1):
            second_b(flow, side).start()

    def late(flow):
        for side in (0, 1):
            second_a(flow, side).wait()
            own = slab(flow, (1, 3)[side], cuts[side])[...]
            tiny1[flow][cuts[side]] = (tiny1[flow][cuts[side]].astype(F32) + own.astype(F32)).astype(BF)
            second_c(flow, side).start()

    def finish(flow):
        which, axis, low, width = FLOWS[flow]
        for side in (0, 1):
            second_b(flow, side).wait()
            second_c(flow, side).wait()
        own = sums[flow][place[axes(flow)[1]]].astype(F32)
        outs[which][:, low : low + width] = own + tiny2[flow][...].astype(F32) + tiny3[flow][...].astype(F32)

    even = [i for i, f in enumerate(FLOWS) if f[0] == 0]
    odd = [i for i, f in enumerate(FLOWS) if f[0] == 1]

    def stage(work, flows):
        for flow in flows:
            work(flow)

    def gather(axis, by):
        if axis == "y":
            ref = all_packed.at[x, z, y]
            return copies.remote("gather_y", by - 1, ref, ref, neighbour("y", by), 2 + by)
        if axis == "z":
            ref = all_packed.at[x, z]
            return copies.remote("gather_z", by - 1, ref, ref, neighbour("z", by), 2 + by)
        return copies.remote("gather_x", 0, all_packed.at[x], all_packed.at[x], partner)

    def gathered(axis, by):
        if axis == "y":
            ref = all_packed.at[x, z, (y + 4 - by) % 4]
            return copies.remote("gather_y", by - 1, ref, ref, neighbour("y", by), 2 + by)
        if axis == "z":
            ref = all_packed.at[x, (z + 4 - by) % 4]
            return copies.remote("gather_z", by - 1, ref, ref, neighbour("z", by), 2 + by)
        ref = all_packed.at[1 - x]
        return copies.remote("gather_x", 0, ref, ref, partner)

    def window(c, q):
        source = grad_own.at[c, :, pl.ds(256 * q, WINDOW)]
        return copies.remote("window", c * 4, source, windows_in.at[c], (dp, q), c * 4 + q)

    def own_window(c):
        return copies.local("window", c * 4, grad_own.at[c, :, pl.ds(0, WINDOW)], windows_in.at[c])

    shift = shift_matrix(section)

    def unpack(value, c):
        return mm(mm(value, shift, NT).astype(BF), slots_of_tokens(shape_ref[c]), TN).astype(BF)

    @pl.when(section == 0)
    def _():
        pl.semaphore_wait(barrier, 10)

    @pl.when(section != 0)
    def _():
        pl.semaphore_wait(barrier, 7)

    @pl.when(section == 0)
    def _():
        for c in range(2):
            own_window(c).start()
            for q in (1, 2, 3):
                window(c, q).start()

    for by in (1, 2, 3):
        gather("y", by).start()

    def attention_products(r):
        rows = pl.ds(0, 4 * r)
        for copy in load_left(r, False) + load_right(r, False):
            copy.wait()

        def product(k, carry):
            put(sums_first, k, mm(left[rows, columns(k)], right[x * k, rows], TN))
            return carry

        lax.fori_loop(0, 2, product, 0)
        stage(begin, even)
        second_out[...] = jnp.zeros_like(second_out)

    def feed_products(r):
        rows = pl.ds(0, 4 * r)
        for copy in load_left(r, True):
            copy.wait()

        def second_product(k, carry):
            put(sums_second, k, mm(left[rows, columns(k)], right[1, rows], TN))
            return carry

        def first_product(k, carry):
            put(sums_first, k, mm(other[rows, columns(k)], right[0, rows], TN))

            @pl.when(k == 0)
            def _():
                stage(forward, odd)

            return carry

        lax.fori_loop(0, 2, second_product, 0)
        stage(begin, odd)
        for copy in load_right(r, True):
            copy.wait()

        def inner_gradient(c, carry):
            theirs = pl.ds(pl.multiple_of((2 + c) * r, 128), r)
            active_grad = mm(right[1, theirs], w2[...], NT)
            other[theirs] = (active_grad * other[theirs].astype(F32)).astype(BF)
            return carry

        lax.fori_loop(0, 2, inner_gradient, 0)
        lax.fori_loop(0, 2, first_product, 0)
        stage(begin, even)

    for which, r in ((0, VALID), (2, KEPT)):

        @pl.when(section == which)
        def _():
            attention_products(r)

    for which, r in ((1, VALID), (3, KEPT)):

        @pl.when(section == which)
        def _():
            feed_products(r)

    for by in (1, 2, 3):
        gather("y", by).wait_send()
        gathered("y", by).wait_recv()
    for by in (1, 2, 3):
        gather("z", by).start()

    @pl.when(is_odd)
    def _():
        stage(middle, odd)

    stage(forward, even)
    for by in (1, 2, 3):
        gather("z", by).wait_send()
        gathered("z", by).wait_recv()
    gather("x", 0).start()
    for c in range(2):
        result_out[c] = unpack(result_ref[c], c)
    for work, later in ((middle, late), (late, finish)):

        @pl.when(is_odd)
        def _():
            stage(later, odd)

        stage(work, even)
    stage(finish, even)

    gather("x", 0).wait_send()
    gathered("x", 0).wait_recv()

    for c in range(2):

        @pl.when(section == 0)
        def _():
            own_window(c).wait()
            for q in (1, 2, 3):
                window(c, q).wait_send()

        @pl.when(section != 0)
        def _():
            window(c, 0).wait_recv()

        canvas_out[c] = unpack(windows_in[c], c)


def final(grid_shape, packed, result_window, parts, w2):
    anywhere = pl.BlockSpec(memory_space=pl.ANY)
    vmem = pl.BlockSpec(memory_space=VMEM)
    widths = [f[3] for f in FLOWS]
    pair = [VMEM((2, 2, BLOCK, w), BF) for w in widths]
    tiny = [VMEM((BLOCK, w), BF) for w in widths]
    count = sum(n for _, n in FINAL_COPIES)
    canvas = array(2, QUARTER, SLOTS)
    return pl.pallas_call(
        final_kernel,
        in_specs=[pl.BlockSpec(memory_space=pltpu.SMEM)] + [vmem] * 2 + [anywhere] * 10,
        out_specs=[vmem] * 5,
        out_shape=[array(BLOCK, D, dtype=F32)] * 2 + [canvas] * 2 + [array(2, 4, 4, PACKED, 128)],
        scratch_shapes=[
            VMEM((4 * VALID, HALF), BF),
            VMEM((2, 4 * VALID, D), BF),
            VMEM((4 * VALID, HALF), BF),
            VMEM((HALF, D), BF),
            VMEM((16, BLOCK, D), BF),
            VMEM((16, BLOCK, D), BF),
            VMEM((2, VALID, WINDOW), BF),
        ]
        + pair * 3
        + [VMEM((4, BLOCK, w), BF) for w in widths]
        + tiny * 3
        + [pltpu.SemaphoreType.DMA((count,)), pltpu.SemaphoreType.DMA((count,))],
        compiler_params=pltpu.CompilerParams(collective_id=0, has_side_effects=True, vmem_limit_bytes=63 * 2**20),
        cost_estimate=cost(20e9, 60e6),
        name="final",
    )(grid_shape, packed, result_window, *parts, w2)


STRIPE = 128


def closing_kernel(
    packed_ref, first_ref, second_ref, result_ref, canvas_ref,
    first_out, second_out, result_out, canvas_out, product_out, bias_out,
    wide, sums, signals, stage, sems,
):
    wide[...] = packed_ref[...].astype(F32)

    def column(row):
        return wide[pl.ds(row, 32, stride=PACKED), :].astype(BF)

    for c in range(2):
        lines = pl.ds(32 * c, 32)
        for t in range(9):
            signals[lines, t * 128 : (t + 1) * 128] = column(54 + c * 9 + t)
        for t in range(27):
            sums[lines, t * 128 : (t + 1) * 128] = column(c * 27 + t)
    bias_out[...] = jnp.sum(sums[...].astype(F32), axis=0, keepdims=True)

    def write(j):
        lines = pl.ds(j * STRIPE, STRIPE)
        return pltpu.make_async_copy(stage.at[j % 3], product_out.at[lines, :], sems.at[j])

    for j in range(D // STRIPE):
        if j >= 3:
            write(j - 3).wait()
        stage[j % 3] = mm(signals[:, j * STRIPE : (j + 1) * STRIPE], sums[...], TN)
        write(j).start()
    first_out[...] = first_ref[...]
    second_out[...] = second_ref[...]
    result_out[...] = result_ref[...]
    canvas_out[...] = canvas_ref[...]
    for j in range(D // STRIPE - 3, D // STRIPE):
        write(j).wait()


def closing(packed, first, second, result, canvas):
    anywhere = pl.BlockSpec(memory_space=pl.ANY)
    vmem = pl.BlockSpec(memory_space=VMEM)
    return pl.pallas_call(
        closing_kernel,
        in_specs=[vmem] * 5,
        out_specs=[vmem] * 4 + [anywhere, vmem],
        out_shape=[
            array(*first.shape, dtype=F32),
            array(*second.shape, dtype=F32),
            array(*result.shape),
            array(*canvas.shape),
            array(D, 3 * D, dtype=F32),
            array(1, 3 * D, dtype=F32),
        ],
        scratch_shapes=[
            VMEM((32 * PACKED, 128), F32),
            VMEM((64, 3 * D), BF),
            VMEM((64, D), BF),
            VMEM((3, STRIPE, 3 * D), F32),
            pltpu.SemaphoreType.DMA((D // STRIPE,)),
        ],
        compiler_params=pltpu.CompilerParams(vmem_limit_bytes=63 * 2**20),
        cost_estimate=cost(2 * 64 * D * 3 * D, 4 * D * 3 * D),
        name="closing",
    )(packed, first, second, result, canvas)


def local(
    canvas_in,
    conditioning,
    grid_shape,
    kept_rank,
    first_weight,
    second_weight,
    modulation_weight,
    modulation_bias,
    out_grad,
):
    w1, w2 = first_weight[0], second_weight[0]
    outputs = pipeline(
        grid_shape,
        canvas_in.transpose(0, 2, 1),
        out_grad.transpose(0, 2, 1),
        kept_rank,
        conditioning,
        modulation_bias,
        w1,
        w2,
        modulation_weight[0],
    )
    first_sum, second_sum, result, canvas_grad, packed = final(grid_shape, outputs[10], outputs[9], outputs[:9], w2)
    first_sum, second_sum, result, canvas_grad, modulation_grad, bias_grad = closing(
        packed.reshape(32 * PACKED, 128), first_sum, second_sum, result, canvas_grad
    )
    return (
        result.transpose(0, 2, 1),
        canvas_grad.transpose(0, 2, 1),
        first_sum.T[None],
        second_sum[None],
        modulation_grad[None],
        bias_grad,
    )


def solution(mesh):
    placed = (
        P("dp", None, "section"),
        P("dp", None),
        P("dp"),
        P("dp", None),
        P("section", None, None),
        P("section", None, None),
        P("section", None, None),
        P("section", None),
        P("dp", None, "section"),
    )
    return jax.shard_map(
        local,
        mesh=mesh,
        in_specs=placed,
        out_specs=(
            P("dp", None, "section"),
            P("dp", None, "section"),
            P("section", None, "dp"),
            P("section", "dp", None),
            P("section", None, None),
            P("section", None),
        ),
        check_vma=False,
    )
```

```python
import functools
import math

import jax
import jax.numpy as jnp
from jax import lax
from jax.experimental import pallas as pl
from jax.experimental.pallas import tpu as pltpu
from jax.sharding import PartitionSpec as P

HEADS = 16
SIDE = 20
SLOTS = SIDE * SIDE
VALID = 256
KEPT = 128
D = 1152
FF = 4608
HALF = FF // 2
QUARTER = D // 4
WINDOW = 384
PACKED = 80
PIECES = ((0, 256), (256, 256), (512, 256), (768, 384))
HEAD = D // HEADS
BLOCK = FF // 32
EPSILON = 1e-06
FACTOR = 1.0 / math.sqrt(HEAD)
LOG2E = math.log2(math.e)
NEGATIVE = -1e30
BF = jnp.bfloat16
F32 = jnp.float32
VMEM = pltpu.VMEM
MESH = pl.DeviceIdType.MESH
NT = (((1,), (1,)), ((), ()))
TN = (((0,), (0,)), ((), ()))
C0 = math.sqrt(2.0 / math.pi)


def mm(a, b, dims=(((1,), (0,)), ((), ()))):
    return lax.dot_general(a, b, dims, preferred_element_type=F32)


def cost(flops, nbytes):
    return pl.CostEstimate(flops=int(flops), bytes_accessed=int(nbytes), transcendentals=0)


def array(*shape, dtype=BF):
    return jax.ShapeDtypeStruct(shape, dtype)


def norm_stats(x):
    mean = jnp.mean(x, axis=-1, keepdims=True)
    centred = x - mean
    rstd = lax.rsqrt(jnp.mean(centred * centred, axis=-1, keepdims=True) + EPSILON)
    return centred * rstd, rstd


def norm_forward(rows, shift, scale):
    normed, _ = norm_stats(rows)
    return (normed * (1.0 + scale) + shift).astype(BF)


def norm_backward(rows, scale, upstream, hidden_grad):
    normed, rstd = norm_stats(rows)
    shift_grad = jnp.sum(hidden_grad, axis=0, keepdims=True)
    scale_grad = jnp.sum(hidden_grad * normed, axis=0, keepdims=True)
    scaled = hidden_grad * (1.0 + scale)
    mean_scaled = jnp.mean(scaled, axis=-1, keepdims=True)
    mean_product = jnp.mean(scaled * normed, axis=-1, keepdims=True)
    grad = upstream + (scaled - mean_scaled - normed * mean_product) * rstd
    return grad.astype(BF), shift_grad, scale_grad


def gelu_pair(v):
    square = v * v
    t = jnp.tanh(v * (C0 + (C0 * 0.044715) * square))
    half = 0.5 * (1.0 + t)
    slope = half + (0.5 * v) * (1.0 - t * t) * (C0 + (3.0 * C0 * 0.044715) * square)
    return v * half, slope


def kept_spread(kept_row):
    line = lax.broadcasted_iota(jnp.int32, (VALID, KEPT), 0)
    return (line == kept_row).astype(F32)


def pick_kept(rows, kept_row):
    return mm(kept_spread(kept_row).astype(BF), rows, TN).astype(BF)


def merge_kept(base, kept_rows, kept_row):
    spread = kept_spread(kept_row)
    chosen = jnp.sum(spread, axis=1, keepdims=True) > 0.5
    return jnp.where(chosen, mm(spread.astype(BF), kept_rows).astype(BF), base)


def grid_of(shape_id):
    lines = jnp.where(shape_id == 1, 12, jnp.where(shape_id == 2, 20, 16))
    width = jnp.where(shape_id == 1, 20, jnp.where(shape_id == 2, 12, 16))
    return lines, width


def slots_of_tokens(shape_id):
    lines, width = grid_of(shape_id)
    slot = lax.broadcasted_iota(jnp.int32, (1, SLOTS), 1)
    line = (slot * 3277) >> 16
    column = slot - line * SIDE
    token = jnp.where((line < lines) & (column < width), line * width + column, -1)
    return (lax.broadcasted_iota(jnp.int32, (VALID, SLOTS), 0) == token).astype(BF)


def shift_matrix(section):
    line = lax.broadcasted_iota(jnp.int32, (QUARTER, WINDOW), 0)
    lane = lax.broadcasted_iota(jnp.int32, (QUARTER, WINDOW), 1)
    return (lane == line + 32 * section).astype(BF)


HEADS_OF_GROUP = ((0, 0), (0, 72), (128, 16), (128, 88))


def overlaid(parts):
    first, last = parts[0] + parts[1], parts[2] + parts[3]
    return jnp.concatenate([first[:, 0:128], first[:, 128:256] + last[:, 0:128], last[:, 128:256]], axis=1)


def only_head(value, offset):
    lane = lax.broadcasted_iota(jnp.int32, value.shape, 1)
    return jnp.where((lane >= offset) & (lane < offset + HEAD), value, jnp.zeros_like(value))


def key_bias(live, keys):
    lane = lax.broadcasted_iota(jnp.int32, (1, keys), 1)
    return jnp.where(lane < live, 0.0, NEGATIVE).astype(F32)


def softmax_of(q, k, bias):
    scores = mm(q, k, NT)
    if bias is not None:
        scores = scores + bias
    top = jnp.max(scores, axis=-1, keepdims=True)
    grown = jnp.exp2((scores - top) * (FACTOR * LOG2E))
    return grown * (1.0 / jnp.sum(grown, axis=-1, keepdims=True))


class Copies:
    def __init__(self, send, arrive):
        self.send, self.arrive, self.first, self.size = send, arrive, {}, 0

    def name(self, key, count):
        self.first[key] = self.size
        self.size += count

    def remote(self, key, index, source, target, device, sender=None):
        at = self.first[key]
        return pltpu.make_async_remote_copy(
            src_ref=source,
            dst_ref=target,
            send_sem=self.send.at[at + (index if sender is None else sender)],
            recv_sem=self.arrive.at[at + index],
            device_id=device,
            device_id_type=MESH,
        )

    def local(self, key, index, source, target):
        return pltpu.make_async_copy(source, target, self.send.at[self.first[key] + index])


PIPE_COPIES = (
    ("wm", 3), ("w1", 2), ("w2", 2), ("in", 8), ("og", 16), ("forward", 2), ("done", 2), ("backward", 2), ("result", 8),
    ("hidden", 2), ("mixed", 2), ("pair", 16), ("own_hidden", 2), ("own_mixed", 2), ("own_x", 2), ("own_y", 2), ("own_grad", 2),
    ("other_hidden", 2), ("other_active", 2), ("other_slope", 2),
)


def pipeline_kernel(
    shape_ref, canvas_ref, ograd_ref, kept_ref, cond_ref, bias_ref, w1_hbm, w2_hbm, wm_hbm,
    hidden_own, hidden_other, mixed_own, mixed_other, x_own, y_own, grad_own, active_other, slope_other, window_out, packed_out,
    w1, w2, rows, packs, packs_kept, quarters, grads, up, base, hidden, big, branch, outs, picked, landed, back, bgs, parts, acc, up_mixed, hidden2, extra, mod,
    small, send, arrive, go,
):
    dp, section = lax.axis_index("dp"), lax.axis_index("section")
    high = dp // 16
    partner = ((dp + 16) % 32, section)
    copies = Copies(send, arrive)
    for key, count in PIPE_COPIES:
        copies.name(key, count)
    is_feed = section % 2 == 1

    def load_wm(j):
        return copies.local("wm", j, wm_hbm.at[:, pl.ds(j * D, D)], w2.at[j // 2, pl.ds(j % 2 * D, D)])

    def load_w1(j):
        return copies.local("w1", j, w1_hbm.at[:, pl.ds(j * HALF, HALF)], w1.at[j])

    def load_w2(j):
        return copies.local("w2", j, w2_hbm.at[pl.ds(j * HALF, HALF), :], w2.at[j])

    barrier = pltpu.get_barrier_semaphore()
    for by in (1, 2, 3):
        pl.semaphore_signal(barrier, inc=1, device_id=(dp, (section + by) % 4), device_id_type=MESH)
    pl.semaphore_signal(barrier, inc=1, device_id=partner, device_id_type=MESH)

    for j in range(3):
        load_wm(j).start()
    for j in range(2):
        load_w1(j).start()

    shift = shift_matrix(section)

    def pack(source, c):
        return mm(mm(slots_of_tokens(shape_ref[c]), source[c], NT).astype(BF), shift).astype(BF)

    def send_in(c):
        return copies.remote("in", c * 4 + section, packs.at[0, c], quarters.at[c, section], (dp, 0), c * 4)

    def og_copy(c, s, target):
        if target == 3:
            source, landing = packs_kept.at[c], grads.at[c, s, pl.ds(0, KEPT)]
        else:
            source, landing = packs.at[1, c], grads.at[c, s]
        return copies.remote("og", c * 4 + s, source, landing, (dp, target), 8 + c * 4 + target)

    def take_in(c, s):
        return copies.remote("in", c * 4 + s, packs.at[0, c], quarters.at[c, s], (dp, 0), c * 4)

    packs[0, 0] = pack(canvas_ref, 0)
    pl.semaphore_wait(barrier, 4)

    @pl.when(section != 0)
    def _():
        send_in(0).start()

    packs[0, 1] = pack(canvas_ref, 1)

    @pl.when(section >= 2)
    def _():
        send_in(0).wait_send()

    @pl.when(section != 0)
    def _():
        send_in(1).start()

    for c in range(2):
        low = pack(ograd_ref, c)
        packs[1, c] = low
        packs_kept[c] = pick_kept(low, kept_ref[c : c + 1, :])

    cond = cond_ref[...].astype(F32)
    signal = (cond * (1.0 / (1.0 + jnp.exp(-cond)))).astype(BF)
    small[...] = jnp.zeros_like(small)
    for c in range(2):
        for i in range(9):
            small[54 + c * 9 + i : 55 + c * 9 + i, :] = signal[c : c + 1, i * 128 : (i + 1) * 128].astype(F32)
    for j in range(3):
        load_wm(j).wait()
        part = mm(signal, w2[j // 2, j % 2 * D : (j % 2 + 1) * D]) + bias_ref[:, j * D : (j + 1) * D]
        for c in range(2):
            mod[c, j : j + 1, :] = part[c : c + 1, :]

    @pl.when(is_feed)
    def _():
        for j in range(2):
            load_w2(j).start()

    @pl.when(section >= 2)
    def _():
        send_in(1).wait_send()

    for target in (3, 1):
        for c in range(2):

            @pl.when(section != target)
            def _():
                og_copy(c, section, target).start()

    for j in range(2):
        load_w1(j).wait()

    def shift_of(c):
        return mod[c, 0:1, :]

    def scale_of(c):
        return mod[c, 1:2, :]

    def gate_of(c):
        return mod[c, 2:3, :]

    def put_sums(c, which, value):
        for i in range(9):
            small[pl.ds(c * 27 + which * 9 + i, 1), :] = value[:, i * 128 : (i + 1) * 128]

    def join(parts_ref, c, r, own, target):
        tiles = {}
        for q in range(4):
            value = own if q == target else parts_ref[c, q, part(r)]
            for t in range(3):
                tile = value[:, t * 128 : (t + 1) * 128]
                at = 2 * q + t
                tiles[at] = tile if at not in tiles else tiles[at] + tile
        return jnp.concatenate([tiles[t] for t in range(9)], axis=1)

    def part(r):
        return pl.ds(0, r)

    def send_forward(c, r, source):
        return copies.remote("forward", c, source.at[c, part(r)], rows.at[c, part(r)], (dp, (section + 1) % 4))

    def send_backward(c, r):
        return copies.remote("backward", c, back.at[c, part(r)], up.at[c, part(r)], (dp, (section + 3) % 4))

    def send_done(c):
        return copies.remote("done", c, picked.at[c], landed.at[c], (dp, 1))

    def send_hidden(c, r):
        return copies.remote("hidden", c, hidden.at[c, part(r)], hidden2.at[c, part(r)], partner)

    def keep_hidden(c, r):
        return copies.local("own_hidden", c, hidden.at[c, part(r)], hidden_own.at[c, part(r)])

    def send_mixed(c, r, source, at):
        return copies.remote("mixed", c, source.at[at, part(r)], mixed_other.at[c, part(r)], partner)

    def keep_mixed(c, r, source, at):
        return copies.local("own_mixed", c, source.at[at, part(r)], mixed_own.at[c, part(r)])

    def keep_x(c, r, at):
        return copies.local("own_x", c, big.at[at, part(r)], x_own.at[c, part(r)])

    def keep_y(c, r):
        return copies.local("own_y", c, big.at[4 + c * 2 + high, part(r)], y_own.at[c, part(r)])

    def send_pair(c, k, piece, r):
        columns = pl.ds(k * D + PIECES[piece][0], PIECES[piece][1])
        source = big.at[4 + c * 2 + 1 - high, part(r), columns]
        return copies.remote("pair", (c * 2 + k) * 4 + piece, source, y_own.at[c, part(r), columns], partner)

    def mixed_keep(c, r):
        return copies.local("own_mixed", c, big.at[c * 2 + 1, part(r), pl.ds(D, D)], mixed_own.at[c, part(r)])

    def mixed_send(c, r):
        source = big.at[c * 2 + 1, part(r), pl.ds(D, D)]
        return copies.remote("mixed", c, source, mixed_other.at[c, part(r)], partner)

    def keep_grad(c):
        return copies.local("own_grad", c, back.at[c], grad_own.at[c])

    def attend(c, r, live):
        x = rows[c, part(r)].astype(F32)
        hid = norm_forward(x, shift_of(c), scale_of(c))
        hidden[c, part(r)] = hid
        send_hidden(c, r).start()
        keep_hidden(c, r).start()
        big[c * 2, part(r)] = mm(hid, w1[0]).astype(BF)
        big[c * 2 + 1, part(r), 0:D] = mm(hid, w1[1, :, 0:D]).astype(BF)
        bias = None if live is None else key_bias(live, r)
        parts[0, part(r)] = jnp.zeros((r, D), F32)

        def group(g, carry):
            cut = pl.ds(pl.multiple_of(g * 256, 128), WINDOW)
            cut_k = pl.ds(pl.multiple_of(D + g * 256, 128), WINDOW)
            q4 = big[c * 2, part(r), cut]
            k4 = big[c * 2, part(r), cut_k]
            v4 = big[c * 2 + 1, part(r), cut]
            results = []
            for start, offset in HEADS_OF_GROUP:
                side = slice(start, start + 256)
                q = only_head(q4[:, side], offset + 32 * g)
                v = only_head(v4[:, side], offset + 32 * g)
                results.append(mm(softmax_of(q, k4[:, side], bias).astype(BF), v))
            parts[0, part(r), cut] += overlaid(results)
            return carry

        lax.fori_loop(0, 4, group, 0)
        mixed = parts[0, part(r)].astype(BF)
        big[c * 2 + 1, part(r), D:HALF] = mixed
        mixed_keep(c, r).start()
        out = mm(mixed, w1[1, :, D:HALF])
        branch[c, part(r)] = out.astype(BF)
        outs[c, part(r)] = (rows[c, part(r)].astype(F32) + gate_of(c) * out).astype(BF)
        send_forward(c, r, outs).start()

    def attend_back(c, r, live, to_section):
        upstream = up[c, part(r)].astype(F32)
        put_sums(c, 2, jnp.sum(upstream * branch[c, part(r)].astype(F32), axis=0, keepdims=True))
        bg = (upstream * gate_of(c)).astype(BF)
        big[4 + c * 2 + 1, part(r), D:HALF] = bg
        up_mixed[part(r)] = mm(bg, w1[1, :, D:HALF], NT).astype(BF)
        bias = None if live is None else key_bias(live, r)
        parts[:, part(r)] = jnp.zeros((3, r, D), F32)

        def put_parts(low, width):
            cut = pl.ds(low, width)
            big[4 + c * 2, part(r), cut] = (parts[0, part(r), cut] * FACTOR).astype(BF)
            big[4 + c * 2, part(r), pl.ds(D + low, width)] = (parts[1, part(r), cut] * FACTOR).astype(BF)
            big[4 + c * 2 + 1, part(r), cut] = parts[2, part(r), cut].astype(BF)

        def group(g, carry):
            if not to_section:
                for piece in range(3):

                    @pl.when(g == piece + 1)
                    def _():
                        put_parts(*PIECES[piece])
                        for k in range(2):
                            send_pair(c, k, piece, r).start()

            cut = pl.ds(pl.multiple_of(g * 256, 128), WINDOW)
            cut_k = pl.ds(pl.multiple_of(D + g * 256, 128), WINDOW)
            q4 = big[c * 2, part(r), cut]
            k4 = big[c * 2, part(r), cut_k]
            v4 = big[c * 2 + 1, part(r), cut]
            mg4 = up_mixed[part(r), cut]
            dq, dk, dv = [], [], []
            for start, offset in HEADS_OF_GROUP:
                side = slice(start, start + 256)
                q = only_head(q4[:, side], offset + 32 * g)
                k = only_head(k4[:, side], offset + 32 * g)
                mg = only_head(mg4[:, side], offset + 32 * g)
                soft = softmax_of(q, k, bias)
                soft_grad = mm(mg, v4[:, side], NT)
                dv.append(mm(soft.astype(BF), mg, TN))
                product = soft * soft_grad
                score_grad = (product - soft * jnp.sum(product, axis=-1, keepdims=True)).astype(BF)
                dq.append(mm(score_grad, k))
                dk.append(mm(score_grad, q, TN))
            parts[0, part(r), cut] += overlaid(dq)
            parts[1, part(r), cut] += overlaid(dk)
            parts[2, part(r), cut] += overlaid(dv)
            return carry

        lax.fori_loop(0, 4, group, 0)
        if to_section:
            put_parts(0, PIECES[3][0])
        put_parts(*PIECES[3])
        if not to_section:
            for k in range(2):
                send_pair(c, k, 3, r).start()
        keep_x(c, r, 4 + c * 2 + high).start()
        hidden_grad = mm(big[4 + c * 2, part(r)], w1[0], NT)
        hidden_grad += mm(big[4 + c * 2 + 1, part(r), 0:D], w1[1, :, 0:D], NT)
        grad, shift_grad, scale_grad = norm_backward(
            rows[c, part(r)].astype(F32), scale_of(c), up[c, part(r)].astype(F32), hidden_grad
        )
        back[c, part(r)] = grad
        if to_section:
            send_backward(c, r).start()
        else:
            keep_grad(c).start()
        put_sums(c, 0, shift_grad)
        put_sums(c, 1, scale_grad)

    def exchange_mixed(r):
        for c in range(2):

            @pl.when(high == 0)
            def _():
                mixed_send(c, r).start()

    def finish_attention(r, to_section):
        for c in range(2):
            send_hidden(c, r).wait()
            keep_hidden2(c, r).start()
            keep_hidden(c, r).wait()

            @pl.when(high == 0)
            def _():
                mixed_send(c, r).wait_send()

            @pl.when(high == 1)
            def _():
                mixed_send(c, r).wait_recv()

            mixed_keep(c, r).wait()
            send_forward(c, r, outs).wait_send()
            keep_x(c, r, 4 + c * 2 + high).wait()
            for k in range(2):
                for piece in range(4):
                    send_pair(c, k, piece, r).wait()
            keep_hidden2(c, r).wait()
            if not to_section:
                keep_grad(c).wait()

    def keep_hidden2(c, r):
        return copies.local("other_hidden", c, hidden2.at[c, part(r)], hidden_other.at[c, part(r)])

    def keep_other(c, r):
        return (
            keep_hidden2(c, r),
            copies.local("other_active", c, extra.at[0, c, part(r)], active_other.at[c, part(r)]),
            copies.local("other_slope", c, extra.at[1, c, part(r)], slope_other.at[c, part(r)]),
        )

    def work_for_partner(c, r):
        active, slope = gelu_pair(mm(hidden2[c, part(r)], w1[high]))
        extra[0, c, part(r)] = active.astype(BF)
        extra[1, c, part(r)] = slope.astype(BF)
        for copy in keep_other(c, r):
            copy.start()

    def send_result(c, q):
        return copies.remote(
            "result", c, outs.at[c, :, pl.ds(256 * q, WINDOW)], window_out.at[c], (dp, q), c * 4 + q
        )

    def keep_result(c):
        return copies.local("result", c * 4 + 1, outs.at[c, :, pl.ds(256, WINDOW)], window_out.at[c])

    @pl.when(section == 0)
    def _():
        def live_of(c):
            lines, width = grid_of(shape_ref[c])
            return lines * width

        def forward(c, carry):
            for s in (1, 2, 3):
                take_in(c, s).wait_recv()
            rows[c] = join(quarters, c, VALID, packs[0, c], 0)
            attend(c, VALID, live_of(c))
            return carry

        def backward(c, carry):
            send_backward(c, VALID).wait_recv()
            attend_back(c, VALID, live_of(c), False)
            return carry

        lax.fori_loop(0, 2, forward, 0)
        pl.semaphore_wait(go, 1)
        exchange_mixed(VALID)
        lax.fori_loop(0, 2, backward, 0)
        finish_attention(VALID, False)

    @pl.when(section == 1)
    def _():
        for j in range(2):
            load_w2(j).wait()

        def forward(c, carry):
            send_forward(c, VALID, outs).wait_recv()
            hid = norm_forward(rows[c].astype(F32), shift_of(c), scale_of(c))
            hidden[c] = hid
            keep_hidden(c, VALID).start()
            for j in range(2):
                active, slope = gelu_pair(mm(hid, w1[j]))
                low = active.astype(BF)
                big[c * 2 + j] = low
                big[4 + c * 2 + j] = slope.astype(BF)
                if j == 0:
                    acc[...] = mm(low, w2[j])
                else:
                    acc[...] += mm(low, w2[j])
            keep_x(c, VALID, c * 2 + high).start()
            out = acc[...]
            branch[c] = out.astype(BF)
            low = (rows[c].astype(F32) + gate_of(c) * out).astype(BF)
            outs[c] = low
            picked[c] = pick_kept(low, kept_ref[pl.ds(c, 1), :])
            send_forward(c, KEPT, picked).start()
            return carry

        lax.fori_loop(0, 2, forward, 0)
        for c in range(2):
            send_forward(c, KEPT, picked).wait_send()
        for c in range(2):
            send_hidden(c, VALID).start()
        for c in range(2):
            for s in (0, 2, 3):
                og_copy(c, s, 1).wait_recv()
            base[c] = join(grads, c, VALID, packs[1, c], 1)
        for c in range(2):
            send_hidden(c, VALID).wait()
        pl.semaphore_signal(go, inc=1, device_id=(dp, 0), device_id_type=MESH)
        for c in range(2):
            work_for_partner(c, VALID)
        for c in range(2):
            send_done(c).wait_recv()
            outs[c] = merge_kept(outs[c], landed[c], kept_ref[c : c + 1, :])
            for q in (0, 2, 3):
                send_result(c, q).start()
            keep_result(c).start()

        def backward(c, carry):
            send_backward(c, KEPT).wait_recv()
            low = merge_kept(base[c], up[c, part(KEPT)], kept_ref[pl.ds(c, 1), :])
            base[c] = low
            upstream = low.astype(F32)
            bg = (upstream * gate_of(c)).astype(BF)
            bgs[c] = bg
            send_mixed(c, VALID, bgs, c).start()
            keep_mixed(c, VALID, bgs, c).start()
            put_sums(c, 2, jnp.sum(upstream * branch[c].astype(F32), axis=0, keepdims=True))
            for j in range(2):
                slope = big[4 + c * 2 + j].astype(F32)
                inner_grad = (mm(bg, w2[j], NT) * slope).astype(BF)
                big[4 + c * 2 + j] = inner_grad
                if j == 0:
                    acc[...] = mm(inner_grad, w1[j], NT)
                else:
                    acc[...] += mm(inner_grad, w1[j], NT)
            keep_y(c, VALID).start()
            grad, shift_grad, scale_grad = norm_backward(
                rows[c].astype(F32), scale_of(c), base[c].astype(F32), acc[...]
            )
            back[c] = grad
            send_backward(c, VALID).start()
            put_sums(c, 0, shift_grad)
            put_sums(c, 1, scale_grad)
            return carry

        lax.fori_loop(0, 2, backward, 0)
        for c in range(2):
            for copy in keep_other(c, VALID):
                copy.wait()
            keep_hidden(c, VALID).wait()
            send_mixed(c, VALID, bgs, c).wait()
            keep_mixed(c, VALID, bgs, c).wait()
            send_backward(c, VALID).wait_send()
            for q in (0, 2, 3):
                send_result(c, q).wait_send()
            keep_result(c).wait()
            keep_x(c, VALID, c * 2 + high).wait()
            keep_y(c, VALID).wait()

    @pl.when(section == 2)
    def _():
        def forward(c, carry):
            send_forward(c, KEPT, outs).wait_recv()
            attend(c, KEPT, None)
            return carry

        def backward(c, carry):
            send_backward(c, KEPT).wait_recv()
            attend_back(c, KEPT, None, True)
            return carry

        lax.fori_loop(0, 2, forward, 0)
        exchange_mixed(KEPT)
        lax.fori_loop(0, 2, backward, 0)
        for c in range(2):
            send_backward(c, KEPT).wait_send()
        for c in range(2):
            for k in range(2):
                for piece in range(4):
                    send_pair(c, k, piece, KEPT).start()
        finish_attention(KEPT, True)


    @pl.when(section == 3)
    def _():
        for j in range(2):
            load_w2(j).wait()
        for c in range(2):
            for s in (0, 1, 2):
                og_copy(c, s, 3).wait_recv()
            low = join(grads, c, KEPT, packs_kept[c], 3)
            base[c, part(KEPT)] = low
            bg = (low.astype(F32) * gate_of(c)).astype(BF)
            bgs[c, part(KEPT)] = bg
            send_mixed(c, KEPT, bgs, c).start()
            keep_mixed(c, KEPT, bgs, c).start()

        def run(c, carry):
            send_forward(c, KEPT, outs).wait_recv()
            hid = norm_forward(rows[c, part(KEPT)].astype(F32), shift_of(c), scale_of(c))
            hidden[c, part(KEPT)] = hid
            send_hidden(c, KEPT).start()
            keep_hidden(c, KEPT).start()
            bg = bgs[c, part(KEPT)]
            for j in range(2):
                active, slope = gelu_pair(mm(hid, w1[j]))
                low = active.astype(BF)
                inner_grad = (mm(bg, w2[j], NT) * slope).astype(BF)
                big[c * 2 + j, part(KEPT)] = low
                big[4 + c * 2 + j, part(KEPT)] = inner_grad
                ahead, behind = mm(low, w2[j]), mm(inner_grad, w1[j], NT)
                if j == 0:
                    parts[0, part(KEPT)] = ahead
                    parts[1, part(KEPT)] = behind
                else:
                    parts[0, part(KEPT)] += ahead
                    parts[1, part(KEPT)] += behind
            x = rows[c, part(KEPT)].astype(F32)
            upstream = base[c, part(KEPT)].astype(F32)
            grad, shift_grad, scale_grad = norm_backward(x, scale_of(c), upstream, parts[1, part(KEPT)])
            back[c, part(KEPT)] = grad
            send_backward(c, KEPT).start()
            out = parts[0, part(KEPT)]
            picked[c] = (x + gate_of(c) * out).astype(BF)
            send_done(c).start()
            put_sums(c, 0, shift_grad)
            put_sums(c, 1, scale_grad)
            put_sums(c, 2, jnp.sum(upstream * out, axis=0, keepdims=True))
            keep_x(c, KEPT, c * 2 + high).start()
            keep_y(c, KEPT).start()
            return carry

        lax.fori_loop(0, 2, run, 0)
        for c in range(2):
            send_hidden(c, KEPT).wait()
            work_for_partner(c, KEPT)
        for c in range(2):
            for copy in keep_other(c, KEPT):
                copy.wait()
            keep_hidden(c, KEPT).wait()
            send_mixed(c, KEPT, bgs, c).wait()
            keep_mixed(c, KEPT, bgs, c).wait()
            send_backward(c, KEPT).wait_send()
            keep_x(c, KEPT, c * 2 + high).wait()
            keep_y(c, KEPT).wait()
            send_done(c).wait_send()

    @pl.when(section != 1)
    def _():
        for c in range(2):
            send_result(c, 0).wait_recv()

    for c in range(2):

        @pl.when(section == 1)
        def _():
            send_in(c).wait_send()

        for target in (3, 1):

            @pl.when(section != target)
            def _():
                og_copy(c, section, target).wait_send()

    packed_out[...] = small[...].astype(BF)


def pipeline(grid_shape, canvas_in, out_grad, kept_rank, conditioning, bias, w1, w2, wm):
    anywhere = pl.BlockSpec(memory_space=pl.ANY)
    vmem = pl.BlockSpec(memory_space=VMEM)
    canvas = array(2, VALID, D)
    count = sum(n for _, n in PIPE_COPIES)
    return pl.pallas_call(
        pipeline_kernel,
        in_specs=[pl.BlockSpec(memory_space=pltpu.SMEM)] + [vmem] * 5 + [anywhere] * 3,
        out_specs=[anywhere] * 10 + [vmem],
        out_shape=[canvas] * 4
        + [array(2, VALID, HALF)] * 2
        + [canvas]
        + [array(2, VALID, HALF)] * 2
        + [array(2, VALID, WINDOW), array(PACKED, 128)],
        scratch_shapes=[
            VMEM((2, D, HALF), BF),
            VMEM((2, HALF, D), BF),
            VMEM((2, VALID, D), BF),
            VMEM((2, 2, VALID, WINDOW), BF),
            VMEM((2, KEPT, WINDOW), BF),
            VMEM((2, 4, VALID, WINDOW), BF),
            VMEM((2, 4, VALID, WINDOW), BF),
            VMEM((2, VALID, D), BF),
            VMEM((2, VALID, D), BF),
            VMEM((2, VALID, D), BF),
            VMEM((8, VALID, HALF), BF),
            VMEM((2, VALID, D), BF),
            VMEM((2, VALID, D), BF),
            VMEM((2, KEPT, D), BF),
            VMEM((2, KEPT, D), BF),
            VMEM((2, VALID, D), BF),
            VMEM((2, VALID, D), BF),
            VMEM((3, VALID, D), F32),
            VMEM((VALID, D), F32),
            VMEM((VALID, D), BF),
            VMEM((2, VALID, D), BF),
            VMEM((2, 2, VALID, HALF), BF),
            VMEM((2, 3, D), F32),
            VMEM((PACKED, 128), F32),
            pltpu.SemaphoreType.DMA((count,)),
            pltpu.SemaphoreType.DMA((count,)),
            pltpu.SemaphoreType.REGULAR,
        ],
        compiler_params=pltpu.CompilerParams(collective_id=1, has_side_effects=True, vmem_limit_bytes=63 * 2**20),
        cost_estimate=cost(40e9, 60e6),
        name="pipeline",
    )(grid_shape, canvas_in, out_grad, kept_rank, conditioning, bias, w1, w2, wm)


FLOWS = ((0, "y", 0, 640), (0, "z", 640, 512), (1, "y", 0, 512), (1, "z", 512, 640))
CUT = 80
FINAL_COPIES = (
    ("flow", 48), ("left", 8), ("right", 8), ("weights", 1),
    ("gather_y", 6), ("gather_z", 6), ("gather_x", 1), ("window", 8),
)


def final_kernel(
    shape_ref, packed_ref, result_ref, hidden_own, hidden_other, mixed_own, mixed_other, x_own, y_own, grad_own, active_other, slope_other, w2_hbm,
    first_out, second_out, result_out, canvas_out, all_packed,
    left, right, other, w2, sums_first, sums_second, windows_in, *scratch,
):
    count = len(FLOWS)
    ones, twos, threes, sums, tiny1, tiny2, tiny3 = (scratch[i * count : (i + 1) * count] for i in range(7))
    copies = Copies(scratch[7 * count], scratch[7 * count + 1])
    for key, number in FINAL_COPIES:
        copies.name(key, number)
    dp, section = lax.axis_index("dp"), lax.axis_index("section")
    x, z, y = dp // 16, (dp // 4) % 4, dp % 4
    place = {"y": y, "z": z}
    is_odd = section % 2 == 1

    def neighbour(axis, by):
        if axis == "y":
            return (x * 16 + z * 4 + (y + by) % 4, section)
        return (x * 16 + ((z + by) % 4) * 4 + y, section)

    partner = ((dp + 16) % 32, section)
    barrier = pltpu.get_barrier_semaphore()
    for axis in ("y", "z"):
        for by in (1, 2, 3):
            pl.semaphore_signal(barrier, inc=1, device_id=neighbour(axis, by), device_id_type=MESH)
    pl.semaphore_signal(barrier, inc=1, device_id=partner, device_id_type=MESH)

    @pl.when(section != 0)
    def _():
        pl.semaphore_signal(barrier, inc=1, device_id=(dp, 0), device_id_type=MESH)

    def load_left(r, feed):
        result = []
        for c in range(2):
            part, own, theirs = pl.ds(0, r), pl.ds(c * r, r), pl.ds((2 + c) * r, r)
            result.append(copies.local("left", c, x_own.at[c, part], left.at[own]))
            if feed:
                result.append(copies.local("left", 2 + c, active_other.at[c, part], left.at[theirs]))
            else:
                result.append(copies.local("left", 2 + c, y_own.at[c, part], left.at[theirs]))
            result.append(copies.local("right", 4 + c, mixed_own.at[c, part], right.at[1, own]))
            result.append(copies.local("right", 6 + c, mixed_other.at[c, part], right.at[1, theirs]))
        return result

    def load_right(r, feed):
        result = []
        for c in range(2):
            part, own, theirs = pl.ds(0, r), pl.ds(c * r, r), pl.ds((2 + c) * r, r)
            if feed:
                result.append(copies.local("left", 4 + c, y_own.at[c, part], other.at[own]))
                result.append(copies.local("left", 6 + c, slope_other.at[c, part], other.at[theirs]))
            result.append(copies.local("right", c, hidden_own.at[c, part], right.at[0, own]))
            result.append(copies.local("right", 2 + c, hidden_other.at[c, part], right.at[0, theirs]))
        if feed:
            result.append(copies.local("weights", 0, w2_hbm.at[pl.ds(x * HALF, HALF), :], w2))
        return result

    for which, (r, feed) in enumerate(((VALID, False), (VALID, True), (KEPT, False), (KEPT, True))):

        @pl.when(section == which)
        def _():
            for c in load_left(r, feed) + load_right(r, feed):
                c.start()

    all_packed[x, z, y] = packed_ref[...]

    def put(target, k, value):
        target[pl.ds(8 * k, 8)] = value.astype(BF).reshape(8, BLOCK, D)

    def columns(k):
        return pl.ds(pl.multiple_of(k * D, 128), D)

    data = (sums_first, sums_second)
    outs = (first_out, second_out)
    halves = (pl.ds(0, 2), pl.ds(2, 2))
    cuts = (pl.ds(0, CUT), pl.ds(CUT, BLOCK - CUT))

    def axes(flow):
        axis = FLOWS[flow][1]
        return axis, "z" if axis == "y" else "y"

    def step(flow, phase, kind, side, source, target):
        number = ((flow * 2 + phase) * 3 + kind) * 2 + side
        return copies.remote("flow", number, source, target, neighbour(axes(flow)[phase], (1, 3)[side]))

    def block(flow, by, half):
        which, axis, low, width = FLOWS[flow]
        position = (place[axis] + by) % 4
        columns = pl.ds(low, width)
        if axis == "y":
            return [data[which].at[4 * (2 * half + i) + position, :, columns] for i in range(2)]
        return [data[which].at[4 * position + 2 * half + i, :, columns] for i in range(2)]

    def pair_ref(flow, by, half):
        which, axis, low, width = FLOWS[flow]
        position = (place[axis] + by) % 4
        columns = pl.ds(low, width)
        grid = data[which].reshape(4, 4, BLOCK, D)
        if axis == "y":
            return grid.at[pl.ds(2 * half, 2), position, :, columns]
        return grid.at[position, pl.ds(2 * half, 2), :, columns]

    def first_a(flow, side):
        return step(flow, 0, 0, side, pair_ref(flow, 2, side), ones[flow].at[side])

    def first_b(flow, side):
        return step(flow, 0, 1, side, pair_ref(flow, (1, 3)[side], 1 - side), twos[flow].at[side])

    def first_c(flow, side):
        return step(flow, 0, 2, side, ones[flow].at[side], threes[flow].at[side])

    def slab(flow, by, cut):
        return sums[flow].at[(place[axes(flow)[1]] + by) % 4, cut]

    def second_a(flow, side):
        return step(flow, 1, 0, side, slab(flow, 2, cuts[side]), tiny1[flow].at[cuts[side]])

    def second_b(flow, side):
        cut = cuts[1 - side]
        return step(flow, 1, 1, side, slab(flow, (1, 3)[side], cut), tiny2[flow].at[cut])

    def second_c(flow, side):
        return step(flow, 1, 2, side, tiny1[flow].at[cuts[side]], tiny3[flow].at[cuts[side]])

    def begin(flow):
        for side in (0, 1):
            first_a(flow, side).start()
        for side in (0, 1):
            first_b(flow, side).start()

    def forward(flow):
        for side in (0, 1):
            first_a(flow, side).wait()
            own = block(flow, (1, 3)[side], side)
            for i in range(2):
                total = ones[flow][side, i].astype(F32) + own[i][...].astype(F32)
                ones[flow][side, i] = total.astype(BF)
            first_c(flow, side).start()

    def middle(flow):
        for side in (0, 1):
            first_b(flow, side).wait()
            first_c(flow, side).wait()
        for half in (0, 1):
            own = block(flow, 0, half)
            for i in range(2):
                total = own[i][...].astype(F32) + threes[flow][half, i].astype(F32)
                sums[flow][2 * half + i] = (total + twos[flow][1 - half, i].astype(F32)).astype(BF)
        for side in (0, 1):
            second_a(flow, side).start()
        for side in (0, 1):
            second_b(flow, side).start()

    def late(flow):
        for side in (0, 1):
            second_a(flow, side).wait()
            own = slab(flow, (1, 3)[side], cuts[side])[...]
            tiny1[flow][cuts[side]] = (tiny1[flow][cuts[side]].astype(F32) + own.astype(F32)).astype(BF)
            second_c(flow, side).start()

    def finish(flow):
        which, axis, low, width = FLOWS[flow]
        for side in (0, 1):
            second_b(flow, side).wait()
            second_c(flow, side).wait()
        own = sums[flow][place[axes(flow)[1]]].astype(F32)
        outs[which][:, low : low + width] = own + tiny2[flow][...].astype(F32) + tiny3[flow][...].astype(F32)

    even = [i for i, f in enumerate(FLOWS) if f[0] == 0]
    odd = [i for i, f in enumerate(FLOWS) if f[0] == 1]

    def stage(work, flows):
        for flow in flows:
            work(flow)

    def gather(axis, by):
        if axis == "y":
            ref = all_packed.at[x, z, y]
            return copies.remote("gather_y", by - 1, ref, ref, neighbour("y", by), 2 + by)
        if axis == "z":
            ref = all_packed.at[x, z]
            return copies.remote("gather_z", by - 1, ref, ref, neighbour("z", by), 2 + by)
        return copies.remote("gather_x", 0, all_packed.at[x], all_packed.at[x], partner)

    def gathered(axis, by):
        if axis == "y":
            ref = all_packed.at[x, z, (y + 4 - by) % 4]
            return copies.remote("gather_y", by - 1, ref, ref, neighbour("y", by), 2 + by)
        if axis == "z":
            ref = all_packed.at[x, (z + 4 - by) % 4]
            return copies.remote("gather_z", by - 1, ref, ref, neighbour("z", by), 2 + by)
        ref = all_packed.at[1 - x]
        return copies.remote("gather_x", 0, ref, ref, partner)

    def window(c, q):
        source = grad_own.at[c, :, pl.ds(256 * q, WINDOW)]
        return copies.remote("window", c * 4, source, windows_in.at[c], (dp, q), c * 4 + q)

    def own_window(c):
        return copies.local("window", c * 4, grad_own.at[c, :, pl.ds(0, WINDOW)], windows_in.at[c])

    shift = shift_matrix(section)

    def unpack(value, c):
        return mm(mm(value, shift, NT).astype(BF), slots_of_tokens(shape_ref[c]), TN).astype(BF)

    @pl.when(section == 0)
    def _():
        pl.semaphore_wait(barrier, 10)

    @pl.when(section != 0)
    def _():
        pl.semaphore_wait(barrier, 7)

    @pl.when(section == 0)
    def _():
        for c in range(2):
            own_window(c).start()
            for q in (1, 2, 3):
                window(c, q).start()

    for by in (1, 2, 3):
        gather("y", by).start()

    def attention_products(r):
        rows = pl.ds(0, 4 * r)
        for copy in load_left(r, False) + load_right(r, False):
            copy.wait()

        def product(k, carry):
            put(sums_first, k, mm(left[rows, columns(k)], right[x * k, rows], TN))
            return carry

        lax.fori_loop(0, 2, product, 0)
        stage(begin, even)
        second_out[...] = jnp.zeros_like(second_out)

    def feed_products(r):
        rows = pl.ds(0, 4 * r)
        for copy in load_left(r, True):
            copy.wait()

        def second_product(k, carry):
            put(sums_second, k, mm(left[rows, columns(k)], right[1, rows], TN))
            return carry

        def first_product(k, carry):
            put(sums_first, k, mm(other[rows, columns(k)], right[0, rows], TN))

            @pl.when(k == 0)
            def _():
                stage(forward, odd)

            return carry

        lax.fori_loop(0, 2, second_product, 0)
        stage(begin, odd)
        for copy in load_right(r, True):
            copy.wait()

        def inner_gradient(c, carry):
            theirs = pl.ds(pl.multiple_of((2 + c) * r, 128), r)
            active_grad = mm(right[1, theirs], w2[...], NT)
            other[theirs] = (active_grad * other[theirs].astype(F32)).astype(BF)
            return carry

        lax.fori_loop(0, 2, inner_gradient, 0)
        lax.fori_loop(0, 2, first_product, 0)
        stage(begin, even)

    for which, r in ((0, VALID), (2, KEPT)):

        @pl.when(section == which)
        def _():
            attention_products(r)

    for which, r in ((1, VALID), (3, KEPT)):

        @pl.when(section == which)
        def _():
            feed_products(r)

    for by in (1, 2, 3):
        gather("y", by).wait_send()
        gathered("y", by).wait_recv()
    for by in (1, 2, 3):
        gather("z", by).start()

    @pl.when(is_odd)
    def _():
        stage(middle, odd)

    stage(forward, even)
    for by in (1, 2, 3):
        gather("z", by).wait_send()
        gathered("z", by).wait_recv()
    gather("x", 0).start()
    for c in range(2):
        result_out[c] = unpack(result_ref[c], c)

    @pl.when(section == 0)
    def _():
        for c in range(2):
            own_window(c).wait()
            canvas_out[c] = unpack(windows_in[c], c)

    for work, later in ((middle, late), (late, finish)):

        @pl.when(is_odd)
        def _():
            stage(later, odd)

        stage(work, even)
    stage(finish, even)

    gather("x", 0).wait_send()
    gathered("x", 0).wait_recv()

    for c in range(2):

        @pl.when(section == 0)
        def _():
            for q in (1, 2, 3):
                window(c, q).wait_send()

        @pl.when(section != 0)
        def _():
            window(c, 0).wait_recv()
            canvas_out[c] = unpack(windows_in[c], c)


def final(grid_shape, packed, result_window, parts, w2):
    anywhere = pl.BlockSpec(memory_space=pl.ANY)
    vmem = pl.BlockSpec(memory_space=VMEM)
    widths = [f[3] for f in FLOWS]
    pair = [VMEM((2, 2, BLOCK, w), BF) for w in widths]
    tiny = [VMEM((BLOCK, w), BF) for w in widths]
    count = sum(n for _, n in FINAL_COPIES)
    canvas = array(2, QUARTER, SLOTS)
    return pl.pallas_call(
        final_kernel,
        in_specs=[pl.BlockSpec(memory_space=pltpu.SMEM)] + [vmem] * 2 + [anywhere] * 10,
        out_specs=[vmem] * 5,
        out_shape=[array(BLOCK, D, dtype=F32)] * 2 + [canvas] * 2 + [array(2, 4, 4, PACKED, 128)],
        scratch_shapes=[
            VMEM((4 * VALID, HALF), BF),
            VMEM((2, 4 * VALID, D), BF),
            VMEM((4 * VALID, HALF), BF),
            VMEM((HALF, D), BF),
            VMEM((16, BLOCK, D), BF),
            VMEM((16, BLOCK, D), BF),
            VMEM((2, VALID, WINDOW), BF),
        ]
        + pair * 3
        + [VMEM((4, BLOCK, w), BF) for w in widths]
        + tiny * 3
        + [pltpu.SemaphoreType.DMA((count,)), pltpu.SemaphoreType.DMA((count,))],
        compiler_params=pltpu.CompilerParams(collective_id=0, has_side_effects=True, vmem_limit_bytes=63 * 2**20),
        cost_estimate=cost(20e9, 60e6),
        name="final",
    )(grid_shape, packed, result_window, *parts, w2)


STRIPE = 128


def closing_kernel(
    packed_ref, first_ref, second_ref, result_ref, canvas_ref,
    first_out, second_out, result_out, canvas_out, product_out, bias_out,
    wide, sums, signals, stage, sems,
):
    wide[...] = packed_ref[...].astype(F32)

    def column(row):
        return wide[pl.ds(row, 32, stride=PACKED), :].astype(BF)

    for c in range(2):
        lines = pl.ds(32 * c, 32)
        for t in range(9):
            signals[lines, t * 128 : (t + 1) * 128] = column(54 + c * 9 + t)
        for t in range(27):
            sums[lines, t * 128 : (t + 1) * 128] = column(c * 27 + t)
    bias_out[...] = jnp.sum(sums[...].astype(F32), axis=0, keepdims=True)

    def write(j):
        lines = pl.ds(j * STRIPE, STRIPE)
        return pltpu.make_async_copy(stage.at[j % 3], product_out.at[lines, :], sems.at[j])

    for j in range(D // STRIPE):
        if j >= 3:
            write(j - 3).wait()
        stage[j % 3] = mm(signals[:, j * STRIPE : (j + 1) * STRIPE], sums[...], TN)
        write(j).start()
    first_out[...] = first_ref[...]
    second_out[...] = second_ref[...]
    result_out[...] = result_ref[...]
    canvas_out[...] = canvas_ref[...]
    for j in range(D // STRIPE - 3, D // STRIPE):
        write(j).wait()


def closing(packed, first, second, result, canvas):
    anywhere = pl.BlockSpec(memory_space=pl.ANY)
    vmem = pl.BlockSpec(memory_space=VMEM)
    return pl.pallas_call(
        closing_kernel,
        in_specs=[vmem] * 5,
        out_specs=[vmem] * 4 + [anywhere, vmem],
        out_shape=[
            array(*first.shape, dtype=F32),
            array(*second.shape, dtype=F32),
            array(*result.shape),
            array(*canvas.shape),
            array(D, 3 * D, dtype=F32),
            array(1, 3 * D, dtype=F32),
        ],
        scratch_shapes=[
            VMEM((32 * PACKED, 128), F32),
            VMEM((64, 3 * D), BF),
            VMEM((64, D), BF),
            VMEM((3, STRIPE, 3 * D), F32),
            pltpu.SemaphoreType.DMA((D // STRIPE,)),
        ],
        compiler_params=pltpu.CompilerParams(vmem_limit_bytes=63 * 2**20),
        cost_estimate=cost(2 * 64 * D * 3 * D, 4 * D * 3 * D),
        name="closing",
    )(packed, first, second, result, canvas)


def local(
    canvas_in,
    conditioning,
    grid_shape,
    kept_rank,
    first_weight,
    second_weight,
    modulation_weight,
    modulation_bias,
    out_grad,
):
    w1, w2 = first_weight[0], second_weight[0]
    outputs = pipeline(
        grid_shape,
        canvas_in.transpose(0, 2, 1),
        out_grad.transpose(0, 2, 1),
        kept_rank,
        conditioning,
        modulation_bias,
        w1,
        w2,
        modulation_weight[0],
    )
    first_sum, second_sum, result, canvas_grad, packed = final(grid_shape, outputs[10], outputs[9], outputs[:9], w2)
    first_sum, second_sum, result, canvas_grad, modulation_grad, bias_grad = closing(
        packed.reshape(32 * PACKED, 128), first_sum, second_sum, result, canvas_grad
    )
    return (
        result.transpose(0, 2, 1),
        canvas_grad.transpose(0, 2, 1),
        first_sum.T[None],
        second_sum[None],
        modulation_grad[None],
        bias_grad,
    )


def solution(mesh):
    placed = (
        P("dp", None, "section"),
        P("dp", None),
        P("dp"),
        P("dp", None),
        P("section", None, None),
        P("section", None, None),
        P("section", None, None),
        P("section", None),
        P("dp", None, "section"),
    )
    return jax.shard_map(
        local,
        mesh=mesh,
        in_specs=placed,
        out_specs=(
            P("dp", None, "section"),
            P("dp", None, "section"),
            P("section", None, "dp"),
            P("section", "dp", None),
            P("section", None, None),
            P("section", None),
        ),
        check_vma=False,
    )
```
